32 devices in a mesh: rows: 8 (over z, y), seq: 4 (over x, core).
Axes of the slice: x: 2, y: 2, z: 4, core: 2. Of those that a mesh axis runs over, the one named last changes fastest.
Arguments:
- decoder_input: bfloat16 [8, 1408, 768], P('rows', 'seq'), may hold values from -6 to 6
- encoder_output: bfloat16 [8, 4096, 768], P('rows', 'seq'), may hold values from -6 to 6
- cotangent: bfloat16 [8, 1408, 768], P('rows', 'seq'), may hold values from -6 to 6
- decoder_segment: int32 [8, 1408], P('rows'), may hold values from 0 to 2, as said below
- decoder_padding: int32 [8, 1408], P('rows'), may hold values from 0 to 1, as said below
- encoder_segment: int32 [8, 4096], P('rows'), may hold values from 0 to 2, as said below
- encoder_padding: int32 [8, 4096], P('rows'), may hold values from 0 to 1, as said below
- distance_bucket: int32 [1408], replicated, may hold values from 0 to 31, as said below
- attention_weight: float32 [768, 8, 768], P(('rows', 'seq'))
- attention_moment: float32 [768, 8, 768], P(('rows', 'seq')), may hold values from -64 to 64
- attention_rowwise: float32 [8, 768], P(None, ('rows', 'seq')), may hold values from 11.264 to 45.056
- attention_colwise: float32 [8, 768], replicated, may hold values from 11.264 to 45.056
- expand_weight: float32 [768, 2, 2048], P(('rows', 'seq')), may hold values from -0.21875 to 0.21875
- expand_moment: float32 [768, 2, 2048], P(('rows', 'seq')), may hold values from -64 to 64
- expand_rowwise: float32 [2, 768], P(None, ('rows', 'seq')), may hold values from 11.264 to 45.056
- expand_colwise: float32 [2, 2048], replicated, may hold values from 11.264 to 45.056
- contract_weight: float32 [2048, 768], P(('rows', 'seq')), may hold values from -0.25 to 0.25
- contract_moment: float32 [2048, 768], P(('rows', 'seq')), may hold values from -64 to 64
- contract_rowwise: float32 [2048], P(('rows', 'seq')), may hold values from 11.264 to 45.056
- contract_colwise: float32 [768], replicated, may hold values from 11.264 to 45.056
- norm_gain: float32 [3, 768], replicated
- gain_moment: float32 [3, 768], replicated, may hold values from -64 to 64
- gain_second: float32 [3, 768], replicated, may hold values from 11.264 to 45.056
- relative_table: float32 [32, 12], replicated, may hold values from -4 to 4
- table_moment: float32 [32, 12], replicated, may hold values from -64 to 64
- table_second: float32 [32, 12], replicated, may hold values from 11.264 to 45.056
Outputs:
- layer_output: bfloat16 [8, 1408, 768], P('rows', 'seq')
- input_gradient: float32 [8, 1408, 768], P('rows', 'seq')
- encoder_gradient: float32 [8, 4096, 768], P('rows', 'seq')
- attention_gradient: float32 [768, 8, 768], P(('rows', 'seq'))
- moment_attention: float32 [768, 8, 768], P(('rows', 'seq'))
- rowwise_attention: float32 [8, 768], P(None, ('rows', 'seq'))
- colwise_attention: float32 [8, 768], replicated
- updated_attention: float32 [768, 8, 768], P(('rows', 'seq'))
- expand_gradient: float32 [768, 2, 2048], P(('rows', 'seq'))
- moment_expand: float32 [768, 2, 2048], P(('rows', 'seq'))
- rowwise_expand: float32 [2, 768], P(None, ('rows', 'seq'))
- colwise_expand: float32 [2, 2048], replicated
- updated_expand: float32 [768, 2, 2048], P(('rows', 'seq'))
- contract_gradient: float32 [2048, 768], P(('rows', 'seq'))
- moment_contract: float32 [2048, 768], P(('rows', 'seq'))
- rowwise_contract: float32 [2048], P(('rows', 'seq'))
- colwise_contract: float32 [768], replicated
- updated_contract: float32 [2048, 768], P(('rows', 'seq'))
- gain_gradient: float32 [3, 768], replicated
- moment_gain: float32 [3, 768], replicated
- second_gain: float32 [3, 768], replicated
- updated_gain: float32 [3, 768], replicated
- table_gradient: float32 [32, 12], replicated
- moment_table: float32 [32, 12], replicated
- second_table: float32 [32, 12], replicated
- updated_table: float32 [32, 12], replicated
The draws below stay inside these ranges and needn't reach their ends.
Inputs may be any that keep to these rules, and one draw needn't show every extreme that they name: `decoder_segment`: never falls along a row; every row holds documents 0, 1 and 2, and document 1 starts among the first 352 positions and ends among the last 352. `decoder_padding`: in each row the zeros form a non-empty tail inside document 2, which keeps a real position. `encoder_segment`: never falls along a row; every row holds documents 0, 1 and 2, and document 1 starts among the first 1024 positions and ends among the last 1024. `encoder_padding`: in each row the zeros form a non-empty tail inside document 2, which keeps a real position. `distance_bucket`: never falls; entry d is d for d below 16, and the last entry is 31.
All inputs are finite; a program needn't handle non-finite values.
Results may differ from the reference program's by a relative error of at most 0.024.
The reference program's roundings to bfloat16 on the way count: a program that leaves them out, or rounds other values in their place, can miss the bound.
Values may be sent and summed in bfloat16 or wider, within the bound.
A program may use at most 384 MiB of HBM per device.

```python
import math
import jax
import jax.numpy as jnp
from jax import lax

D = 768
FF = 2048
HEADS = 12
BUCKETS = 32
HEAD_DIM = 64
DEC_LEN = 1408
ENC_LEN = 4096
STEP = 10
ROWS = 8
DEC_DEV = 352
ENC_DEV = 1024


def decoder_bounds(key):
    first_cut = jax.random.randint(jax.random.fold_in(key, 101), (ROWS, 1), 1, DEC_DEV)
    second_cut = jax.random.randint(jax.random.fold_in(key, 102), (ROWS, 1), DEC_LEN - DEC_DEV + 1, DEC_LEN - 1)
    pad_start = jax.random.randint(jax.random.fold_in(key, 103), (ROWS, 1), second_cut + 1, DEC_LEN)
    return (first_cut, second_cut, pad_start)


def encoder_bounds(key):
    first_cut = jax.random.randint(jax.random.fold_in(key, 201), (ROWS, 1), 1, ENC_DEV)
    second_cut = jax.random.randint(jax.random.fold_in(key, 202), (ROWS, 1), ENC_LEN - ENC_DEV + 1, ENC_LEN - 1)
    pad_start = jax.random.randint(jax.random.fold_in(key, 203), (ROWS, 1), second_cut + 1, ENC_LEN)
    return (first_cut, second_cut, pad_start)


def draw_decoder_segment(key, part):
    first_cut, second_cut, pad_start = decoder_bounds(key)
    position = jnp.arange(DEC_LEN, dtype=jnp.int32)[None, :]
    return (position >= first_cut).astype(jnp.int32) + (position >= second_cut).astype(jnp.int32)


def draw_decoder_padding(key, part):
    first_cut, second_cut, pad_start = decoder_bounds(key)
    position = jnp.arange(DEC_LEN, dtype=jnp.int32)[None, :]
    return (position < pad_start).astype(jnp.int32)


def draw_encoder_segment(key, part):
    first_cut, second_cut, pad_start = encoder_bounds(key)
    position = jnp.arange(ENC_LEN, dtype=jnp.int32)[None, :]
    return (position >= first_cut).astype(jnp.int32) + (position >= second_cut).astype(jnp.int32)


def draw_encoder_padding(key, part):
    first_cut, second_cut, pad_start = encoder_bounds(key)
    position = jnp.arange(ENC_LEN, dtype=jnp.int32)[None, :]
    return (position < pad_start).astype(jnp.int32)


def draw_distance_bucket(key, part):
    key = jax.random.fold_in(key, 7)
    position = jnp.arange(DEC_LEN, dtype=jnp.int32)
    coin_value = jax.random.randint(key, (DEC_LEN,), 0, position + 1)
    increment = jnp.where(position < BUCKETS // 2, jnp.minimum(position, 1), (coin_value < 4).astype(jnp.int32))
    bucket = jnp.minimum(jnp.cumsum(increment), BUCKETS - 1)
    return jnp.where(position == DEC_LEN - 1, BUCKETS - 1, bucket).astype(jnp.int32)


def draw_norm_gain(key, part):
    key = jax.random.fold_in(key, 9)
    position = jnp.arange(D, dtype=jnp.float32) / (D - 1)
    baseline = 0.6 * 3.0 ** position
    jitter = jax.random.uniform(key, (3, D), jnp.float32, 0.8, 1.25)
    return baseline[None, :] * jitter


def draw_attention_weight(key, part):
    key = jax.random.fold_in(key, 13)
    spread = jnp.array([1.0, 1.0, 1.0, 4.0, 1.0, 1.0, 1.0, 4.0], jnp.float32) * D ** (-0.5)
    baseline = jax.random.truncated_normal(key, -4.0, 4.0, (D, 8, D), jnp.float32)
    return baseline * spread[None, :, None]


def levels(own_key, dims, cuts, least, largest):
    level = 1.0
    for dim, blocks in cuts:
        heights = jax.random.uniform(jax.random.fold_in(jax.random.fold_in(own_key, 6), dim), (blocks,), jnp.float32, least / len(cuts), largest / len(cuts))
        level = level * jnp.repeat(jnp.exp(heights), dims[dim] // blocks).reshape((-1,) + (1,) * (len(dims) - 1 - dim))
    return level


def centred(stream_key, dims, scale, limit, pieces=(), kind=jnp.bfloat16):
    entries = scale * jax.random.normal(stream_key, dims, jnp.float32)
    if pieces:
        entries = entries * levels(stream_key, dims, pieces, -0.22, 0.18)
    return jnp.clip(entries, -limit, limit).astype(kind)


def setup_inputs(seed: int = 0) -> dict:
    streams_of = jax.random.split(jax.random.key(seed), 27)
    decoder_input = centred(streams_of[0], (ROWS, DEC_LEN, D), 1.0, 6.0, ((0, 8), (1, 4)))
    encoder_output = centred(streams_of[1], (ROWS, ENC_LEN, D), 1.0, 6.0, ((0, 8), (1, 4)))
    cotangent = centred(streams_of[2], (ROWS, DEC_LEN, D), 1.0, 6.0, ((0, 8), (1, 4)))
    decoder_segment = draw_decoder_segment(jax.random.fold_in(streams_of[26], 71), 0)
    decoder_padding = draw_decoder_padding(jax.random.fold_in(streams_of[26], 71), 0)
    encoder_segment = draw_encoder_segment(jax.random.fold_in(streams_of[26], 71), 0)
    encoder_padding = draw_encoder_padding(jax.random.fold_in(streams_of[26], 71), 0)
    distance_bucket = draw_distance_bucket(jax.random.fold_in(streams_of[26], 71), 0)
    attention_weight = draw_attention_weight(jax.random.fold_in(streams_of[26], 71), 0)
    attention_moment = centred(streams_of[9], (D, 8, D), (0.11 * (ROWS * DEC_LEN) ** 0.5), 64.0, ((0, 32),), jnp.float32)
    attention_rowwise = jnp.clip(jnp.exp(math.log(45.056) - 1.3862944 * jax.random.uniform(streams_of[10], (8, D), jnp.float32) ** levels(streams_of[10], (8, D), ((1, 32),), -0.2, 0.2)), 11.264, 45.056)
    attention_colwise = jnp.clip(jnp.exp(jax.random.uniform(streams_of[11], (8, D), jnp.float32, math.log(11.264), math.log(45.056))), 11.264, 45.056)
    expand_weight = centred(streams_of[12], (D, 2, FF), D ** -0.5, 0.21875, ((0, 32),), jnp.float32)
    expand_moment = centred(streams_of[13], (D, 2, FF), (0.11 * (ROWS * DEC_LEN) ** 0.5), 64.0, ((0, 32),), jnp.float32)
    expand_rowwise = jnp.clip(jnp.exp(math.log(45.056) - 1.3862944 * jax.random.uniform(streams_of[14], (2, D), jnp.float32) ** levels(streams_of[14], (2, D), ((1, 32),), -0.2, 0.2)), 11.264, 45.056)
    expand_colwise = jnp.clip(jnp.exp(jax.random.uniform(streams_of[15], (2, FF), jnp.float32, math.log(11.264), math.log(45.056))), 11.264, 45.056)
    contract_weight = centred(streams_of[16], (FF, D), (FF // 4) ** -0.5, 0.25, ((0, 32),), jnp.float32)
    contract_moment = centred(streams_of[17], (FF, D), (0.11 * (ROWS * DEC_LEN) ** 0.5), 64.0, ((0, 32),), jnp.float32)
    contract_rowwise = jnp.clip(jnp.exp(math.log(45.056) - 1.3862944 * jax.random.uniform(streams_of[18], (FF,), jnp.float32) ** levels(streams_of[18], (FF,), ((0, 32),), -0.2, 0.2)), 11.264, 45.056)
    contract_colwise = jnp.clip(jnp.exp(jax.random.uniform(streams_of[19], (D,), jnp.float32, math.log(11.264), math.log(45.056))), 11.264, 45.056)
    norm_gain = draw_norm_gain(jax.random.fold_in(streams_of[26], 71), 0)
    gain_moment = centred(streams_of[21], (3, D), (0.11 * (ROWS * DEC_LEN) ** 0.5), 64.0, (), jnp.float32)
    gain_second = jnp.clip(jnp.exp(jax.random.uniform(streams_of[22], (3, D), jnp.float32, math.log(11.264), math.log(45.056))), 11.264, 45.056)
    relative_table = centred(streams_of[23], (BUCKETS, HEADS), 1.0, 4.0, (), jnp.float32)
    table_moment = centred(streams_of[24], (BUCKETS, HEADS), (0.11 * (ROWS * DEC_LEN) ** 0.5), 64.0, (), jnp.float32)
    table_second = jnp.clip(jnp.exp(jax.random.uniform(streams_of[25], (BUCKETS, HEADS), jnp.float32, math.log(11.264), math.log(45.056))), 11.264, 45.056)
    return {"decoder_input": decoder_input, "encoder_output": encoder_output, "cotangent": cotangent, "decoder_segment": decoder_segment, "decoder_padding": decoder_padding, "encoder_segment": encoder_segment, "encoder_padding": encoder_padding, "distance_bucket": distance_bucket, "attention_weight": attention_weight, "attention_moment": attention_moment, "attention_rowwise": attention_rowwise, "attention_colwise": attention_colwise, "expand_weight": expand_weight, "expand_moment": expand_moment, "expand_rowwise": expand_rowwise, "expand_colwise": expand_colwise, "contract_weight": contract_weight, "contract_moment": contract_moment, "contract_rowwise": contract_rowwise, "contract_colwise": contract_colwise, "norm_gain": norm_gain, "gain_moment": gain_moment, "gain_second": gain_second, "relative_table": relative_table, "table_moment": table_moment, "table_second": table_second}


HIGHEST = lax.Precision.HIGHEST
NORM_EPS = 1e-06
MASKED = -1e+30
BETA_ONE = 0.9
BETA_TWO = 0.999
ADAM_EPS = 1e-08
WEIGHT_DECAY = 0.01
MATRIX_RATE = 0.15
VECTOR_RATE = 1.0

@jax.custom_vjp
def low(v):
    return lax.optimization_barrier(v.astype(jnp.bfloat16)).astype(jnp.float32)

@jax.custom_vjp
def low_back(v):
    return v

def low_keep(v):
    return (low(v), None)

def low_pass(kept, grad):
    return (grad,)

def back_keep(v):
    return (v, None)

def back_low(kept, grad):
    return (low(grad),)
low.defvjp(low_keep, low_pass)
low_back.defvjp(back_keep, back_low)

def normalize(values, scaling):
    return values * lax.rsqrt(lax.optimization_barrier(jnp.mean(values * values, -1, keepdims=True)) + NORM_EPS) * scaling

def product(left, right):
    return jnp.dot(left, right, precision=HIGHEST)

def gated(gate_values, up_values):
    return jax.nn.gelu(gate_values, approximate=True) * up_values

def attend(queries, key_rows, value_rows, offset, allowed):
    length = queries.shape[0]
    query_heads = queries.reshape(length, HEADS, HEAD_DIM)
    key_heads = key_rows.reshape(key_rows.shape[0], HEADS, HEAD_DIM)
    value_heads = value_rows.reshape(value_rows.shape[0], HEADS, HEAD_DIM)
    scored = jnp.einsum('qhd,khd->hqk', query_heads, key_heads, precision=HIGHEST) * HEAD_DIM ** (-0.5) + offset
    scored = jnp.where(allowed[None], low_back(scored), MASKED)
    probability = low(jax.nn.softmax(scored, axis=-1))
    result = jnp.einsum('hqk,khd->qhd', probability, value_heads, precision=HIGHEST).reshape(length, D)
    return low(low_back(result))

def layer_row(weights, inputs):
    attention, expand, contract, gains, bias = weights
    decoder_row, encoder_row, segment_row, padding_row, encoder_segments, encoder_real = inputs
    position = jnp.arange(DEC_LEN)
    causal = position[None, :] <= position[:, None]
    itself = position[None, :] == position[:, None]
    self_allowed = causal & (segment_row[None, :] == segment_row[:, None]) & ((padding_row[None, :] == 1) | itself)
    cross_allowed = (encoder_segments[None, :] == segment_row[:, None]) & (encoder_real[None, :] == 1)
    first_norm = low(normalize(decoder_row, gains[0]))
    queries = low(low_back(product(first_norm, attention[:, 0])))
    key_rows = low(low_back(product(first_norm, attention[:, 1])))
    value_rows = low(low_back(product(first_norm, attention[:, 2])))
    self_result = attend(queries, key_rows, value_rows, bias, self_allowed)
    after_self = decoder_row + low_back(product(self_result, attention[:, 3]))
    cross_norm = low(normalize(after_self, gains[1]))
    cross_queries = low(low_back(product(cross_norm, attention[:, 4])))
    encoder_low = low(encoder_row)
    cross_keys = low(low_back(product(encoder_low, attention[:, 5])))
    cross_values = low(low_back(product(encoder_low, attention[:, 6])))
    cross_result = attend(cross_queries, cross_keys, cross_values, 0.0, cross_allowed)
    after_cross = after_self + low_back(product(cross_result, attention[:, 7]))
    feed_norm = low(normalize(after_cross, gains[2]))
    gate_values = low_back(product(feed_norm, expand[:, 0]))
    up_values = low_back(product(feed_norm, expand[:, 1]))
    hidden = low(gated(gate_values, up_values))
    return after_cross + low_back(product(hidden, contract))

def forward_pass(decoder_values, encoder_values, attention, expand, contract, gains, table, distance_bucket, integer_rows):
    onehot = (distance_bucket[:, None] == jnp.arange(BUCKETS)[None, :]).astype(jnp.float32)
    bias_rows = product(onehot, table)
    position = jnp.arange(DEC_LEN)
    distance = jnp.clip(position[:, None] - position[None, :], 0, DEC_LEN - 1)
    bias = jnp.transpose(bias_rows[distance], (2, 0, 1))
    weights = (low(attention), low(expand), low(contract), gains, bias)
    row_step = jax.checkpoint(layer_row)

    def run_row(inputs):
        return row_step(weights, inputs)
    return lax.map(run_row, (decoder_values, encoder_values) + integer_rows)

def factored(gradient, moment, rowwise, colwise, weight):
    square = gradient * gradient
    rowwise_new = BETA_TWO * rowwise + (1.0 - BETA_TWO) * lax.optimization_barrier(jnp.mean(square, 2)).T
    colwise_new = BETA_TWO * colwise + (1.0 - BETA_TWO) * lax.optimization_barrier(jnp.mean(square, 0))
    moment_new = BETA_ONE * moment + (1.0 - BETA_ONE) * gradient
    second = rowwise_new.T[:, :, None] * colwise_new[None] / lax.optimization_barrier(jnp.mean(rowwise_new, 1))[None, :, None]
    stepped = moment_new / (1.0 - BETA_ONE ** STEP) / (jnp.sqrt(second / (1.0 - BETA_TWO ** STEP)) + ADAM_EPS)
    updated = weight - MATRIX_RATE * (stepped + WEIGHT_DECAY * weight)
    return (moment_new, rowwise_new, colwise_new, updated)

def adaptive(gradient, moment, second, weight):
    moment_new = BETA_ONE * moment + (1.0 - BETA_ONE) * gradient
    second_new = BETA_TWO * second + (1.0 - BETA_TWO) * gradient * gradient
    stepped = moment_new / (1.0 - BETA_ONE ** STEP) / (jnp.sqrt(second_new / (1.0 - BETA_TWO ** STEP)) + ADAM_EPS)
    return (moment_new, second_new, weight - VECTOR_RATE * stepped)

def reference(decoder_input, encoder_output, cotangent, decoder_segment, decoder_padding, encoder_segment, encoder_padding, distance_bucket, attention_weight, attention_moment, attention_rowwise, attention_colwise, expand_weight, expand_moment, expand_rowwise, expand_colwise, contract_weight, contract_moment, contract_rowwise, contract_colwise, norm_gain, gain_moment, gain_second, relative_table, table_moment, table_second):
    integer_rows = (decoder_segment, decoder_padding, encoder_segment, encoder_padding)

    def whole(decoder_values, encoder_values, attention, expand, contract, gains, table):
        return forward_pass(decoder_values, encoder_values, attention, expand, contract, gains, table, distance_bucket, integer_rows)
    result, backward = jax.vjp(whole, decoder_input.astype(jnp.float32), encoder_output.astype(jnp.float32), attention_weight, expand_weight, contract_weight, norm_gain, relative_table)
    input_gradient, encoder_gradient, attention_gradient, expand_gradient, contract_gradient, gain_gradient, table_gradient = backward(cotangent.astype(jnp.float32))
    attention_new = factored(attention_gradient, attention_moment, attention_rowwise, attention_colwise, attention_weight)
    expand_new = factored(expand_gradient, expand_moment, expand_rowwise, expand_colwise, expand_weight)
    contract_new = factored(contract_gradient[:, None], contract_moment[:, None], contract_rowwise[None], contract_colwise[None], contract_weight[:, None])
    gain_new = adaptive(gain_gradient, gain_moment, gain_second, norm_gain)
    table_new = adaptive(table_gradient, table_moment, table_second, relative_table)
    return (result.astype(jnp.bfloat16), input_gradient, encoder_gradient, attention_gradient, attention_new[0], attention_new[1], attention_new[2], attention_new[3], expand_gradient, expand_new[0], expand_new[1], expand_new[2], expand_new[3], contract_gradient, contract_new[0][:, 0], contract_new[1][0], contract_new[2][0], contract_new[3][:, 0], gain_gradient, gain_new[0], gain_new[1], gain_new[2], table_gradient, table_new[0], table_new[1], table_new[2])
```

```python
import jax
import jax.numpy as jnp
from jax import lax
from jax.experimental import pallas as pl
from jax.experimental.pallas import tpu as pltpu
from jax.sharding import PartitionSpec as P

D = 768
FF = 2048
HEADS = 12
BUCKETS = 32
STEP = 10
HIGHEST = lax.Precision.HIGHEST
NORM_EPS = 1e-06
BETA_ONE = 0.9
BETA_TWO = 0.999
ADAM_EPS = 1e-08
WEIGHT_DECAY = 0.01
MATRIX_RATE = 0.15
VECTOR_RATE = 1.0
HD = 64
NEG = -1e30
F32 = jnp.float32
BF = jnp.bfloat16

def nt(a,b): return lax.dot_general(a,b,(((1,),(1,)),((),())),preferred_element_type=F32)
def nn(a,b): return lax.dot_general(a,b,(((1,),(0,)),((),())),preferred_element_type=F32)
def tn(a,b): return lax.dot_general(a,b,(((0,),(0,)),((),())),preferred_element_type=F32)

def cross_fwd(q,k,v,qa,ka,qb=352,kc=1024):
    Lq,W=q.shape; Lk=k.shape[0]; H=W//HD
    nk=Lk//kc
    def kern(q_ref,k_ref,v_ref,qa_ref,ka_ref,o_ref,of_ref,lse_ref,kaug,vs,s_s,m_s,l_s,acc):
        @pl.when(pl.program_id(0)==0)
        def _():
            for h in range(H):
                kaug[h,:,0:HD]=k_ref[:,h*HD:(h+1)*HD]
                kaug[h,:,HD:2*HD]=ka_ref[...]
                vs[h]=v_ref[:,h*HD:(h+1)*HD]
        lane=lax.broadcasted_iota(jnp.int32,(qb,128),1)
        lses=jnp.zeros((qb,128),F32)
        outs=[]
        for h in range(H):
            qh=(q_ref[:,h*HD:(h+1)*HD]*BF(0.125)).astype(BF)
            qg=jnp.concatenate([qh,qa_ref[...]],axis=1)
            m_s[...]=jnp.full((qb,128),-3e38,F32)
            for c in range(nk):
                s=nt(qg,kaug[h,c*kc:(c+1)*kc,:])
                s_s[:,c*kc:(c+1)*kc]=s
                mm=m_s[...]
                for t in range(kc//128): mm=jnp.maximum(mm,s[:,t*128:(t+1)*128])
                m_s[...]=mm
            m=jnp.max(m_s[...],axis=1,keepdims=True)
            l_s[...]=jnp.zeros((qb,128),F32)
            acc[...]=jnp.zeros((qb,HD),F32)
            for c in range(nk):
                p=jnp.exp(s_s[:,c*kc:(c+1)*kc]-m)
                ll=l_s[...]
                for t in range(kc//128): ll=ll+p[:,t*128:(t+1)*128]
                l_s[...]=ll
                acc[...]+=nn(p.astype(BF),vs[h,c*kc:(c+1)*kc,:])
            l=jnp.sum(l_s[...],axis=1,keepdims=True)
            o=acc[...]/l
            outs.append(o)
            lses=jnp.where(lane==h,m+jnp.log(l),lses)
        oo=jnp.concatenate(outs,axis=1)
        o_ref[...]=oo.astype(BF)
        of_ref[...]=oo
        lse_ref[...]=lses
    full=lambda s: pl.BlockSpec(s,lambda i:(0,)*len(s))
    row=lambda w: pl.BlockSpec((qb,w),lambda i:(i,0))
    return pl.pallas_call(kern,grid=(Lq//qb,),
        out_shape=(jax.ShapeDtypeStruct((Lq,W),BF),jax.ShapeDtypeStruct((Lq,W),F32),jax.ShapeDtypeStruct((Lq,128),F32)),
        in_specs=[row(W),full((Lk,W)),full((Lk,W)),row(HD),full((Lk,HD))],
        out_specs=(row(W),row(W),row(128)),
        scratch_shapes=[pltpu.VMEM((H,Lk,2*HD),BF),pltpu.VMEM((H,Lk,HD),BF),pltpu.VMEM((qb,Lk),F32),pltpu.VMEM((qb,128),F32),pltpu.VMEM((qb,128),F32),pltpu.VMEM((qb,HD),F32)],
        compiler_params=pltpu.CompilerParams(vmem_limit_bytes=56*2**20),name="cross_fwd")(q,k,v,qa,ka)

def split3(x):
    a=x.astype(BF); r=x-a.astype(F32)
    b=r.astype(BF); c=(r-b.astype(F32)).astype(BF)
    return a,b,c

def cross_bwd(q,k,v,do,of,lse,qa,ka,qb=256,kc=1024):
    Lq,W=q.shape; Lk=k.shape[0]; H=W//HD
    nq=-(-Lq//qb); Lp=nq*qb; nk=Lk//kc
    def kern(q_ref,k_ref,v_ref,do_ref,of_ref,lse_ref,qa_ref,ka_ref,dq_ref,dk_ref,dv_ref,kaug,vaug,qaug,doaug,dkacc,dvacc,dqs,dks,dvs):
        h=pl.program_id(0); i=pl.program_id(1)
        for hh in range(H):
            @pl.when((h==hh)&(i==0))
            def _():
                sl=slice(hh*HD,(hh+1)*HD)
                kaug[:,0:HD]=k_ref[:,sl]
                lane=lax.broadcasted_iota(jnp.int32,(Lk,HD),1)
                kaug[:,HD:2*HD]=jnp.where((lane>=3)&(lane<6),BF(1),ka_ref[...])
                vaug[:,0:HD]=v_ref[:,sl]
                vaug[:,HD:2*HD]=jnp.where(lane<3,BF(1),BF(0)).astype(BF)
                lq=lax.broadcasted_iota(jnp.int32,(Lq,HD),1)
                a,b,c=split3(-lse_ref[:,hh:hh+1])
                aug=jnp.where(lq==3,a,jnp.where(lq==4,b,jnp.where(lq==5,c,qa_ref[...])))
                qaug[0:Lq,0:HD]=q_ref[:,sl]*BF(0.125)
                qaug[0:Lq,HD:2*HD]=aug
                dd=do_ref[:,sl]
                delta=jnp.sum(dd.astype(F32)*of_ref[:,sl],axis=1,keepdims=True)
                a,b,c=split3(-delta)
                aug=jnp.where(lq==0,a,jnp.where(lq==1,b,jnp.where(lq==2,c,BF(0))))
                doaug[0:Lq,0:HD]=dd
                doaug[0:Lq,HD:2*HD]=aug
                if Lp>Lq:
                    qaug[Lq:Lp,:]=jnp.zeros((Lp-Lq,2*HD),BF)
                    doaug[Lq:Lp,:]=jnp.zeros((Lp-Lq,2*HD),BF)
                dkacc[...]=jnp.zeros_like(dkacc)
                dvacc[...]=jnp.zeros_like(dvacc)
        off=pl.multiple_of(i*qb,qb)
        qg=qaug[pl.ds(off,qb),:]
        dg=doaug[pl.ds(off,qb),:]
        qp=qg[:,0:HD]; dp_=dg[:,0:HD]
        dq=jnp.zeros((qb,HD),F32)
        def step(c,dq):
            o=pl.multiple_of(c*kc,kc)
            kk=kaug[pl.ds(o,kc),:]
            p=jnp.exp(nt(kk,qg))
            g=nt(vaug[pl.ds(o,kc),:],dg)
            ds=(p*g).astype(BF)
            dvacc[pl.ds(o,kc),:]+=nn(p.astype(BF),dp_)
            dkacc[pl.ds(o,kc),:]+=nn(ds,qp)
            return dq+tn(ds,kk[:,0:HD])
        for c in range(nk): dq=step(c,dq)
        dqs[h,pl.ds(off,qb),:]=(dq*0.125).astype(BF)
        @pl.when(i==nq-1)
        def _():
            dks[h]=dkacc[...].astype(BF)
            dvs[h]=dvacc[...].astype(BF)
        @pl.when((i==nq-1)&(h==H-1))
        def _():
            dq_ref[...]=jnp.concatenate([dqs[t,0:Lq,:] for t in range(H)],axis=1)
            dk_ref[...]=jnp.concatenate([dks[t] for t in range(H)],axis=1)
            dv_ref[...]=jnp.concatenate([dvs[t] for t in range(H)],axis=1)
    full=lambda s: pl.BlockSpec(s,lambda h,i:(0,)*len(s))
    return pl.pallas_call(kern,grid=(H,nq),
        out_shape=(jax.ShapeDtypeStruct((Lq,W),BF),jax.ShapeDtypeStruct((Lk,W),BF),jax.ShapeDtypeStruct((Lk,W),BF)),
        in_specs=[full((Lq,W)),full((Lk,W)),full((Lk,W)),full((Lq,W)),full((Lq,W)),full((Lq,128)),full((Lq,HD)),full((Lk,HD))],
        out_specs=(full((Lq,W)),full((Lk,W)),full((Lk,W))),
        scratch_shapes=[pltpu.VMEM((Lk,2*HD),BF),pltpu.VMEM((Lk,2*HD),BF),pltpu.VMEM((Lp,2*HD),BF),pltpu.VMEM((Lp,2*HD),BF),
            pltpu.VMEM((Lk,HD),F32),pltpu.VMEM((Lk,HD),F32),pltpu.VMEM((H,Lp,HD),BF),pltpu.VMEM((H,Lk,HD),BF),pltpu.VMEM((H,Lk,HD),BF)],
        compiler_params=pltpu.CompilerParams(vmem_limit_bytes=60*2**20),name="cross_bwd")(q,k,v,do,of,lse,qa,ka)

def toeplitz(win, shift):
    x=jnp.broadcast_to(win,(128,256))
    return pltpu.roll(x,shift,1,stride=1,stride_axis=0)[:,0:128]

def eye128():
    return lax.broadcasted_iota(jnp.int32,(128,128),0)==lax.broadcasted_iota(jnp.int32,(128,128),1)

def self_fwd(q,k,v,rev,qa,ka):
    Lq,W=q.shape; H=W//HD; nb=Lq//128
    def kern(q_ref,k_ref,v_ref,rev_ref,qa_ref,ka_ref,o_ref,of_ref,lse_ref,qaug,kaug,kdiag,vs,os,tz):
        h=pl.program_id(0)
        for hh in range(H):
            @pl.when(h==hh)
            def _():
                sl=slice(hh*HD,(hh+1)*HD)
                qaug[:,0:HD]=q_ref[:,sl]*BF(0.125); qaug[:,HD:]=qa_ref[...]
                kaug[:,0:HD]=k_ref[:,sl]; kaug[:,HD:]=ka_ref[...]
                kdiag[:,0:HD]=k_ref[:,sl]; kdiag[:,HD:]=jnp.zeros((Lq,HD),BF)
                vs[...]=v_ref[:,sl]
        @pl.when(h==0)
        def _():
            lse_ref[...]=jnp.zeros((Lq,128),F32)
        for d in range(nb):
            tz[d]=toeplitz(rev_ref[pl.ds(h,1),(nb-1-d)*128:(nb+1-d)*128],129)
        eye=eye128()
        lane=lax.broadcasted_iota(jnp.int32,(128,128),1)
        for q0 in range(0,Lq,256):
            qn=min(256,Lq-q0); kend=q0+qn
            s=nt(qaug[q0:q0+qn,:],kaug[0:kend,:])
            for a in range(qn//128):
                qt=q0//128+a
                r0=q0+a*128
                rows=slice(r0,r0+128)
                sd=nt(qaug[rows,:],kdiag[rows,:])
                tiles=[]
                for b in range(qt+1):
                    t=s[a*128:(a+1)*128,b*128:(b+1)*128]
                    if b==qt: t=jnp.where(eye,sd,t)
                    tiles.append(t+tz[qt-b])
                m=tiles[0]
                for t in tiles[1:]: m=jnp.maximum(m,t)
                m=jnp.max(m,axis=1,keepdims=True)
                ps=[jnp.exp(t-m) for t in tiles]
                l=ps[0]
                for t in ps[1:]: l=l+t
                l=jnp.sum(l,axis=1,keepdims=True)
                pb=jnp.concatenate([t.astype(BF) for t in ps],axis=1)
                os[h,rows,:]=nn(pb,vs[0:(qt+1)*128,:])/l
                lse_ref[rows,:]=jnp.where(lane==h,m+jnp.log(l),lse_ref[rows,:])
        @pl.when(h==H-1)
        def _():
            oo=jnp.concatenate([os[t] for t in range(H)],axis=1)
            o_ref[...]=oo.astype(BF)
            of_ref[...]=oo
    full=lambda s: pl.BlockSpec(s,lambda h:(0,)*len(s))
    return pl.pallas_call(kern,grid=(H,),
        out_shape=(jax.ShapeDtypeStruct((Lq,W),BF),jax.ShapeDtypeStruct((Lq,W),F32),jax.ShapeDtypeStruct((Lq,128),F32)),
        in_specs=[full((Lq,W)),full((Lq,W)),full((Lq,W)),full(rev.shape),full((Lq,HD)),full((Lq,HD))],
        out_specs=(full((Lq,W)),full((Lq,W)),full((Lq,128))),
        scratch_shapes=[pltpu.VMEM((Lq,2*HD),BF)]*3+[pltpu.VMEM((Lq,HD),BF),pltpu.VMEM((H,Lq,HD),F32),pltpu.VMEM((nb,128,128),F32)],
        compiler_params=pltpu.CompilerParams(vmem_limit_bytes=48*2**20),name="self_fwd")(q,k,v,rev,qa,ka)

def self_bwd(q,k,v,do,of,lse,fwd,qa,ka):
    Lq,W=q.shape; H=W//HD; nb=Lq//128
    def kern(q_ref,k_ref,v_ref,do_ref,of_ref,lse_ref,fwd_ref,qa_ref,ka_ref,dq_ref,dk_ref,dv_ref,gb_ref,qaug,kaug,kdiag,vaug,doaug,dkacc,dvacc,dqs,dks,dvs,tz,ga):
        h=pl.program_id(0)
        for hh in range(H):
            @pl.when(h==hh)
            def _():
                sl=slice(hh*HD,(hh+1)*HD)
                lane=lax.broadcasted_iota(jnp.int32,(Lq,HD),1)
                kaug[:,0:HD]=k_ref[:,sl]
                ones=(lane>=3)&(lane<6)
                kaug[:,HD:]=jnp.where(ones,BF(1),ka_ref[...])
                kdiag[:,0:HD]=k_ref[:,sl]
                kdiag[:,HD:]=jnp.where(ones,BF(1),BF(0)).astype(BF)
                vaug[:,0:HD]=v_ref[:,sl]
                vaug[:,HD:]=jnp.where(lane<3,BF(1),BF(0)).astype(BF)
                a,b,c=split3(-lse_ref[:,hh:hh+1])
                qaug[:,0:HD]=q_ref[:,sl]*BF(0.125)
                qaug[:,HD:]=jnp.where(lane==3,a,jnp.where(lane==4,b,jnp.where(lane==5,c,qa_ref[...])))
                dd=do_ref[:,sl]
                delta=jnp.sum(dd.astype(F32)*of_ref[:,sl],axis=1,keepdims=True)
                a,b,c=split3(-delta)
                doaug[:,0:HD]=dd
                doaug[:,HD:]=jnp.where(lane==0,a,jnp.where(lane==1,b,jnp.where(lane==2,c,BF(0))))
        dkacc[...]=jnp.zeros_like(dkacc)
        dvacc[...]=jnp.zeros_like(dvacc)
        ga[...]=jnp.zeros_like(ga)
        for d in range(nb):
            tz[d]=toeplitz(fwd_ref[pl.ds(h,1),d*128:(d+2)*128],128)
        eye=eye128()
        for q0 in range(0,Lq,256):
            qn=min(256,Lq-q0); kend=q0+qn
            qg=qaug[q0:kend,:]; dg=doaug[q0:kend,:]
            s=nt(kaug[0:kend,:],qg)
            g=nt(vaug[0:kend,:],dg)
            pcols=[]; dcols=[]
            for a in range(qn//128):
                qt=q0//128+a
                rows=slice(q0+a*128,q0+(a+1)*128)
                sd=nt(kdiag[rows,:],qaug[rows,:])
                pt=[]; dt=[]
                for b in range(kend//128):
                    d=qt-b
                    if d<0:
                        pt.append(jnp.zeros((128,128),BF)); dt.append(jnp.zeros((128,128),BF)); continue
                    t=s[b*128:(b+1)*128,a*128:(a+1)*128]
                    if d==0: t=jnp.where(eye,sd,t)
                    p=jnp.exp(t+tz[d])
                    ds=(p*g[b*128:(b+1)*128,a*128:(a+1)*128]).astype(BF)
                    ga[d]+=ds.astype(F32)
                    pt.append(p.astype(BF)); dt.append(ds)
                pcols.append(jnp.concatenate(pt,axis=0)); dcols.append(jnp.concatenate(dt,axis=0))
            P=jnp.concatenate(pcols,axis=1); DS=jnp.concatenate(dcols,axis=1)
            dvacc[0:kend,:]+=nn(P,dg[:,0:HD])
            dkacc[0:kend,:]+=nn(DS,qg[:,0:HD])
            dqs[h,q0:kend,:]=(tn(DS,kaug[0:kend,0:HD])*0.125).astype(BF)
        dks[h]=dkacc[...].astype(BF)
        dvs[h]=dvacc[...].astype(BF)
        flip=(lax.broadcasted_iota(jnp.int32,(128,128),0)+lax.broadcasted_iota(jnp.int32,(128,128),1)==127).astype(F32)
        for d in range(nb):
            y=lax.dot_general(flip,ga[d],(((1,),(0,)),((),())),preferred_element_type=F32,precision=lax.Precision.HIGHEST)
            x=pltpu.roll(jnp.concatenate([y,jnp.zeros((128,128),F32)],axis=1),1,1,stride=1,stride_axis=0)
            gb_ref[pl.ds(h,1),d*256:(d+1)*256]=jnp.sum(x,axis=0,keepdims=True)
        @pl.when(h==H-1)
        def _():
            dq_ref[...]=jnp.concatenate([dqs[t] for t in range(H)],axis=1)
            dk_ref[...]=jnp.concatenate([dks[t] for t in range(H)],axis=1)
            dv_ref[...]=jnp.concatenate([dvs[t] for t in range(H)],axis=1)
    full=lambda s: pl.BlockSpec(s,lambda h:(0,)*len(s))
    return pl.pallas_call(kern,grid=(H,),
        out_shape=(jax.ShapeDtypeStruct((Lq,W),BF),)*3+(jax.ShapeDtypeStruct((H,nb*256),F32),),
        in_specs=[full((Lq,W))]*5+[full((Lq,128)),full(fwd.shape),full((Lq,HD)),full((Lq,HD))],
        out_specs=(full((Lq,W)),)*3+(full((H,nb*256)),),
        scratch_shapes=[pltpu.VMEM((Lq,2*HD),BF)]*5+[pltpu.VMEM((Lq,HD),F32)]*2+[pltpu.VMEM((H,Lq,HD),BF)]*3+[pltpu.VMEM((nb,128,128),F32)]*2,
        compiler_params=pltpu.CompilerParams(vmem_limit_bytes=48*2**20),name="self_bwd")(q,k,v,do,of,lse,fwd,qa,ka)

def fold_bias(gb,Lq):
    H=gb.shape[0]; nb=Lq//128
    x=gb.reshape(H,nb,2,128)
    low=x[:,:,0].reshape(H,Lq); high=x[:,:,1].reshape(H,Lq)
    return high+jnp.concatenate([low[:,128:],jnp.zeros((H,128),gb.dtype)],axis=1)


def normalize(values, scaling):
    return values * lax.rsqrt(jnp.mean(values * values, -1, keepdims=True) + NORM_EPS) * scaling


def gated(gate_values, up_values):
    return jax.nn.gelu(gate_values, approximate=True) * up_values


def factored_start(gradient, rowwise):
    square = gradient * gradient
    rowwise_new = BETA_TWO * rowwise + (1.0 - BETA_TWO) * jnp.mean(square, 2).T
    return (rowwise_new, jnp.sum(square, 0), jnp.sum(rowwise_new, 1))


def factored_finish(gradient, moment, rowwise_new, colwise, weight, column_sum, row_sum, total_rows):
    colwise_new = BETA_TWO * colwise + (1.0 - BETA_TWO) * (column_sum / total_rows)
    moment_new = BETA_ONE * moment + (1.0 - BETA_ONE) * gradient
    second = rowwise_new.T[:, :, None] * colwise_new[None] / (row_sum / total_rows)[None, :, None]
    stepped = (
        moment_new / (1.0 - BETA_ONE**STEP) / (jnp.sqrt(second / (1.0 - BETA_TWO**STEP)) + ADAM_EPS)
    )
    updated = weight - MATRIX_RATE * (stepped + WEIGHT_DECAY * weight)
    return (moment_new, colwise_new, updated)


def adaptive(gradient, moment, second, weight):
    moment_new = BETA_ONE * moment + (1.0 - BETA_ONE) * gradient
    second_new = BETA_TWO * second + (1.0 - BETA_TWO) * gradient * gradient
    stepped = (
        moment_new
        / (1.0 - BETA_ONE**STEP)
        / (jnp.sqrt(second_new / (1.0 - BETA_TWO**STEP)) + ADAM_EPS)
    )
    return (moment_new, second_new, weight - VECTOR_RATE * stepped)


def make_shards(n, rows):
    devices = n * rows
    both = ("rows", "seq")
    hpd = -(-HEADS // n)
    wd = hpd * HD
    wide = n * wd

    def widen(values):
        extra = wide - values.shape[-1]
        return values if extra == 0 else jnp.pad(values, [(0, 0)] * (values.ndim - 1) + [(0, extra)])

    def to_seq(values):
        return lax.all_to_all(values, "seq", 0, 1, tiled=True)

    def along_seq(values):
        if n % 2:
            return lax.all_gather(values, "seq", axis=0, tiled=True)
        shard = lax.axis_index("seq")
        length = values.shape[0]
        whole = jnp.zeros((n * length,) + values.shape[1:], values.dtype)
        for step in range(0, n, 2):
            block = values
            if step:
                block = lax.ppermute(values, "seq", [(i, (i + step) % n) for i in range(n)])
            beside = lax.ppermute(block, "seq", [(i, i ^ 1) for i in range(n)])
            for part, owner in ((block, shard), (beside, shard ^ 1)):
                place = lax.rem(owner + n - step, n) * length
                whole = lax.dynamic_update_slice_in_dim(whole, part, place, 0)
        return whole

    def own_columns(weight):
        count, j = weight.shape[:2]
        parts = jnp.moveaxis(widen(weight).reshape(count, j, n, wd), 2, 0).reshape(1, n, count, j * wd)
        parts = jnp.broadcast_to(parts, (rows,) + parts.shape[1:]).reshape(devices, count, j * wd)
        return lax.all_to_all(parts, both, 0, 0, tiled=True).reshape(devices * count, j, wd)

    def by_heads(weight):
        count, j = weight.shape[:2]
        return jnp.moveaxis(widen(weight).reshape(count, j, n, wd), 2, 1).reshape(count, n * j * wd)

    def sum_columns(gradient):
        total, width = gradient.shape
        count, j = total // devices, width // wd
        got = lax.all_to_all(gradient.astype(BF).reshape(devices, count, width), both, 0, 0, tiled=True)
        got = jnp.sum(got.reshape(rows, n, count, j, wd).astype(F32), 0)
        return jnp.moveaxis(got, 0, 2).reshape(count, j, wide)[:, :, :D]

    def sum_rows(gradient):
        count, width = D // devices, gradient.shape[1]
        if wide == D and wd == rows * count:
            got = lax.all_to_all(
                gradient.astype(BF).reshape(rows, count, width), "rows", 0, 0, tiled=True
            )
            got = jnp.sum(got.astype(F32), 0)
            places = [(r * n + s, s * rows + r) for r in range(rows) for s in range(n)]
            return lax.ppermute(got, both, places)
        whole = lax.dynamic_update_slice_in_dim(
            jnp.zeros((wide, width), BF), gradient.astype(BF), lax.axis_index("seq") * wd, 0
        )[:D]
        return lax.psum_scatter(whole, both, scatter_dimension=0, tiled=True).astype(F32)

    def shards(
        decoder_input,
        encoder_output,
        cotangent,
        decoder_segment,
        decoder_padding,
        encoder_segment,
        encoder_padding,
        distance_bucket,
        attention_weight,
        attention_moment,
        attention_rowwise,
        attention_colwise,
        expand_weight,
        expand_moment,
        expand_rowwise,
        expand_colwise,
        contract_weight,
        contract_moment,
        contract_rowwise,
        contract_colwise,
        norm_gain,
        gain_moment,
        gain_second,
        relative_table,
        table_moment,
        table_second,
    ):
        shard = lax.axis_index("seq")
        length = decoder_segment.shape[1]
        attention_low = attention_weight.astype(BF)
        first_columns = own_columns(attention_low[:, 0:3]).reshape(D, 3 * wd)
        row_input = along_seq(decoder_input[0])
        attention_full = lax.all_gather(
            jnp.concatenate(
                (
                    attention_low[:, 3],
                    attention_low[:, 7],
                    by_heads(attention_low[:, 4:5]),
                    by_heads(attention_low[:, 5:7]),
                    by_heads(attention_low[:, 0:3]),
                ),
                1,
            ),
            both, axis=0, tiled=True,
        )
        row_encoder = along_seq(encoder_output[0])
        expand_full = lax.all_gather(
            expand_weight.astype(BF).reshape(-1, 2 * FF), both, axis=0, tiled=True
        )
        contract_full = lax.all_gather(contract_weight.astype(BF), both, axis=0, tiled=True)
        edges = (0, D, 2 * D, 2 * D + wide, 2 * D + 3 * wide, 2 * D + 6 * wide)
        self_out_weight, cross_out_weight, cross_query_weight, cross_pair_weight, first_weight = (
            attention_full[:, low:high] for low, high in zip(edges[:-1], edges[1:])
        )
        cross_query_columns = lax.dynamic_slice_in_dim(cross_query_weight, shard * wd, wd, 1)
        cross_columns = lax.dynamic_slice_in_dim(cross_pair_weight, shard * 2 * wd, 2 * wd, 1)

        def own_rows(matrix):
            padded = jnp.pad(matrix, ((0, wide - D), (0, 0))) if wide > D else matrix
            return lax.dynamic_slice_in_dim(padded, shard * wd, wd, 0)

        document = jnp.arange(HD, dtype=jnp.int32)[None, :]
        decoder_document = decoder_segment[0][:, None] == document
        query_side = decoder_document.astype(BF)
        self_side = jnp.where(
            (document < 3) & ~(decoder_document & (decoder_padding[0][:, None] == 1)), NEG, 0.0
        ).astype(BF)
        cross_side = jnp.where(
            (document < 3)
            & ~((encoder_segment[0][:, None] == document) & (encoder_padding[0][:, None] == 1)),
            NEG,
            0.0,
        ).astype(BF)
        onehot = (
            distance_bucket[:, None] == jnp.arange(BUCKETS, dtype=jnp.int32)[None, :]
        ).astype(F32)
        table_own = lax.dynamic_slice_in_dim(
            jnp.pad(relative_table, ((0, 0), (0, n * hpd - HEADS))), shard * hpd, hpd, 1
        )
        bias = jnp.einsum("db,bh->hd", onehot, table_own, precision=HIGHEST)
        beyond = jnp.full((hpd, 128), NEG, F32)
        bias_forward = jnp.concatenate((beyond, bias), 1)
        bias_backward = jnp.concatenate((bias[:, ::-1], beyond), 1)

        def dot(left, right):
            return jnp.dot(left, right, preferred_element_type=F32)

        def dot_back(left, right):
            return lax.dot_general(left, right, (((1,), (1,)), ((), ())), preferred_element_type=F32)

        def outer(left, right):
            return lax.dot_general(left, right, (((0,), (0,)), ((), ())), preferred_element_type=F32)

        row_norm = normalize(row_input.astype(F32), norm_gain[0]).astype(BF)
        self_proj = dot(row_norm, first_columns).astype(BF)
        query, key, value = (
            self_proj[:, 0:wd],
            self_proj[:, wd : 2 * wd],
            self_proj[:, 2 * wd : 3 * wd],
        )
        self_heads, self_exact, self_lse = self_fwd(
            query, key, value, bias_backward, query_side, self_side
        )
        inputs = decoder_input[0].astype(F32)
        self_out = to_seq(self_heads)[:, :D]
        after_self = inputs + dot(self_out, self_out_weight)
        cross_norm = normalize(after_self, norm_gain[1]).astype(BF)
        row_cross_norm = along_seq(cross_norm)
        cross_query = dot(row_cross_norm, cross_query_columns).astype(BF)
        cross_pair = dot(row_encoder, cross_columns).astype(BF)
        cross_key, cross_value = cross_pair[:, 0:wd], cross_pair[:, wd : 2 * wd]
        cross_heads, cross_exact, cross_lse = cross_fwd(
            cross_query, cross_key, cross_value, query_side, cross_side
        )
        cross_out = to_seq(cross_heads)[:, :D]
        after_cross = after_self + dot(cross_out, cross_out_weight)
        feed_norm = normalize(after_cross, norm_gain[2]).astype(BF)
        hidden_pair = dot(feed_norm, expand_full)
        gate_values, up_values = hidden_pair[:, 0:FF], hidden_pair[:, FF:]
        feed_branch = cotangent[0]
        grad_result = feed_branch.astype(F32)
        grad_hidden = dot_back(feed_branch, contract_full)
        hidden_wide, gated_back = jax.vjp(gated, gate_values, up_values)
        hidden = hidden_wide.astype(BF)
        layer_output = (after_cross + dot(hidden, contract_full)).astype(BF)
        grad_gate, grad_up = gated_back(grad_hidden)
        grad_pair = jnp.concatenate((grad_gate.astype(BF), grad_up.astype(BF)), 1)
        unused_norm, norm_back = jax.vjp(normalize, after_cross, norm_gain[2])
        feed_part, feed_gain = norm_back(dot_back(grad_pair, expand_full))
        grad_after_cross = grad_result + feed_part
        cross_branch = grad_after_cross.astype(BF)
        row_cross_branch = along_seq(cross_branch)
        cross_grad = dot_back(row_cross_branch, own_rows(cross_out_weight)).astype(BF)
        cross_out_sum = sum_rows(outer(cross_heads, row_cross_branch))
        contract_sum = lax.psum_scatter(
            outer(hidden, feed_branch).astype(BF), both, scatter_dimension=0, tiled=True
        ).astype(F32)
        expand_sum = lax.psum_scatter(
            outer(feed_norm, grad_pair).astype(BF), both, scatter_dimension=0, tiled=True
        ).astype(F32).reshape(-1, 2, FF)
        cross_qgrad, cross_kgrad, cross_vgrad = cross_bwd(
            cross_query, cross_key, cross_value, cross_grad, cross_exact, cross_lse, query_side, cross_side
        )
        grad_cross_query = to_seq(cross_qgrad)
        unused_norm, norm_back = jax.vjp(normalize, after_self, norm_gain[1])
        cross_part, cross_gain = norm_back(dot_back(grad_cross_query, cross_query_weight))
        grad_after_self = grad_after_cross + cross_part
        self_branch = grad_after_self.astype(BF)
        row_self_branch = along_seq(self_branch)
        self_grad = dot_back(row_self_branch, own_rows(self_out_weight)).astype(BF)
        self_out_sum = sum_rows(outer(self_heads, row_self_branch))
        cross_grads = jnp.concatenate((cross_kgrad, cross_vgrad), 1)
        cross_sum = sum_columns(
            jnp.concatenate(
                (outer(row_cross_norm, cross_qgrad), outer(row_encoder, cross_grads)), 1
            )
        )
        encoder_gradient = dot_back(
            to_seq(cross_grads), cross_pair_weight
        )
        self_qgrad, self_kgrad, self_vgrad, pair_bias = self_bwd(
            query, key, value, self_grad, self_exact, self_lse, bias_forward, query_side, self_side
        )
        grad_bias = fold_bias(pair_bias, length)
        table_own_grad = jnp.einsum("hd,db->bh", grad_bias, onehot, precision=HIGHEST)
        table_local = lax.dynamic_update_slice_in_dim(
            jnp.zeros((BUCKETS, n * hpd), F32), table_own_grad, shard * hpd, 1
        )[:, :HEADS]
        self_grads = jnp.concatenate((self_qgrad, self_kgrad, self_vgrad), 1)
        self_sum = sum_columns(outer(row_norm, self_grads))
        unused_norm, norm_back = jax.vjp(normalize, inputs, norm_gain[0])
        self_part, self_gain = norm_back(
            dot_back(to_seq(self_grads), first_weight)
        )
        input_gradient = grad_after_self + self_part

        attention_sum = jnp.concatenate(
            (self_sum, self_out_sum[:, None], cross_sum, cross_out_sum[:, None]), 1
        )
        attention_rows, attention_columns, attention_rowsum = factored_start(
            attention_sum, attention_rowwise
        )
        expand_rows, expand_columns, expand_rowsum = factored_start(expand_sum, expand_rowwise)
        contract_rows, contract_columns, contract_rowsum = factored_start(
            contract_sum[:, None, :], contract_rowwise[None, :]
        )
        gain_local = jnp.stack((self_gain, cross_gain, feed_gain), 0)
        (
            attention_total,
            expand_total,
            contract_total,
            attention_rowtotal,
            expand_rowtotal,
            contract_rowtotal,
            gain_gradient,
            table_gradient,
        ) = lax.psum(
            (
                attention_columns,
                expand_columns,
                contract_columns,
                attention_rowsum,
                expand_rowsum,
                contract_rowsum,
                gain_local,
                table_local,
            ),
            both,
        )
        attention_new = factored_finish(
            attention_sum,
            attention_moment,
            attention_rows,
            attention_colwise,
            attention_weight,
            attention_total,
            attention_rowtotal,
            D,
        )
        expand_new = factored_finish(
            expand_sum,
            expand_moment,
            expand_rows,
            expand_colwise,
            expand_weight,
            expand_total,
            expand_rowtotal,
            D,
        )
        contract_new = factored_finish(
            contract_sum[:, None, :],
            contract_moment[:, None, :],
            contract_rows,
            contract_colwise[None, :],
            contract_weight[:, None, :],
            contract_total,
            contract_rowtotal,
            FF,
        )
        gain_new = adaptive(gain_gradient, gain_moment, gain_second, norm_gain)
        table_new = adaptive(table_gradient, table_moment, table_second, relative_table)
        return (
            layer_output[None],
            input_gradient[None],
            encoder_gradient[None],
            attention_sum,
            attention_new[0],
            attention_rows,
            attention_new[1],
            attention_new[2],
            expand_sum,
            expand_new[0],
            expand_rows,
            expand_new[1],
            expand_new[2],
            contract_sum,
            contract_new[0][:, 0],
            contract_rows[0],
            contract_new[1][0],
            contract_new[2][:, 0],
            gain_gradient,
            gain_new[0],
            gain_new[1],
            gain_new[2],
            table_gradient,
            table_new[0],
            table_new[1],
            table_new[2],
        )

    return shards


def solution(mesh):
    placed = (
        P("rows", "seq", None),
        P("rows", "seq", None),
        P("rows", "seq", None),
        P("rows", None),
        P("rows", None),
        P("rows", None),
        P("rows", None),
        P(),
        P(("rows", "seq"), None, None),
        P(("rows", "seq"), None, None),
        P(None, ("rows", "seq")),
        P(),
        P(("rows", "seq"), None, None),
        P(("rows", "seq"), None, None),
        P(None, ("rows", "seq")),
        P(),
        P(("rows", "seq"), None),
        P(("rows", "seq"), None),
        P(("rows", "seq")),
        P(),
        P(),
        P(),
        P(),
        P(),
        P(),
        P(),
    )
    return jax.shard_map(
        make_shards(mesh.shape["seq"], mesh.shape["rows"]),
        mesh=mesh,
        in_specs=placed,
        out_specs=(
            P("rows", "seq", None),
            P("rows", "seq", None),
            P("rows", "seq", None),
            P(("rows", "seq"), None, None),
            P(("rows", "seq"), None, None),
            P(None, ("rows", "seq")),
            P(),
            P(("rows", "seq"), None, None),
            P(("rows", "seq"), None, None),
            P(("rows", "seq"), None, None),
            P(None, ("rows", "seq")),
            P(),
            P(("rows", "seq"), None, None),
            P(("rows", "seq"), None),
            P(("rows", "seq"), None),
            P(("rows", "seq")),
            P(),
            P(("rows", "seq"), None),
            P(),
            P(),
            P(),
            P(),
            P(),
            P(),
            P(),
            P(),
        ),
        check_vma=False,
    )
```

```python
import jax
import jax.numpy as jnp
from jax import lax
from jax.experimental import pallas as pl
from jax.experimental.pallas import tpu as pltpu
from jax.sharding import PartitionSpec as P

D = 768
FF = 2048
HEADS = 12
BUCKETS = 32
STEP = 10
HIGHEST = lax.Precision.HIGHEST
NORM_EPS = 1e-06
BETA_ONE = 0.9
BETA_TWO = 0.999
ADAM_EPS = 1e-08
WEIGHT_DECAY = 0.01
MATRIX_RATE = 0.15
VECTOR_RATE = 1.0
HD = 64
NEG = -1e30
F32 = jnp.float32
BF = jnp.bfloat16

def nt(a,b): return lax.dot_general(a,b,(((1,),(1,)),((),())),preferred_element_type=F32)
def nn(a,b): return lax.dot_general(a,b,(((1,),(0,)),((),())),preferred_element_type=F32)
def tn(a,b): return lax.dot_general(a,b,(((0,),(0,)),((),())),preferred_element_type=F32)

def cross_fwd(q,kv,qa,ka,qb=352,kc=1024):
    Lq,W=q.shape; Lk=kv.shape[0]; H=W//HD
    nk=Lk//kc
    def kern(q_ref,kv_ref,qa_ref,ka_ref,o_ref,of_ref,lse_ref,kaug,vs,s_s,m_s,l_s,acc):
        @pl.when(pl.program_id(0)==0)
        def _():
            for h in range(H):
                kaug[h,:,0:HD]=kv_ref[:,2*h*HD:(2*h+1)*HD]
                kaug[h,:,HD:2*HD]=ka_ref[...]
                vs[h]=kv_ref[:,(2*h+1)*HD:(2*h+2)*HD]
        lane=lax.broadcasted_iota(jnp.int32,(qb,128),1)
        lses=jnp.zeros((qb,128),F32)
        outs=[]
        for h in range(H):
            qh=(q_ref[:,h*HD:(h+1)*HD]*BF(0.125)).astype(BF)
            qg=jnp.concatenate([qh,qa_ref[...]],axis=1)
            m_s[...]=jnp.full((qb,128),-3e38,F32)
            for c in range(nk):
                s=nt(qg,kaug[h,c*kc:(c+1)*kc,:])
                s_s[:,c*kc:(c+1)*kc]=s
                mm=m_s[...]
                for t in range(kc//128): mm=jnp.maximum(mm,s[:,t*128:(t+1)*128])
                m_s[...]=mm
            m=jnp.max(m_s[...],axis=1,keepdims=True)
            l_s[...]=jnp.zeros((qb,128),F32)
            acc[...]=jnp.zeros((qb,HD),F32)
            for c in range(nk):
                p=jnp.exp(s_s[:,c*kc:(c+1)*kc]-m)
                ll=l_s[...]
                for t in range(kc//128): ll=ll+p[:,t*128:(t+1)*128]
                l_s[...]=ll
                acc[...]+=nn(p.astype(BF),vs[h,c*kc:(c+1)*kc,:])
            l=jnp.sum(l_s[...],axis=1,keepdims=True)
            o=acc[...]/l
            outs.append(o)
            lses=jnp.where(lane==h,m+jnp.log(l),lses)
        oo=jnp.concatenate(outs,axis=1)
        o_ref[...]=oo.astype(BF)
        of_ref[...]=oo
        lse_ref[...]=lses
    full=lambda s: pl.BlockSpec(s,lambda i:(0,)*len(s))
    row=lambda w: pl.BlockSpec((qb,w),lambda i:(i,0))
    return pl.pallas_call(kern,grid=(Lq//qb,),
        out_shape=(jax.ShapeDtypeStruct((Lq,W),BF),jax.ShapeDtypeStruct((Lq,W),F32),jax.ShapeDtypeStruct((Lq,128),F32)),
        in_specs=[row(W),full((Lk,2*W)),row(HD),full((Lk,HD))],
        out_specs=(row(W),row(W),row(128)),
        scratch_shapes=[pltpu.VMEM((H,Lk,2*HD),BF),pltpu.VMEM((H,Lk,HD),BF),pltpu.VMEM((qb,Lk),F32),pltpu.VMEM((qb,128),F32),pltpu.VMEM((qb,128),F32),pltpu.VMEM((qb,HD),F32)],
        compiler_params=pltpu.CompilerParams(vmem_limit_bytes=56*2**20),cost_estimate=cost(31.0),name="cross_fwd")(q,kv,qa,ka)

def split3(x):
    a=x.astype(BF); r=x-a.astype(F32)
    b=r.astype(BF); c=(r-b.astype(F32)).astype(BF)
    return a,b,c

def cross_bwd(q,kv,do,of,lse,qa,ka,n,qb=256,kc=1024):
    Lq,W=q.shape; Lk=kv.shape[0]; H=W//HD
    nq=-(-Lq//qb); Lp=nq*qb; nk=Lk//kc
    def kern(q_ref,kv_ref,do_ref,of_ref,lse_ref,qa_ref,ka_ref,dq_ref,home_ref,dqw,last_ref,*rest):
        dkv_refs=rest[:n]
        (kaug,vaug,qaug,doaug,dkacc,dvacc,dqs,dkvs,q_out,q_in,kv_out,kv_in,own)=rest[n:]
        h=pl.program_id(0); i=pl.program_id(1)
        r,s=lax.axis_index("rows"),lax.axis_index("seq")
        def home(p,hh):
            rows=slice(p*(Lk//n),(p+1)*(Lk//n))
            peer=s^p
            return pltpu.make_async_remote_copy(src_ref=dkvs.at[hh,rows],dst_ref=home_ref.at[s,hh],send_sem=kv_out.at[p,hh],
                recv_sem=kv_in.at[p,hh],device_id=(r,peer),device_id_type=MESH)
        def keep(hh):
            return pltpu.make_async_copy(dkvs.at[hh,0:Lk//n],home_ref.at[s,hh],own.at[hh])
        def turn(p):
            return pltpu.make_async_remote_copy(src_ref=dqw.at[s^p],dst_ref=dq_ref.at[s],send_sem=q_out.at[p],
                recv_sem=q_in.at[p],device_id=(r,s^p),device_id_type=MESH)
        def stay():
            return pltpu.make_async_copy(dqw.at[s],dq_ref.at[s],own.at[H])
        @pl.when((h==0)&(i==0))
        def _():
            barrier=pltpu.get_barrier_semaphore()
            for p in range(1,n):
                pl.semaphore_signal(barrier,inc=1,device_id=(r,s^p),device_id_type=MESH)
            pl.semaphore_wait(barrier,n-1)
        for hh in range(H):
            @pl.when((h==hh)&(i==0))
            def _():
                sl=slice(hh*HD,(hh+1)*HD)
                kaug[:,0:HD]=kv_ref[:,2*hh*HD:(2*hh+1)*HD]
                lane=lax.broadcasted_iota(jnp.int32,(Lk,HD),1)
                kaug[:,HD:2*HD]=jnp.where((lane>=3)&(lane<6),BF(1),ka_ref[...])
                vaug[:,0:HD]=kv_ref[:,(2*hh+1)*HD:(2*hh+2)*HD]
                vaug[:,HD:2*HD]=jnp.where(lane<3,BF(1),BF(0)).astype(BF)
                lq=lax.broadcasted_iota(jnp.int32,(Lq,HD),1)
                a,b,c=split3(-lse_ref[:,hh:hh+1])
                aug=jnp.where(lq==3,a,jnp.where(lq==4,b,jnp.where(lq==5,c,qa_ref[...])))
                qaug[0:Lq,0:HD]=q_ref[:,sl]*BF(0.125)
                qaug[0:Lq,HD:2*HD]=aug
                dd=do_ref[:,sl]
                delta=jnp.sum(dd.astype(F32)*of_ref[:,sl],axis=1,keepdims=True)
                a,b,c=split3(-delta)
                aug=jnp.where(lq==0,a,jnp.where(lq==1,b,jnp.where(lq==2,c,BF(0))))
                doaug[0:Lq,0:HD]=dd
                doaug[0:Lq,HD:2*HD]=aug
                if Lp>Lq:
                    qaug[Lq:Lp,:]=jnp.zeros((Lp-Lq,2*HD),BF)
                    doaug[Lq:Lp,:]=jnp.zeros((Lp-Lq,2*HD),BF)
                dkacc[...]=jnp.zeros_like(dkacc)
                dvacc[...]=jnp.zeros_like(dvacc)
        off=pl.multiple_of(i*qb,qb)
        qg=qaug[pl.ds(off,qb),:]
        dg=doaug[pl.ds(off,qb),:]
        qp=qg[:,0:HD]; dp_=dg[:,0:HD]
        dq=jnp.zeros((qb,HD),F32)
        def step(c,dq):
            o=pl.multiple_of(c*kc,kc)
            kk=kaug[pl.ds(o,kc),:]
            p=jnp.exp(nt(kk,qg))
            g=nt(vaug[pl.ds(o,kc),:],dg)
            ds=(p*g).astype(BF)
            dvacc[pl.ds(o,kc),:]+=nn(p.astype(BF),dp_)
            dkacc[pl.ds(o,kc),:]+=nn(ds,qp)
            return dq+tn(ds,kk[:,0:HD])
        for c in range(nk): dq=step(c,dq)
        dqs[h,pl.ds(off,qb),:]=(dq*0.125).astype(BF)
        for hh in range(H):
            @pl.when((i==nq-1)&(h==hh))
            def _():
                dkvs[hh,:,0:HD]=dkacc[...].astype(BF)
                dkvs[hh,:,HD:]=dvacc[...].astype(BF)
                if hh==H-1:
                    for b in range(n):
                        dqw[b]=jnp.concatenate([dqs[t,b*(Lq//n):(b+1)*(Lq//n),:] for t in range(H)],axis=1)
                    for p in range(1,n): turn(p).start()
                    stay().start()
                else:
                    for p in range(1,n): home(p,hh).start()
                    keep(hh).start()
        @pl.when((i==nq-1)&(h==H-1))
        def _():
            for b,dkv_ref in enumerate(dkv_refs):
                part=slice(b*(Lk//n),(b+1)*(Lk//n))
                for t in range(H): dkv_ref[:,2*t*HD:2*(t+1)*HD]=dkvs[t,part,:]
                last_ref[b]=dkvs[H-1,part,:]
            for p in range(1,n): turn(p).wait()
            stay().wait()
            for hh in range(H-1):
                for p in range(1,n): home(p,hh).wait()
                keep(hh).wait()
    full=lambda s: pl.BlockSpec(s,lambda h,i:(0,)*len(s))
    return pl.pallas_call(kern,grid=(H,nq),
        out_shape=(jax.ShapeDtypeStruct((n,Lq//n,W),BF),jax.ShapeDtypeStruct((n,H-1,Lk//n,2*HD),BF),jax.ShapeDtypeStruct((n,Lq//n,W),BF),jax.ShapeDtypeStruct((n,Lk//n,2*HD),BF))+(jax.ShapeDtypeStruct((Lk//n,2*W),BF),)*n,
        in_specs=[full((Lq,W)),full((Lk,2*W)),full((Lq,W)),full((Lq,W)),full((Lq,128)),full((Lq,HD)),full((Lk,HD))],
        out_specs=(ANY,ANY,full((n,Lq//n,W)),full((n,Lk//n,2*HD)))+(full((Lk//n,2*W)),)*n,
        scratch_shapes=[pltpu.VMEM((Lk,2*HD),BF),pltpu.VMEM((Lk,2*HD),BF),pltpu.VMEM((Lp,2*HD),BF),pltpu.VMEM((Lp,2*HD),BF),
            pltpu.VMEM((Lk,HD),F32),pltpu.VMEM((Lk,HD),F32),pltpu.VMEM((H,Lp,HD),BF),pltpu.VMEM((H,Lk,2*HD),BF)]
            +[pltpu.SemaphoreType.DMA((n,))]*2+[pltpu.SemaphoreType.DMA((n,H))]*2+[pltpu.SemaphoreType.DMA((H+1,))],
        compiler_params=pltpu.CompilerParams(vmem_limit_bytes=60*2**20,collective_id=10,has_side_effects=True),cost_estimate=cost(68.0),name="cross_bwd")(q,kv,do,of,lse,qa,ka)

def toeplitz(win, shift):
    x=jnp.broadcast_to(win,(128,256))
    return pltpu.roll(x,shift,1,stride=1,stride_axis=0)[:,0:128]

def eye128():
    return lax.broadcasted_iota(jnp.int32,(128,128),0)==lax.broadcasted_iota(jnp.int32,(128,128),1)

def self_fwd(qkv,rev,qa,ka):
    Lq,W=qkv.shape[0],qkv.shape[1]//3; H=W//HD; nb=Lq//128
    def kern(qkv_ref,rev_ref,qa_ref,ka_ref,o_ref,of_ref,lse_ref,qaug,kaug,kdiag,vs,os,tz):
        h=pl.program_id(0)
        for hh in range(H):
            @pl.when(h==hh)
            def _():
                sl=slice(hh*HD,(hh+1)*HD)
                qaug[:,0:HD]=qkv_ref[:,sl]*BF(0.125); qaug[:,HD:]=qa_ref[...]
                kaug[:,0:HD]=qkv_ref[:,W+hh*HD:W+(hh+1)*HD]; kaug[:,HD:]=ka_ref[...]
                kdiag[:,0:HD]=qkv_ref[:,W+hh*HD:W+(hh+1)*HD]; kdiag[:,HD:]=jnp.zeros((Lq,HD),BF)
                vs[...]=qkv_ref[:,2*W+hh*HD:2*W+(hh+1)*HD]
        @pl.when(h==0)
        def _():
            lse_ref[...]=jnp.zeros((Lq,128),F32)
        for d in range(nb):
            tz[d]=toeplitz(rev_ref[pl.ds(h,1),(nb-1-d)*128:(nb+1-d)*128],129)
        eye=eye128()
        lane=lax.broadcasted_iota(jnp.int32,(128,128),1)
        for q0 in range(0,Lq,256):
            qn=min(256,Lq-q0); kend=q0+qn
            s=nt(qaug[q0:q0+qn,:],kaug[0:kend,:])
            for a in range(qn//128):
                qt=q0//128+a
                r0=q0+a*128
                rows=slice(r0,r0+128)
                sd=nt(qaug[rows,:],kdiag[rows,:])
                tiles=[]
                for b in range(qt+1):
                    t=s[a*128:(a+1)*128,b*128:(b+1)*128]
                    if b==qt: t=jnp.where(eye,sd,t)
                    tiles.append(t+tz[qt-b])
                m=tiles[0]
                for t in tiles[1:]: m=jnp.maximum(m,t)
                m=jnp.max(m,axis=1,keepdims=True)
                ps=[jnp.exp(t-m) for t in tiles]
                l=ps[0]
                for t in ps[1:]: l=l+t
                l=jnp.sum(l,axis=1,keepdims=True)
                pb=jnp.concatenate([t.astype(BF) for t in ps],axis=1)
                os[h,rows,:]=nn(pb,vs[0:(qt+1)*128,:])/l
                lse_ref[rows,:]=jnp.where(lane==h,m+jnp.log(l),lse_ref[rows,:])
        @pl.when(h==H-1)
        def _():
            oo=jnp.concatenate([os[t] for t in range(H)],axis=1)
            o_ref[...]=oo.astype(BF)
            of_ref[...]=oo
    full=lambda s: pl.BlockSpec(s,lambda h:(0,)*len(s))
    return pl.pallas_call(kern,grid=(H,),
        out_shape=(jax.ShapeDtypeStruct((Lq,W),BF),jax.ShapeDtypeStruct((Lq,W),F32),jax.ShapeDtypeStruct((Lq,128),F32)),
        in_specs=[full((Lq,3*W)),full(rev.shape),full((Lq,HD)),full((Lq,HD))],
        out_specs=(full((Lq,W)),full((Lq,W)),full((Lq,128))),
        scratch_shapes=[pltpu.VMEM((Lq,2*HD),BF)]*3+[pltpu.VMEM((Lq,HD),BF),pltpu.VMEM((H,Lq,HD),F32),pltpu.VMEM((nb,128,128),F32)],
        compiler_params=pltpu.CompilerParams(vmem_limit_bytes=48*2**20),cost_estimate=cost(15.0),name="self_fwd")(qkv,rev,qa,ka)

MESH = pl.DeviceIdType.MESH
ANY = pl.BlockSpec(memory_space=pl.ANY)
VM = pl.BlockSpec(memory_space=pltpu.VMEM)


def cost(micros):
    return pl.CostEstimate(flops=int(micros * 1.0e9), bytes_accessed=int(micros * 3.0e6), transcendentals=0)


def greet_all(count, n):
    r, s = lax.axis_index("rows"), lax.axis_index("seq")
    barrier = pltpu.get_barrier_semaphore()

    def greet(step, carry):
        j = lax.rem((s if count == n else r * n + s) + step, count)
        device = (r, j) if count == n else (lax.div(j, n), lax.rem(j, n))
        pl.semaphore_signal(barrier, inc=1, device_id=device, device_id_type=MESH)
        return carry

    lax.fori_loop(1, count, greet, 0)
    pl.semaphore_wait(barrier, count - 1)


class Exchange:
    def __init__(self, plans, n, rows):
        self.kinds = [kind for kind, x in plans]
        self.count = len(plans)
        self.n, self.rows = n, rows
        shapes = [(n * rows,) + x.shape[1:] if kind == "own" else x.shape for kind, x in plans]
        self.shapes = tuple(jax.ShapeDtypeStruct(shape, x.dtype) for shape, (kind, x) in zip(shapes, plans))
        self.scratch = [pltpu.SemaphoreType.DMA((shape[0],)) for shape in shapes for side in range(2)]
        self.scratch += [pltpu.SemaphoreType.DMA((self.count,))]

    def each(self, sent, got, sems, act):
        n, rows = self.n, self.rows
        r, s = lax.axis_index("rows"), lax.axis_index("seq")
        me = r * n + s
        for p, kind in enumerate(self.kinds):
            x, y, out_sem, in_sem, own = sent[p], got[p], sems[2 * p], sems[2 * p + 1], sems[-1].at[p]

            def remote(block, slot, device, leave, arrive, x=x, y=y, out_sem=out_sem, in_sem=in_sem):
                return pltpu.make_async_remote_copy(
                    src_ref=x.at[block], dst_ref=y.at[slot], send_sem=out_sem.at[leave], recv_sem=in_sem.at[arrive],
                    device_id=device, device_id_type=MESH,
                )

            if kind == "rows":
                def send(j, carry, act=act, x=x, y=y, own=own, remote=remote):
                    target = s * rows + j
                    away = remote(j, r, (lax.div(target, n), lax.rem(target, n)), j, r)

                    @pl.when(target != me)
                    def _():
                        act(away, True)

                    @pl.when(target == me)
                    def _():
                        act(pltpu.make_async_copy(x.at[j], y.at[r], own), None)

                    return carry

                def take(q, carry, act=act, remote=remote):
                    @pl.when((q != r) | (lax.div(me, rows) != s))
                    def _():
                        act(remote(0, q, (r, s), 0, q), False)

                    return carry

                lax.fori_loop(0, rows, send, 0)
                lax.fori_loop(0, rows, take, 0)
                continue
            if kind == "xor":
                act(pltpu.make_async_copy(x.at[0], y.at[s], own), None)
                for p in range(1, n):
                    away = remote(p, s, (r, s ^ p), p, p)
                    act(away, True)
                    act(away, False)
                continue
            length, here = (n, s) if kind == "seq" else (n * rows, me)
            act(pltpu.make_async_copy(x.at[s if kind == "own" else here], y.at[here], own), None)

            def both_ways(step, carry, act=act, length=length, here=here, kind=kind, remote=remote):
                j = lax.rem(here + step, length)
                device = (r, j) if kind == "seq" else (lax.div(j, n), lax.rem(j, n))
                away = remote(lax.rem(j, n) if kind == "own" else j, here, device, step, step)
                act(away, True)
                act(away, False)
                return carry

            lax.fori_loop(1, length, both_ways, 0)

    def start(self, sent, got, sems, greet=True):
        near = all(kind == "seq" for kind in self.kinds)
        if greet:
            greet_all(self.n if near else self.n * self.rows, self.n)
        self.each(sent, got, sems, lambda copy, away: copy.start() if away is not False else None)

    def wait(self, sent, got, sems):
        def act(copy, away):
            if away is None:
                copy.wait()
            elif away:
                copy.wait_send()
            else:
                copy.wait_recv()

        self.each(sent, got, sems, act)


class Job:
    def __init__(self, inputs=(), outs=(), body=None):
        self.inputs, self.outs, self.body = list(inputs), tuple(outs), body
        self.scratch = [pltpu.VMEM(x.shape, x.dtype) for x in self.inputs]
        self.scratch += [pltpu.SemaphoreType.DMA((len(self.inputs),))] if self.inputs else []

    def split(self, refs, before, between, after):
        i, o = len(self.inputs), len(self.outs)
        head, refs = refs[:before], refs[before:]
        ins, refs = refs[:i], refs[i:]
        middle, refs = refs[:between], refs[between:]
        outs, refs = refs[:o], refs[o:]
        return head + middle + refs[:after], ins, outs, refs[after:]

    def run(self, ins, outs, scratch):
        if not self.inputs:
            return
        held, sem = scratch[:-1], scratch[-1]
        copies = [pltpu.make_async_copy(x, y, sem.at[k]) for k, (x, y) in enumerate(zip(ins, held))]
        for copy in copies:
            copy.start()
        for copy in copies:
            copy.wait()
        self.body(held, outs)


def exchange(plans, n, rows, collective_id, job=None):
    ride, job = Exchange(plans, n, rows), job or Job()

    def kern(*refs):
        refs, ins, outs, scratch = job.split(refs, ride.count, ride.count, len(ride.scratch))
        sent, got, sems = refs[: ride.count], refs[ride.count : 2 * ride.count], refs[2 * ride.count :]
        ride.start(sent, got, sems)
        job.run(ins, outs, scratch)
        ride.wait(sent, got, sems)

    return pl.pallas_call(
        kern,
        out_shape=ride.shapes + job.outs,
        in_specs=[ANY] * (ride.count + len(job.inputs)),
        out_specs=(ANY,) * ride.count + (VM,) * len(job.outs),
        scratch_shapes=ride.scratch + job.scratch,
        compiler_params=pltpu.CompilerParams(
            collective_id=collective_id, has_side_effects=True, vmem_limit_bytes=56 * 2**20
        ),
        cost_estimate=cost(20.0),name="exchange",
    )(*[x for kind, x in plans], *job.inputs)


def gather_seq(values, n, rows, collective_id, plans=(), job=None):
    ride, job = Exchange(plans, n, rows), job or Job()
    sems_used = ride.scratch if ride.count else []

    def kern(*refs):
        refs, ins, outs, scratch = job.split(refs, 1 + ride.count, 1 + ride.count, 5 + len(sems_used))
        x_ref, sent, o_ref = refs[0], refs[1 : 1 + ride.count], refs[1 + ride.count]
        got, rest = refs[2 + ride.count : 2 + 2 * ride.count], refs[2 + 2 * ride.count :]
        own, out_sem, in_sem, side_out, side_in = rest[:5]
        sems = rest[5:]
        r, s = lax.axis_index("rows"), lax.axis_index("seq")
        beside = s + 1 - 2 * lax.rem(s, 2)
        if ride.count:
            greet_all(n * rows, n)
        else:
            barrier = pltpu.get_barrier_semaphore()
            for step in range(2, n, 2):
                pl.semaphore_signal(barrier, inc=1, device_id=(r, lax.rem(s + step, n)), device_id_type=MESH)
            pl.semaphore_signal(barrier, inc=1, device_id=(r, beside), device_id_type=MESH)
            pl.semaphore_wait(barrier, n // 2)
        far = [
            pltpu.make_async_remote_copy(
                src_ref=x_ref, dst_ref=o_ref.at[s], send_sem=out_sem.at[k], recv_sem=in_sem.at[k],
                device_id=(r, lax.rem(s + 2 * k, n)), device_id_type=MESH,
            )
            for k in range(1, n // 2)
        ]
        for copy in far:
            copy.start()

        def across(k):
            slot = lax.rem(s + n - 2 * k, n)
            return pltpu.make_async_remote_copy(
                src_ref=x_ref if k == 0 else o_ref.at[slot], dst_ref=o_ref.at[slot],
                send_sem=side_out.at[k], recv_sem=side_in.at[k], device_id=(r, beside), device_id_type=MESH,
            )

        near = [across(k) for k in range(n // 2)]
        near[0].start()
        local = pltpu.make_async_copy(x_ref, o_ref.at[s], own)
        local.start()
        if ride.count:
            ride.start(sent, got, sems, greet=False)
        for k, copy in enumerate(far):
            job.run(ins, outs, scratch) if k == 0 else None
            copy.wait_recv()
            near[k + 1].start()
        for copy in near:
            copy.wait()
        for copy in far:
            copy.wait_send()
        local.wait()
        if ride.count:
            ride.wait(sent, got, sems)

    length, features = values.shape
    whole, *got = pl.pallas_call(
        kern,
        out_shape=(jax.ShapeDtypeStruct((n, length, features), values.dtype),) + ride.shapes + job.outs,
        in_specs=[ANY] * (1 + ride.count + len(job.inputs)),
        out_specs=(ANY,) * (1 + ride.count) + (VM,) * len(job.outs),
        scratch_shapes=[pltpu.SemaphoreType.DMA] + [pltpu.SemaphoreType.DMA((n // 2,))] * 4
        + sems_used + job.scratch,
        compiler_params=pltpu.CompilerParams(
            collective_id=collective_id, has_side_effects=True, vmem_limit_bytes=56 * 2**20
        ),
        cost_estimate=cost(20.0),
        name="gather_seq",
    )(values, *[x for kind, x in plans], *job.inputs)
    whole = whole.reshape(n * length, features)
    return (whole, *got) if got else whole


def project_blocks(blocks, weight):
    length, width = blocks[0].shape[0], weight.shape[1]
    count = len(blocks)

    def kern(*refs):
        weight_ref, o_ref = refs[count], refs[count + 1]
        for k in range(count):
            o_ref[k * length : (k + 1) * length, :] = nn(refs[k][...], weight_ref[...]).astype(BF)

    return pl.pallas_call(
        kern,
        out_shape=jax.ShapeDtypeStruct((count * length, width), BF),
        in_specs=[VM] * (count + 1),
        out_specs=VM,
        compiler_params=pltpu.CompilerParams(vmem_limit_bytes=40 * 2**20),
        cost_estimate=cost(8.0),
        name="project_blocks",
    )(*blocks, weight)


def self_bwd(qkv,do,of,lse,fwd,qa,ka,plans,n,rows):
    Lq,W=qkv.shape[0],qkv.shape[1]//3; H=W//HD; nb=Lq//128
    ride=Exchange(plans,n,rows)
    def kern(qkv_ref,do_ref,of_ref,lse_ref,fwd_ref,qa_ref,ka_ref,*rest):
        sent,rest=rest[:ride.count],rest[ride.count:]
        grad_ref,gb_ref=rest[:2]
        got,rest=rest[2:2+ride.count],rest[2+ride.count:]
        (qaug,kaug,kdiag,vaug,doaug,dkacc,dvacc,dqs,dks,dvs,tz,ga),sems=rest[:12],rest[12:]
        h=pl.program_id(0)
        @pl.when(h==0)
        def _():
            ride.start(sent,got,sems)
        for hh in range(H):
            @pl.when(h==hh)
            def _():
                sl=slice(hh*HD,(hh+1)*HD)
                lane=lax.broadcasted_iota(jnp.int32,(Lq,HD),1)
                kaug[:,0:HD]=qkv_ref[:,W+hh*HD:W+(hh+1)*HD]
                ones=(lane>=3)&(lane<6)
                kaug[:,HD:]=jnp.where(ones,BF(1),ka_ref[...])
                kdiag[:,0:HD]=qkv_ref[:,W+hh*HD:W+(hh+1)*HD]
                kdiag[:,HD:]=jnp.where(ones,BF(1),BF(0)).astype(BF)
                vaug[:,0:HD]=qkv_ref[:,2*W+hh*HD:2*W+(hh+1)*HD]
                vaug[:,HD:]=jnp.where(lane<3,BF(1),BF(0)).astype(BF)
                a,b,c=split3(-lse_ref[:,hh:hh+1])
                qaug[:,0:HD]=qkv_ref[:,sl]*BF(0.125)
                qaug[:,HD:]=jnp.where(lane==3,a,jnp.where(lane==4,b,jnp.where(lane==5,c,qa_ref[...])))
                dd=do_ref[:,sl]
                delta=jnp.sum(dd.astype(F32)*of_ref[:,sl],axis=1,keepdims=True)
                a,b,c=split3(-delta)
                doaug[:,0:HD]=dd
                doaug[:,HD:]=jnp.where(lane==0,a,jnp.where(lane==1,b,jnp.where(lane==2,c,BF(0))))
        dkacc[...]=jnp.zeros_like(dkacc)
        dvacc[...]=jnp.zeros_like(dvacc)
        ga[...]=jnp.zeros_like(ga)
        for d in range(nb):
            tz[d]=toeplitz(fwd_ref[pl.ds(h,1),d*128:(d+2)*128],128)
        eye=eye128()
        for q0 in range(0,Lq,256):
            qn=min(256,Lq-q0); kend=q0+qn
            qg=qaug[q0:kend,:]; dg=doaug[q0:kend,:]
            s=nt(kaug[0:kend,:],qg)
            g=nt(vaug[0:kend,:],dg)
            pcols=[]; dcols=[]
            for a in range(qn//128):
                qt=q0//128+a
                rows=slice(q0+a*128,q0+(a+1)*128)
                sd=nt(kdiag[rows,:],qaug[rows,:])
                pt=[]; dt=[]
                for b in range(kend//128):
                    d=qt-b
                    if d<0:
                        pt.append(jnp.zeros((128,128),BF)); dt.append(jnp.zeros((128,128),BF)); continue
                    t=s[b*128:(b+1)*128,a*128:(a+1)*128]
                    if d==0: t=jnp.where(eye,sd,t)
                    p=jnp.exp(t+tz[d])
                    ds=(p*g[b*128:(b+1)*128,a*128:(a+1)*128]).astype(BF)
                    ga[d]+=ds.astype(F32)
                    pt.append(p.astype(BF)); dt.append(ds)
                pcols.append(jnp.concatenate(pt,axis=0)); dcols.append(jnp.concatenate(dt,axis=0))
            P=jnp.concatenate(pcols,axis=1); DS=jnp.concatenate(dcols,axis=1)
            dvacc[0:kend,:]+=nn(P,dg[:,0:HD])
            dkacc[0:kend,:]+=nn(DS,qg[:,0:HD])
            dqs[h,q0:kend,:]=(tn(DS,kaug[0:kend,0:HD])*0.125).astype(BF)
        dks[h]=dkacc[...].astype(BF)
        dvs[h]=dvacc[...].astype(BF)
        flip=(lax.broadcasted_iota(jnp.int32,(128,128),0)+lax.broadcasted_iota(jnp.int32,(128,128),1)==127).astype(F32)
        for d in range(nb):
            y=lax.dot_general(flip,ga[d],(((1,),(0,)),((),())),preferred_element_type=F32,precision=lax.Precision.HIGHEST)
            x=pltpu.roll(jnp.concatenate([y,jnp.zeros((128,128),F32)],axis=1),1,1,stride=1,stride_axis=0)
            gb_ref[pl.ds(h,1),d*256:(d+1)*256]=jnp.sum(x,axis=0,keepdims=True)
        @pl.when(h==H-1)
        def _():
            grad_ref[...]=jnp.concatenate([x[t] for x in (dqs,dks,dvs) for t in range(H)],axis=1)
            ride.wait(sent,got,sems)
    full=lambda s: pl.BlockSpec(s,lambda h:(0,)*len(s))
    return pl.pallas_call(kern,grid=(H,),
        out_shape=(jax.ShapeDtypeStruct((Lq,3*W),BF),jax.ShapeDtypeStruct((H,nb*256),F32))+ride.shapes,
        in_specs=[full((Lq,3*W))]+[full((Lq,W))]*2+[full((Lq,128)),full(fwd.shape),full((Lq,HD)),full((Lq,HD))]+[ANY]*ride.count,
        out_specs=(full((Lq,3*W)),full((H,nb*256)))+(ANY,)*ride.count,
        scratch_shapes=[pltpu.VMEM((Lq,2*HD),BF)]*5+[pltpu.VMEM((Lq,HD),F32)]*2+[pltpu.VMEM((H,Lq,HD),BF)]*3+[pltpu.VMEM((nb,128,128),F32)]*2+ride.scratch,
        compiler_params=pltpu.CompilerParams(vmem_limit_bytes=48*2**20,collective_id=2,has_side_effects=True),cost_estimate=cost(35.0),name="self_bwd")(
            qkv,do,of,lse,fwd,qa,ka,*[x for kind,x in plans])

def fold_bias(gb,Lq):
    H=gb.shape[0]; nb=Lq//128
    x=gb.reshape(H,nb,2,128)
    low=x[:,:,0].reshape(H,Lq); high=x[:,:,1].reshape(H,Lq)
    return high+jnp.concatenate([low[:,128:],jnp.zeros((H,128),gb.dtype)],axis=1)


MESH = pl.DeviceIdType.MESH


def sum_parts(first, cross, self_out, cross_out, n, wd):
    devices, count, wide = first.shape
    total = self_out.shape[0]

    def kern(first_ref, cross_ref, self_out_ref, cross_out_ref, sum_ref, col_ref, mean_ref):
        lane = lax.broadcasted_iota(jnp.int32, (count, 128), 1)
        means = jnp.zeros((count, 128), F32)
        sums = [None] * 8
        for ref, matrices in ((first_ref, (0, 1, 2)), (cross_ref, (4, 5, 6))):
            parts = []
            for s in range(n):
                part = ref[s].astype(F32)
                for r in range(1, devices // n):
                    part = part + ref[r * n + s].astype(F32)
                parts.append(part)
            for k, j in enumerate(matrices):
                if j > 4:
                    low = range(wd + (k - 1) * HD, 3 * wd, 2 * HD)
                    pieces = [part[:, c : c + HD] for part in parts for c in low]
                else:
                    pieces = [part[:, k * wd : (k + 1) * wd] for part in parts]
                sums[j] = jnp.concatenate(pieces, 1)[:, :D]
        for j, ref in ((3, self_out_ref), (7, cross_out_ref)):
            sums[j] = ref[0].astype(F32)
            for r in range(1, total):
                sums[j] = sums[j] + ref[r].astype(F32)
        for j in range(8):
            square = sums[j] * sums[j]
            sum_ref[j] = sums[j]
            col_ref[j : j + 1, :] = jnp.sum(square, 0, keepdims=True)
            means = jnp.where(lane == j, jnp.mean(square, 1, keepdims=True), means)
        mean_ref[...] = means

    return pl.pallas_call(
        kern,
        out_shape=(
            jax.ShapeDtypeStruct((8, count, D), F32),
            jax.ShapeDtypeStruct((8, D), F32),
            jax.ShapeDtypeStruct((count, 128), F32),
        ),
        in_specs=[VM] * 4,
        out_specs=(VM,) * 3,
        compiler_params=pltpu.CompilerParams(vmem_limit_bytes=32 * 2**20),
        cost_estimate=cost(4.0),name="sum_parts",
    )(first, cross, self_out, cross_out)


def sum_everywhere(values, n, rows):
    count = n * rows

    def kern(x_ref, o_ref, got, mine, out_sem, in_sem, out_sem2, in_sem2):
        me = lax.axis_index("rows") * n + lax.axis_index("seq")

        def place(step):
            j = lax.rem(me + step, count)
            return j, (lax.div(j, n), lax.rem(j, n))

        greet_all(count, n)

        def piece(step):
            j, device = place(step)
            return pltpu.make_async_remote_copy(
                src_ref=x_ref.at[j], dst_ref=got.at[step], send_sem=out_sem.at[step], recv_sem=in_sem.at[step],
                device_id=device, device_id_type=MESH,
            )

        def total(step):
            return pltpu.make_async_remote_copy(
                src_ref=mine, dst_ref=o_ref.at[me], send_sem=out_sem2.at[step], recv_sem=in_sem2.at[step],
                device_id=place(step)[1], device_id_type=MESH,
            )

        def start_piece(step, carry):
            piece(step).start()
            return carry

        def add_piece(step, carry):
            piece(step).wait()
            return carry + got[step]

        def start_total(step, carry):
            total(step).start()
            return carry

        def wait_total(step, carry):
            total(step).wait()
            return carry

        lax.fori_loop(1, count, start_piece, 0)
        mine[...] = lax.fori_loop(1, count, add_piece, x_ref[me])
        lax.fori_loop(1, count, start_total, 0)
        o_ref[me] = mine[...]
        lax.fori_loop(1, count, wait_total, 0)

    return pl.pallas_call(
        kern,
        out_shape=jax.ShapeDtypeStruct(values.shape, F32),
        in_specs=[VM],
        out_specs=VM,
        scratch_shapes=[pltpu.VMEM(values.shape, F32), pltpu.VMEM(values.shape[1:], F32)]
        + [pltpu.SemaphoreType.DMA((count,))] * 4,
        compiler_params=pltpu.CompilerParams(collective_id=1, has_side_effects=True),
        cost_estimate=cost(16.0),name="sum_everywhere",
    )(values)


def normalize(values, scaling):
    return values * lax.rsqrt(jnp.mean(values * values, -1, keepdims=True) + NORM_EPS) * scaling


def gated(gate_values, up_values):
    return jax.nn.gelu(gate_values, approximate=True) * up_values


def factored_start(gradient, rowwise):
    square = gradient * gradient
    rowwise_new = BETA_TWO * rowwise + (1.0 - BETA_TWO) * jnp.mean(square, 2).T
    return (rowwise_new, jnp.sum(square, 0), jnp.sum(rowwise_new, 1))


def factored_finish(gradient, moment, rowwise_new, colwise, weight, column_sum, row_sum, total_rows):
    colwise_new = BETA_TWO * colwise + (1.0 - BETA_TWO) * (column_sum / total_rows)
    moment_new = BETA_ONE * moment + (1.0 - BETA_ONE) * gradient
    second = rowwise_new.T[:, :, None] * colwise_new[None] / (row_sum / total_rows)[None, :, None]
    stepped = (
        moment_new / (1.0 - BETA_ONE**STEP) / (jnp.sqrt(second / (1.0 - BETA_TWO**STEP)) + ADAM_EPS)
    )
    updated = weight - MATRIX_RATE * (stepped + WEIGHT_DECAY * weight)
    return (moment_new, colwise_new, updated)


def adaptive(gradient, moment, second, weight):
    moment_new = BETA_ONE * moment + (1.0 - BETA_ONE) * gradient
    second_new = BETA_TWO * second + (1.0 - BETA_TWO) * gradient * gradient
    stepped = (
        moment_new
        / (1.0 - BETA_ONE**STEP)
        / (jnp.sqrt(second_new / (1.0 - BETA_TWO**STEP)) + ADAM_EPS)
    )
    return (moment_new, second_new, weight - VECTOR_RATE * stepped)


def make_shards(n, rows):
    devices = n * rows
    both = ("rows", "seq")
    hpd = -(-HEADS // n)
    wd = hpd * HD
    wide = n * wd

    def widen(values):
        extra = wide - values.shape[-1]
        return values if extra == 0 else jnp.pad(values, [(0, 0)] * (values.ndim - 1) + [(0, extra)])

    def blocks_along_seq(values, gate):
        blocks = []
        for step in range(0, n, 2):
            block = values
            if step:
                block = lax.ppermute(values, "seq", [(i, i ^ step) for i in range(n)])
                block = lax.optimization_barrier((block, gate))[0]
            blocks += [block, lax.ppermute(block, "seq", [(i, i ^ 1) for i in range(n)])]
        return blocks

    def by_heads(weight):
        count, j = weight.shape[:2]
        return jnp.moveaxis(widen(weight).reshape(count, j, n * hpd, HD), 2, 1).reshape(count, wide * j)

    def to_seq(values, collective_id):
        (parts,) = exchange([("seq", values.reshape(n, -1, values.shape[1]))], n, rows, collective_id)
        return side_by_side(parts)[:, :D]

    def side_by_side(parts):
        return jnp.moveaxis(parts, 0, 1).reshape(parts.shape[1], -1)

    def shards(
        decoder_input,
        encoder_output,
        cotangent,
        decoder_segment,
        decoder_padding,
        encoder_segment,
        encoder_padding,
        distance_bucket,
        attention_weight,
        attention_moment,
        attention_rowwise,
        attention_colwise,
        expand_weight,
        expand_moment,
        expand_rowwise,
        expand_colwise,
        contract_weight,
        contract_moment,
        contract_rowwise,
        contract_colwise,
        norm_gain,
        gain_moment,
        gain_second,
        relative_table,
        table_moment,
        table_second,
    ):
        shard = lax.axis_index("seq")
        length = decoder_segment.shape[1]
        attention_low = attention_weight.astype(BF)
        count = expand_weight.shape[0]
        first_parts = jnp.moveaxis(widen(attention_low[:, 0:3]).reshape(count, 3, n, wd), 2, 0)
        row_input, first_columns = gather_seq(
            decoder_input[0], n, rows, 3, [("own", first_parts.reshape(n, count, 3 * wd))]
        )
        first_columns = first_columns.reshape(D, 3 * wd)
        attention_full = lax.all_gather(
            jnp.concatenate(
                (
                    attention_low[:, 3],
                    attention_low[:, 7],
                    by_heads(attention_low[:, 4:5]),
                    by_heads(attention_low[:, 5:7]),
                ),
                1,
            ),
            both, axis=0, tiled=True,
        )
        deep = -(-contract_weight.shape[0] // count)
        spare = deep * count - contract_weight.shape[0]
        contract_low = jnp.pad(contract_weight.astype(BF), ((0, spare), (0, 0)))
        feed_full = lax.all_gather(
            jnp.concatenate(
                (
                    expand_weight.astype(BF).reshape(count, 2 * FF),
                    jnp.moveaxis(contract_low.reshape(deep, count, D), 0, 1).reshape(count, deep * D),
                ),
                1,
            ),
            both, axis=0, tiled=True,
        )
        expand_full = feed_full[:, 0 : 2 * FF]
        contract_full = jnp.concatenate(
            [
                feed_full[:, 2 * FF + g * D : 2 * FF + (g + 1) * D].reshape(devices, count, D)[
                    :, : contract_weight.shape[0] - g * count
                ]
                for g in range(deep)
            ],
            1,
        ).reshape(FF, D)
        edges = (0, D, 2 * D, 2 * D + wide, 2 * D + 3 * wide)
        self_out_weight, cross_out_weight, cross_query_weight, cross_pair_weight = (
            attention_full[:, low:high] for low, high in zip(edges[:-1], edges[1:])
        )
        cross_query_columns = lax.dynamic_slice_in_dim(cross_query_weight, shard * wd, wd, 1)
        cross_columns = lax.dynamic_slice_in_dim(cross_pair_weight, shard * 2 * wd, 2 * wd, 1)

        def own_rows(matrix):
            padded = jnp.pad(matrix, ((0, wide - D), (0, 0))) if wide > D else matrix
            return lax.dynamic_slice_in_dim(padded, shard * wd, wd, 0)

        document = jnp.arange(HD, dtype=jnp.int32)[None, :]
        decoder_document = decoder_segment[0][:, None] == document
        query_side = decoder_document.astype(BF)
        self_side = jnp.where(
            (document < 3) & ~(decoder_document & (decoder_padding[0][:, None] == 1)), NEG, 0.0
        ).astype(BF)
        real_document = jnp.where(encoder_padding[0] == 1, encoder_segment[0], -1).reshape(n, -1)
        real_document = jnp.concatenate(
            [lax.dynamic_slice_in_dim(real_document, shard ^ p, 1, 0)[0] for p in range(n)]
        )
        cross_side = jnp.where(
            (document < 3) & (real_document[:, None] != document), NEG, 0.0
        ).astype(BF)
        onehot = (
            distance_bucket[:, None] == jnp.arange(BUCKETS, dtype=jnp.int32)[None, :]
        ).astype(F32)
        table_own = lax.dynamic_slice_in_dim(
            jnp.pad(relative_table, ((0, 0), (0, n * hpd - HEADS))), shard * hpd, hpd, 1
        )
        bias = jnp.einsum("db,bh->hd", onehot, table_own, precision=HIGHEST)
        beyond = jnp.full((hpd, 128), NEG, F32)
        bias_forward = jnp.concatenate((beyond, bias), 1)
        bias_backward = jnp.concatenate((bias[:, ::-1], beyond), 1)

        def dot(left, right):
            return jnp.dot(left, right, preferred_element_type=F32)

        def dot_back(left, right):
            return lax.dot_general(left, right, (((1,), (1,)), ((), ())), preferred_element_type=F32)

        def outer(left, right):
            return lax.dot_general(left, right, (((0,), (0,)), ((), ())), preferred_element_type=F32)

        row_norm = normalize(row_input.astype(F32), norm_gain[0]).astype(BF)
        self_proj = dot(row_norm, first_columns).astype(BF)
        self_heads, self_exact, self_lse = self_fwd(
            self_proj, bias_backward, query_side, self_side
        )
        inputs = decoder_input[0].astype(F32)
        self_out = to_seq(self_heads, 8)
        after_self = inputs + dot(self_out, self_out_weight)
        encoder_blocks = blocks_along_seq(
            lax.optimization_barrier((encoder_output[0], row_input))[0], after_self
        )
        cross_norm = normalize(after_self, norm_gain[1]).astype(BF)
        row_cross_norm = gather_seq(cross_norm, n, rows, 4)
        cross_query = dot(row_cross_norm, cross_query_columns).astype(BF)
        cross_pair = project_blocks(encoder_blocks, cross_columns)
        cross_heads, cross_exact, cross_lse = cross_fwd(
            cross_query, cross_pair, query_side, cross_side
        )
        cross_out = to_seq(cross_heads, 9)
        after_cross = after_self + dot(cross_out, cross_out_weight)
        feed_norm = normalize(after_cross, norm_gain[2]).astype(BF)
        hidden_pair = dot(feed_norm, expand_full)
        gate_values, up_values = hidden_pair[:, 0:FF], hidden_pair[:, FF:]
        feed_branch = cotangent[0]
        grad_result = feed_branch.astype(F32)
        grad_hidden = dot_back(feed_branch, contract_full)
        hidden_wide, gated_back = jax.vjp(gated, gate_values, up_values)
        hidden = hidden_wide.astype(BF)
        layer_output = (after_cross + dot(hidden, contract_full)).astype(BF)
        grad_gate, grad_up = gated_back(grad_hidden)
        grad_pair = jnp.concatenate((grad_gate.astype(BF), grad_up.astype(BF)), 1)
        unused_norm, norm_back = jax.vjp(normalize, after_cross, norm_gain[2])
        feed_part, feed_gain = norm_back(dot_back(grad_pair, expand_full))
        grad_after_cross = grad_result + feed_part
        cross_branch = grad_after_cross.astype(BF)
        down_rows = deep * count - spare

        def feed_gradients(ins, outs):
            norm_ref, pair_ref, hidden_ref, branch_ref = ins
            (o_ref,) = outs
            for c in range(0, 2 * FF, 512):
                part = tn(norm_ref[...], pair_ref[:, c : c + 512])
                o_ref[:, :, c : c + 512] = part.reshape(devices, count, 512).astype(BF)
            group = devices * 1024 // FF
            for c in range(0, FF, 1024):
                part = tn(hidden_ref[:, c : c + 1024], branch_ref[...]).reshape(group, down_rows, D)
                first = c // 1024 * group
                for g in range(deep):
                    piece = part[:, g * count : (g + 1) * count]
                    if piece.shape[1] < count:
                        low = jnp.zeros((group, count - piece.shape[1], D), F32)
                        piece = jnp.concatenate((piece, low), 1)
                    o_ref[first : first + group, :, 2 * FF + g * D : 2 * FF + (g + 1) * D] = piece.astype(BF)

        if count % 8 == 0:
            row_cross_branch, feed_local = gather_seq(
                cross_branch, n, rows, 5,
                job=Job(
                    (feed_norm, grad_pair, hidden, feed_branch),
                    (jax.ShapeDtypeStruct((devices, count, 2 * FF + deep * D), BF),),
                    feed_gradients,
                ),
            )
            feed_local = feed_local.reshape(D, -1)
        else:
            row_cross_branch = gather_seq(cross_branch, n, rows, 5)
            contract_local = outer(hidden, feed_branch).astype(BF).reshape(devices, -1, D)
            contract_local = jnp.pad(contract_local, ((0, 0), (0, spare), (0, 0)))
            feed_local = jnp.concatenate(
                [outer(feed_norm, grad_pair).astype(BF)]
                + [contract_local[:, g * count : (g + 1) * count].reshape(D, D) for g in range(deep)],
                1,
            )
        feed_sum = lax.psum_scatter(feed_local, both, scatter_dimension=0, tiled=True).astype(F32)
        cross_grad = dot_back(row_cross_branch, own_rows(cross_out_weight)).astype(BF)
        expand_sum = feed_sum[:, 0 : 2 * FF].reshape(count, 2, FF)
        contract_sum = jnp.concatenate(
            [feed_sum[:, 2 * FF + g * D : 2 * FF + (g + 1) * D] for g in range(deep)], 0
        )[: deep * count - spare]
        cross_qparts, cross_home, cross_qgrad, cross_last, *cross_grads = cross_bwd(
            cross_query, cross_pair, cross_grad, cross_exact, cross_lse, query_side, cross_side, n
        )
        grad_cross_query = side_by_side(cross_qparts)[:, :D]
        unused_norm, norm_back = jax.vjp(normalize, after_self, norm_gain[1])
        cross_part, cross_gain = norm_back(dot_back(grad_cross_query, cross_query_weight[:, :D]))
        grad_after_self = grad_after_cross + cross_part
        self_branch = grad_after_self.astype(BF)
        def cross_gradients(ins, outs):
            norm_ref, query_ref, heads_ref, branch_ref = ins[:4]
            o_ref, out_ref = outs
            o_ref[:, 0:wd] = tn(norm_ref[...], query_ref[...]).astype(BF)
            pair = tn(ins[4][...], ins[4 + n][...])
            for p in range(1, n):
                pair = pair + tn(ins[4 + p][...], ins[4 + n + p][...])
            o_ref[:, wd : 3 * wd] = pair.astype(BF)
            out_ref[...] = tn(heads_ref[...], branch_ref[...]).astype(BF)

        row_self_branch, cross_local, cross_out_local = gather_seq(
            self_branch, n, rows, 6,
            job=Job(
                (row_cross_norm, cross_qgrad.reshape(-1, wd), cross_heads, row_cross_branch)
                + tuple(encoder_blocks) + tuple(cross_grads),
                (jax.ShapeDtypeStruct((D, 3 * wd), BF), jax.ShapeDtypeStruct((wd, D), BF)),
                cross_gradients,
            ),
        )
        self_grad = dot_back(row_self_branch, own_rows(self_out_weight)).astype(BF)
        self_out_local = outer(self_heads, row_self_branch).astype(BF)
        matched = wide == D and wd == rows * count
        plans = [
            ("all", cross_local.reshape(devices, count, 3 * wd)),
            ("xor", cross_last),
        ]
        rows_local = (self_out_local, cross_out_local)
        if matched:
            plans += [("rows", x.reshape(rows, count, D)) for x in rows_local]
        self_grads, pair_bias, cross_parts, cross_last_home, *rows_parts = self_bwd(
            self_proj, self_grad, self_exact, self_lse, bias_forward, query_side, self_side, plans, n, rows
        )
        if not matched:
            padded = lax.dynamic_update_slice_in_dim(
                jnp.zeros((wide, 2 * D), BF), jnp.concatenate(rows_local, 1), shard * wd, 0
            )[:D]
            whole = lax.psum_scatter(padded, both, scatter_dimension=0, tiled=True)[None]
            rows_parts = [whole[:, :, :D], whole[:, :, D:]]
        grad_bias = fold_bias(pair_bias, length)
        table_own_grad = jnp.einsum("hd,db->bh", grad_bias, onehot, precision=HIGHEST)
        table_local = lax.dynamic_update_slice_in_dim(
            jnp.zeros((BUCKETS, n * hpd), F32), table_own_grad, shard * hpd, 1
        )[:, :HEADS]
        self_back = dot_back(self_grads, first_columns).astype(BF)
        def encoder_job(ins, outs):
            home_ref, last_ref, weight_ref = ins
            total = None
            for t in range(n):
                for h in range(hpd):
                    grads = last_ref[t] if h == hpd - 1 else home_ref[t, h]
                    low = (t * hpd + h) * 2 * HD
                    part = nt(grads, weight_ref[:, low : low + 2 * HD])
                    total = part if total is None else total + part
            outs[0][...] = total

        self_back_parts, self_parts, encoder_gradient = exchange(
            [
                ("seq", self_back.reshape(n, -1, D)),
                ("all", outer(row_norm, self_grads).astype(BF).reshape(devices, count, 3 * wd)),
            ],
            n, rows, 7,
            job=Job(
                (cross_home, cross_last_home, cross_pair_weight),
                (jax.ShapeDtypeStruct(encoder_output.shape[1:], F32),),
                encoder_job,
            ),
        )
        unused_norm, norm_back = jax.vjp(normalize, inputs, norm_gain[0])
        self_part, self_gain = norm_back(jnp.sum(self_back_parts.astype(F32), 0))
        input_gradient = grad_after_self + self_part

        attention_parts, attention_columns, attention_means = sum_parts(
            self_parts, cross_parts, *rows_parts, n, wd
        )
        attention_sum = jnp.moveaxis(attention_parts, 0, 1)
        attention_rows = BETA_TWO * attention_rowwise + (1.0 - BETA_TWO) * attention_means[:, 0:8].T
        attention_rowsum = jnp.sum(attention_rows, 1)
        expand_rows, expand_columns, expand_rowsum = factored_start(expand_sum, expand_rowwise)
        contract_rows, contract_columns, contract_rowsum = factored_start(
            contract_sum[:, None, :], contract_rowwise[None, :]
        )
        gain_local = jnp.stack((self_gain, cross_gain, feed_gain), 0)
        pieces = (
            attention_columns,
            expand_columns,
            contract_columns,
            attention_rowsum,
            expand_rowsum,
            contract_rowsum,
            gain_local,
            table_local,
        )
        flat = jnp.concatenate([piece.reshape(-1) for piece in pieces])
        size = devices * 8 * 128 * -(-flat.shape[0] // (devices * 8 * 128))
        flat = jnp.pad(flat, (0, size - flat.shape[0])).reshape(devices, -1, 128)
        flat = sum_everywhere(flat, n, rows).reshape(-1)
        sums, start = [], 0
        for piece in pieces:
            sums.append(flat[start : start + piece.size].reshape(piece.shape))
            start += piece.size
        (
            attention_total,
            expand_total,
            contract_total,
            attention_rowtotal,
            expand_rowtotal,
            contract_rowtotal,
            gain_gradient,
            table_gradient,
        ) = sums
        attention_new = factored_finish(
            attention_sum,
            attention_moment,
            attention_rows,
            attention_colwise,
            attention_weight,
            attention_total,
            attention_rowtotal,
            D,
        )
        expand_new = factored_finish(
            expand_sum,
            expand_moment,
            expand_rows,
            expand_colwise,
            expand_weight,
            expand_total,
            expand_rowtotal,
            D,
        )
        contract_new = factored_finish(
            contract_sum[:, None, :],
            contract_moment[:, None, :],
            contract_rows,
            contract_colwise[None, :],
            contract_weight[:, None, :],
            contract_total,
            contract_rowtotal,
            FF,
        )
        gain_new = adaptive(gain_gradient, gain_moment, gain_second, norm_gain)
        table_new = adaptive(table_gradient, table_moment, table_second, relative_table)
        return (
            layer_output[None],
            input_gradient[None],
            encoder_gradient[None],
            attention_sum,
            attention_new[0],
            attention_rows,
            attention_new[1],
            attention_new[2],
            expand_sum,
            expand_new[0],
            expand_rows,
            expand_new[1],
            expand_new[2],
            contract_sum,
            contract_new[0][:, 0],
            contract_rows[0],
            contract_new[1][0],
            contract_new[2][:, 0],
            gain_gradient,
            gain_new[0],
            gain_new[1],
            gain_new[2],
            table_gradient,
            table_new[0],
            table_new[1],
            table_new[2],
        )

    return shards


def solution(mesh):
    placed = (
        P("rows", "seq", None),
        P("rows", "seq", None),
        P("rows", "seq", None),
        P("rows", None),
        P("rows", None),
        P("rows", None),
        P("rows", None),
        P(),
        P(("rows", "seq"), None, None),
        P(("rows", "seq"), None, None),
        P(None, ("rows", "seq")),
        P(),
        P(("rows", "seq"), None, None),
        P(("rows", "seq"), None, None),
        P(None, ("rows", "seq")),
        P(),
        P(("rows", "seq"), None),
        P(("rows", "seq"), None),
        P(("rows", "seq")),
        P(),
        P(),
        P(),
        P(),
        P(),
        P(),
        P(),
    )
    return jax.shard_map(
        make_shards(mesh.shape["seq"], mesh.shape["rows"]),
        mesh=mesh,
        in_specs=placed,
        out_specs=(
            P("rows", "seq", None),
            P("rows", "seq", None),
            P("rows", "seq", None),
            P(("rows", "seq"), None, None),
            P(("rows", "seq"), None, None),
            P(None, ("rows", "seq")),
            P(),
            P(("rows", "seq"), None, None),
            P(("rows", "seq"), None, None),
            P(("rows", "seq"), None, None),
            P(None, ("rows", "seq")),
            P(),
            P(("rows", "seq"), None, None),
            P(("rows", "seq"), None),
            P(("rows", "seq"), None),
            P(("rows", "seq")),
            P(),
            P(("rows", "seq"), None),
            P(),
            P(),
            P(),
            P(),
            P(),
            P(),
            P(),
            P(),
        ),
        check_vma=False,
    )
```

```python
import jax
import jax.numpy as jnp
from jax import lax
from jax.experimental import pallas as pl
from jax.experimental.pallas import tpu as pltpu
from jax.sharding import PartitionSpec as P

D = 768
FF = 2048
HEADS = 12
BUCKETS = 32
STEP = 10
HIGHEST = lax.Precision.HIGHEST
NORM_EPS = 1e-06
BETA_ONE = 0.9
BETA_TWO = 0.999
ADAM_EPS = 1e-08
WEIGHT_DECAY = 0.01
MATRIX_RATE = 0.15
VECTOR_RATE = 1.0
HD = 64
NEG = -1e30
F32 = jnp.float32
BF = jnp.bfloat16

def nt(a,b): return lax.dot_general(a,b,(((1,),(1,)),((),())),preferred_element_type=F32)
def nn(a,b): return lax.dot_general(a,b,(((1,),(0,)),((),())),preferred_element_type=F32)
def tn(a,b): return lax.dot_general(a,b,(((0,),(0,)),((),())),preferred_element_type=F32)

def cross_fwd(q,kv,qa,ka,qb=352,kc=1024):
    Lq,W=q.shape; Lk=kv.shape[0]; H=W//HD
    nk=Lk//kc
    def kern(q_ref,kv_ref,qa_ref,ka_ref,o_ref,of_ref,lse_ref,kaug,vs,s_s,m_s,l_s,acc):
        @pl.when(pl.program_id(0)==0)
        def _():
            for h in range(H):
                kaug[h,:,0:HD]=kv_ref[:,2*h*HD:(2*h+1)*HD]
                kaug[h,:,HD:2*HD]=ka_ref[...]
                vs[h]=kv_ref[:,(2*h+1)*HD:(2*h+2)*HD]
        lane=lax.broadcasted_iota(jnp.int32,(qb,128),1)
        lses=jnp.zeros((qb,128),F32)
        outs=[]
        for h in range(H):
            qh=(q_ref[:,h*HD:(h+1)*HD]*BF(0.125)).astype(BF)
            qg=jnp.concatenate([qh,qa_ref[...]],axis=1)
            m_s[...]=jnp.full((qb,128),-3e38,F32)
            for c in range(nk):
                s=nt(qg,kaug[h,c*kc:(c+1)*kc,:])
                s_s[:,c*kc:(c+1)*kc]=s
                mm=m_s[...]
                for t in range(kc//128): mm=jnp.maximum(mm,s[:,t*128:(t+1)*128])
                m_s[...]=mm
            m=jnp.max(m_s[...],axis=1,keepdims=True)
            l_s[...]=jnp.zeros((qb,128),F32)
            acc[...]=jnp.zeros((qb,HD),F32)
            for c in range(nk):
                p=jnp.exp(s_s[:,c*kc:(c+1)*kc]-m)
                ll=l_s[...]
                for t in range(kc//128): ll=ll+p[:,t*128:(t+1)*128]
                l_s[...]=ll
                acc[...]+=nn(p.astype(BF),vs[h,c*kc:(c+1)*kc,:])
            l=jnp.sum(l_s[...],axis=1,keepdims=True)
            o=acc[...]/l
            outs.append(o)
            lses=jnp.where(lane==h,m+jnp.log(l),lses)
        oo=jnp.concatenate(outs,axis=1)
        o_ref[...]=oo.astype(BF)
        of_ref[...]=oo
        lse_ref[...]=lses
    full=lambda s: pl.BlockSpec(s,lambda i:(0,)*len(s))
    row=lambda w: pl.BlockSpec((qb,w),lambda i:(i,0))
    return pl.pallas_call(kern,grid=(Lq//qb,),
        out_shape=(jax.ShapeDtypeStruct((Lq,W),BF),jax.ShapeDtypeStruct((Lq,W),F32),jax.ShapeDtypeStruct((Lq,128),F32)),
        in_specs=[row(W),full((Lk,2*W)),row(HD),full((Lk,HD))],
        out_specs=(row(W),row(W),row(128)),
        scratch_shapes=[pltpu.VMEM((H,Lk,2*HD),BF),pltpu.VMEM((H,Lk,HD),BF),pltpu.VMEM((qb,Lk),F32),pltpu.VMEM((qb,128),F32),pltpu.VMEM((qb,128),F32),pltpu.VMEM((qb,HD),F32)],
        compiler_params=pltpu.CompilerParams(vmem_limit_bytes=56*2**20),cost_estimate=cost(31.0),name="cross_fwd")(q,kv,qa,ka)

def split3(x):
    a=x.astype(BF); r=x-a.astype(F32)
    b=r.astype(BF); c=(r-b.astype(F32)).astype(BF)
    return a,b,c

def cross_bwd(q,kv,do,of,lse,qa,ka,plans,n,rows,qb=256):
    Lq,W=q.shape; Lk=kv.shape[0]; H=W//HD; kc=Lk//n
    ride=Exchange(plans,n,rows); riders=ride.scratch if plans else []
    def kern(q_ref,kv_ref,do_ref,of_ref,lse_ref,qa_ref,ka_ref,*rest):
        sent,rest=rest[:ride.count],rest[ride.count:]
        dq_ref,home_ref,dqw=rest[:3]
        got,rest=rest[3:3+ride.count],rest[3+ride.count:]
        rest,sems=rest[:len(rest)-len(riders)],rest[len(rest)-len(riders):]
        dkv_refs=rest[:n]
        kaug,vaug,qaug,doaug,ps,dss,dqacc,kt,dqs,dkvs,q_out,q_in,kv_out,kv_in,own=rest[n:]
        h=pl.program_id(0); c=pl.program_id(1)
        r,s=lax.axis_index("rows"),lax.axis_index("seq")
        def home(p):
            return pltpu.make_async_remote_copy(src_ref=dkvs.at[h,p*kc:(p+1)*kc],dst_ref=home_ref.at[s,h],send_sem=kv_out.at[p,h],
                recv_sem=kv_in.at[p,h],device_id=(r,s^p),device_id_type=MESH)
        def keep():
            return pltpu.make_async_copy(dkvs.at[h,0:kc],home_ref.at[s,h],own.at[h])
        def turn(p):
            return pltpu.make_async_remote_copy(src_ref=dqw.at[s^p],dst_ref=dq_ref.at[s],send_sem=q_out.at[p],
                recv_sem=q_in.at[p],device_id=(r,s^p),device_id_type=MESH)
        def stay():
            return pltpu.make_async_copy(dqw.at[s],dq_ref.at[s],own.at[H])
        @pl.when((h==0)&(c==0))
        def _():
            greet_all(n*rows if plans else n,n)
            if plans: ride.start(sent,got,sems,greet=False)
        for hh in range(H):
            @pl.when((h==hh)&(c==0))
            def _():
                sl=slice(hh*HD,(hh+1)*HD)
                kaug[:,0:HD]=kv_ref[:,2*hh*HD:(2*hh+1)*HD]
                lane=lax.broadcasted_iota(jnp.int32,(Lk,HD),1)
                kaug[:,HD:2*HD]=jnp.where((lane>=3)&(lane<6),BF(1),ka_ref[...])
                vaug[:,0:HD]=kv_ref[:,(2*hh+1)*HD:(2*hh+2)*HD]
                vaug[:,HD:2*HD]=jnp.where(lane<3,BF(1),BF(0)).astype(BF)
                lq=lax.broadcasted_iota(jnp.int32,(Lq,HD),1)
                x,y,z=split3(-lse_ref[:,hh:hh+1])
                qaug[0:Lq,0:HD]=q_ref[:,sl]*BF(0.125)
                qaug[0:Lq,HD:2*HD]=jnp.where(lq==3,x,jnp.where(lq==4,y,jnp.where(lq==5,z,qa_ref[...])))
                dd=do_ref[:,sl]
                delta=jnp.sum(dd.astype(F32)*of_ref[:,sl],axis=1,keepdims=True)
                x,y,z=split3(-delta)
                doaug[0:Lq,0:HD]=dd
                doaug[0:Lq,HD:2*HD]=jnp.where(lq==0,x,jnp.where(lq==1,y,jnp.where(lq==2,z,BF(0))))
                dqacc[...]=jnp.zeros_like(dqacc)
                for b in range(n):
                    kt[b]=kv_ref[b*kc:(b+1)*kc,2*hh*HD:(2*hh+1)*HD].astype(F32).T.astype(BF)
        off=pl.multiple_of((n-1-c)*kc,kc)
        kk=kaug[pl.ds(off,kc),:]
        vv=vaug[pl.ds(off,kc),:]
        for i in range(0,Lq,qb):
            part=slice(i,min(i+qb,Lq))
            p=jnp.exp(nt(kk,qaug[part,:]))
            g=nt(vv,doaug[part,:])
            ps[:,part]=p.astype(BF)
            dss[:,part]=(p*g).astype(BF)
        dkvs[h,pl.ds(off,kc),0:HD]=nn(dss[...],qaug[:,0:HD]).astype(BF)
        dkvs[h,pl.ds(off,kc),HD:2*HD]=nn(ps[...],doaug[:,0:HD]).astype(BF)
        dqacc[...]+=nn(kt[n-1-c],dss[...])
        for p in range(1,n):
            @pl.when(c==n-1-p)
            def _():
                home(p).start()
        @pl.when(c==n-1)
        def _():
            keep().start()
            dqs[h]=(dqacc[...].T*0.125).astype(BF)
        @pl.when((c==n-1)&(h==H-1))
        def _():
            for b in range(n):
                dqw[b]=jnp.concatenate([dqs[t,b*(Lq//n):(b+1)*(Lq//n),:] for t in range(H)],axis=1)
            for p in range(1,n): turn(p).start()
            stay().start()
            for b,dkv_ref in enumerate(dkv_refs):
                for t in range(H): dkv_ref[:,2*t*HD:2*(t+1)*HD]=dkvs[t,b*kc:(b+1)*kc,:]
            for p in range(1,n): turn(p).wait()
            stay().wait()
            if plans: ride.wait(sent,got,sems)
        @pl.when(c==n-1)
        def _():
            for p in range(1,n): home(p).wait()
            keep().wait()
    full=lambda s: pl.BlockSpec(s,lambda h,c:(0,)*len(s))
    return pl.pallas_call(kern,grid=(H,n),
        out_shape=(jax.ShapeDtypeStruct((n,Lq//n,W),BF),jax.ShapeDtypeStruct((n,H,kc,2*HD),BF),jax.ShapeDtypeStruct((n,Lq//n,W),BF))+ride.shapes+(jax.ShapeDtypeStruct((kc,2*W),BF),)*n,
        in_specs=[full((Lq,W)),full((Lk,2*W)),full((Lq,W)),full((Lq,W)),full((Lq,128)),full((Lq,HD)),full((Lk,HD))]+[ANY]*ride.count,
        out_specs=(ANY,ANY,full((n,Lq//n,W)))+(ANY,)*ride.count+(full((kc,2*W)),)*n,
        scratch_shapes=[pltpu.VMEM((Lk,2*HD),BF),pltpu.VMEM((Lk,2*HD),BF),pltpu.VMEM((Lq,2*HD),BF),pltpu.VMEM((Lq,2*HD),BF),
            pltpu.VMEM((kc,Lq),BF),pltpu.VMEM((kc,Lq),BF),pltpu.VMEM((HD,Lq),F32),pltpu.VMEM((n,HD,kc),BF),pltpu.VMEM((H,Lq,HD),BF),pltpu.VMEM((H,Lk,2*HD),BF)]
            +[pltpu.SemaphoreType.DMA((n,))]*2+[pltpu.SemaphoreType.DMA((n,H))]*2+[pltpu.SemaphoreType.DMA((H+1,))]+riders,
        compiler_params=pltpu.CompilerParams(vmem_limit_bytes=60*2**20,collective_id=10,has_side_effects=True),cost_estimate=cost(68.0),name="cross_bwd")(q,kv,do,of,lse,qa,ka,*[x for kind,x in plans])

def toeplitz(line, shift):
    return pltpu.roll(jnp.broadcast_to(line,(128,line.shape[1])),shift,1,stride=1,stride_axis=0)

def toeplitz_rows(x):
    return pltpu.roll(x,1,1,stride=1,stride_axis=0)

def eye128():
    return lax.broadcasted_iota(jnp.int32,(128,128),0)==lax.broadcasted_iota(jnp.int32,(128,128),1)

def self_fwd(qkv,rev,qa,ka):
    Lq,W=qkv.shape[0],qkv.shape[1]//3; H=W//HD; nb=Lq//128
    def kern(qkv_ref,rev_ref,qa_ref,ka_ref,o_ref,of_ref,lse_ref,qaug,kaug,kdiag,vs,os,tz):
        h=pl.program_id(0)
        for hh in range(H):
            @pl.when(h==hh)
            def _():
                sl=slice(hh*HD,(hh+1)*HD)
                qaug[:,0:HD]=qkv_ref[:,sl]*BF(0.125); qaug[:,HD:]=qa_ref[...]
                kaug[:,0:HD]=qkv_ref[:,W+hh*HD:W+(hh+1)*HD]; kaug[:,HD:]=ka_ref[...]
                kdiag[:,0:HD]=qkv_ref[:,W+hh*HD:W+(hh+1)*HD]; kdiag[:,HD:]=jnp.zeros((Lq,HD),BF)
                vs[...]=qkv_ref[:,2*W+hh*HD:2*W+(hh+1)*HD]
        @pl.when(h==0)
        def _():
            lse_ref[...]=jnp.zeros((Lq,128),F32)
        bands=toeplitz(rev_ref[pl.ds(h,1),:],(nb+1)*128-127)
        for d in range(nb):
            tz[d]=bands[:,(nb-1-d)*128:(nb-d)*128]
        eye=eye128()
        lane=lax.broadcasted_iota(jnp.int32,(128,128),1)
        for q0 in range(0,Lq,256):
            qn=min(256,Lq-q0); kend=q0+qn
            s=nt(qaug[q0:q0+qn,:],kaug[0:kend,:])
            for a in range(qn//128):
                qt=q0//128+a
                r0=q0+a*128
                rows=slice(r0,r0+128)
                sd=nt(qaug[rows,:],kdiag[rows,:])
                tiles=[]
                for b in range(qt+1):
                    t=s[a*128:(a+1)*128,b*128:(b+1)*128]
                    if b==qt: t=jnp.where(eye,sd,t)
                    tiles.append(t+tz[qt-b])
                m=tiles[0]
                for t in tiles[1:]: m=jnp.maximum(m,t)
                m=jnp.max(m,axis=1,keepdims=True)
                ps=[jnp.exp(t-m) for t in tiles]
                l=ps[0]
                for t in ps[1:]: l=l+t
                l=jnp.sum(l,axis=1,keepdims=True)
                pb=jnp.concatenate([t.astype(BF) for t in ps],axis=1)
                os[h,rows,:]=nn(pb,vs[0:(qt+1)*128,:])/l
                lse_ref[rows,:]=jnp.where(lane==h,m+jnp.log(l),lse_ref[rows,:])
        @pl.when(h==H-1)
        def _():
            oo=jnp.concatenate([os[t] for t in range(H)],axis=1)
            o_ref[...]=oo.astype(BF)
            of_ref[...]=oo
    full=lambda s: pl.BlockSpec(s,lambda h:(0,)*len(s))
    return pl.pallas_call(kern,grid=(H,),
        out_shape=(jax.ShapeDtypeStruct((Lq,W),BF),jax.ShapeDtypeStruct((Lq,W),F32),jax.ShapeDtypeStruct((Lq,128),F32)),
        in_specs=[full((Lq,3*W)),full(rev.shape),full((Lq,HD)),full((Lq,HD))],
        out_specs=(full((Lq,W)),full((Lq,W)),full((Lq,128))),
        scratch_shapes=[pltpu.VMEM((Lq,2*HD),BF)]*3+[pltpu.VMEM((Lq,HD),BF),pltpu.VMEM((H,Lq,HD),F32),pltpu.VMEM((nb,128,128),F32)],
        compiler_params=pltpu.CompilerParams(vmem_limit_bytes=48*2**20),cost_estimate=cost(15.0),name="self_fwd")(qkv,rev,qa,ka)

MESH = pl.DeviceIdType.MESH
ANY = pl.BlockSpec(memory_space=pl.ANY)
VM = pl.BlockSpec(memory_space=pltpu.VMEM)


def cost(micros):
    return pl.CostEstimate(flops=int(micros * 1.0e9), bytes_accessed=int(micros * 3.0e6), transcendentals=0)


def greet_all(count, n):
    r, s = lax.axis_index("rows"), lax.axis_index("seq")
    barrier = pltpu.get_barrier_semaphore()

    def greet(step, carry):
        j = lax.rem((s if count == n else r * n + s) + step, count)
        device = (r, j) if count == n else (lax.div(j, n), lax.rem(j, n))
        pl.semaphore_signal(barrier, inc=1, device_id=device, device_id_type=MESH)
        return carry

    lax.fori_loop(1, count, greet, 0)
    pl.semaphore_wait(barrier, count - 1)


class Exchange:
    def __init__(self, plans, n, rows):
        self.kinds = [kind for kind, x in plans]
        self.count = len(plans)
        self.n, self.rows = n, rows
        shapes = [(n * rows,) + x.shape[1:] if kind == "own" else x.shape for kind, x in plans]
        self.shapes = tuple(jax.ShapeDtypeStruct(shape, x.dtype) for shape, (kind, x) in zip(shapes, plans))
        self.scratch = [pltpu.SemaphoreType.DMA((shape[0],)) for shape in shapes for side in range(2)]
        self.scratch += [pltpu.SemaphoreType.DMA((self.count,))]

    def each(self, sent, got, sems, act):
        n, rows = self.n, self.rows
        r, s = lax.axis_index("rows"), lax.axis_index("seq")
        me = r * n + s
        for p, kind in enumerate(self.kinds):
            x, y, out_sem, in_sem, own = sent[p], got[p], sems[2 * p], sems[2 * p + 1], sems[-1].at[p]

            def remote(block, slot, device, leave, arrive, x=x, y=y, out_sem=out_sem, in_sem=in_sem):
                return pltpu.make_async_remote_copy(
                    src_ref=x.at[block], dst_ref=y.at[slot], send_sem=out_sem.at[leave], recv_sem=in_sem.at[arrive],
                    device_id=device, device_id_type=MESH,
                )

            if kind == "rows":
                def send(j, carry, act=act, x=x, y=y, own=own, remote=remote):
                    target = s * rows + j
                    away = remote(j, r, (lax.div(target, n), lax.rem(target, n)), j, r)

                    @pl.when(target != me)
                    def _():
                        act(away, True)

                    @pl.when(target == me)
                    def _():
                        act(pltpu.make_async_copy(x.at[j], y.at[r], own), None)

                    return carry

                def take(q, carry, act=act, remote=remote):
                    @pl.when((q != r) | (lax.div(me, rows) != s))
                    def _():
                        act(remote(0, q, (r, s), 0, q), False)

                    return carry

                lax.fori_loop(0, rows, send, 0)
                lax.fori_loop(0, rows, take, 0)
                continue
            if kind == "xor":
                act(pltpu.make_async_copy(x.at[0], y.at[s], own), None)
                for p in range(1, n):
                    away = remote(p, s, (r, s ^ p), p, p)
                    act(away, True)
                    act(away, False)
                continue
            length, here = (n, s) if kind == "seq" else (n * rows, me)
            act(pltpu.make_async_copy(x.at[s if kind == "own" else here], y.at[here], own), None)

            def both_ways(step, carry, act=act, length=length, here=here, kind=kind, remote=remote):
                j = lax.rem(here + step, length)
                device = (r, j) if kind == "seq" else (lax.div(j, n), lax.rem(j, n))
                away = remote(lax.rem(j, n) if kind == "own" else j, here, device, step, step)
                act(away, True)
                act(away, False)
                return carry

            lax.fori_loop(1, length, both_ways, 0)

    def start(self, sent, got, sems, greet=True):
        near = all(kind == "seq" for kind in self.kinds)
        if greet:
            greet_all(self.n if near else self.n * self.rows, self.n)
        self.each(sent, got, sems, lambda copy, away: copy.start() if away is not False else None)

    def wait(self, sent, got, sems):
        def act(copy, away):
            if away is None:
                copy.wait()
            elif away:
                copy.wait_send()
            else:
                copy.wait_recv()

        self.each(sent, got, sems, act)


class Job:
    def __init__(self, inputs=(), outs=(), body=None):
        self.inputs, self.outs, self.body = list(inputs), tuple(outs), body
        self.scratch = [pltpu.VMEM(x.shape, x.dtype) for x in self.inputs]
        self.scratch += [pltpu.SemaphoreType.DMA((len(self.inputs),))] if self.inputs else []

    def split(self, refs, before, between, after):
        i, o = len(self.inputs), len(self.outs)
        head, refs = refs[:before], refs[before:]
        ins, refs = refs[:i], refs[i:]
        middle, refs = refs[:between], refs[between:]
        outs, refs = refs[:o], refs[o:]
        return head + middle + refs[:after], ins, outs, refs[after:]

    def run(self, ins, outs, scratch):
        if not self.inputs:
            return
        held, sem = scratch[:-1], scratch[-1]
        copies = [pltpu.make_async_copy(x, y, sem.at[k]) for k, (x, y) in enumerate(zip(ins, held))]
        for copy in copies:
            copy.start()
        for copy in copies:
            copy.wait()
        self.body(held, outs)


def exchange(plans, n, rows, collective_id, job=None):
    ride, job = Exchange(plans, n, rows), job or Job()

    def kern(*refs):
        refs, ins, outs, scratch = job.split(refs, ride.count, ride.count, len(ride.scratch))
        sent, got, sems = refs[: ride.count], refs[ride.count : 2 * ride.count], refs[2 * ride.count :]
        ride.start(sent, got, sems)
        job.run(ins, outs, scratch)
        ride.wait(sent, got, sems)

    return pl.pallas_call(
        kern,
        out_shape=ride.shapes + job.outs,
        in_specs=[ANY] * (ride.count + len(job.inputs)),
        out_specs=(ANY,) * ride.count + (VM,) * len(job.outs),
        scratch_shapes=ride.scratch + job.scratch,
        compiler_params=pltpu.CompilerParams(
            collective_id=collective_id, has_side_effects=True, vmem_limit_bytes=56 * 2**20
        ),
        cost_estimate=cost(20.0),name="exchange",
    )(*[x for kind, x in plans], *job.inputs)


def gather_seq(values, n, rows, collective_id, plans=(), job=None):
    ride, job = Exchange(plans, n, rows), job or Job()
    sems_used = ride.scratch if ride.count else []

    def kern(*refs):
        refs, ins, outs, scratch = job.split(refs, 1 + ride.count, 1 + ride.count, 5 + len(sems_used))
        x_ref, sent, o_ref = refs[0], refs[1 : 1 + ride.count], refs[1 + ride.count]
        got, rest = refs[2 + ride.count : 2 + 2 * ride.count], refs[2 + 2 * ride.count :]
        own, out_sem, in_sem, side_out, side_in = rest[:5]
        sems = rest[5:]
        r, s = lax.axis_index("rows"), lax.axis_index("seq")
        beside = s + 1 - 2 * lax.rem(s, 2)
        if ride.count:
            greet_all(n * rows, n)
        else:
            barrier = pltpu.get_barrier_semaphore()
            for step in range(2, n, 2):
                pl.semaphore_signal(barrier, inc=1, device_id=(r, lax.rem(s + step, n)), device_id_type=MESH)
            pl.semaphore_signal(barrier, inc=1, device_id=(r, beside), device_id_type=MESH)
            pl.semaphore_wait(barrier, n // 2)
        far = [
            pltpu.make_async_remote_copy(
                src_ref=x_ref, dst_ref=o_ref.at[s], send_sem=out_sem.at[k], recv_sem=in_sem.at[k],
                device_id=(r, lax.rem(s + 2 * k, n)), device_id_type=MESH,
            )
            for k in range(1, n // 2)
        ]
        for copy in far:
            copy.start()

        def across(k):
            slot = lax.rem(s + n - 2 * k, n)
            return pltpu.make_async_remote_copy(
                src_ref=x_ref if k == 0 else o_ref.at[slot], dst_ref=o_ref.at[slot],
                send_sem=side_out.at[k], recv_sem=side_in.at[k], device_id=(r, beside), device_id_type=MESH,
            )

        near = [across(k) for k in range(n // 2)]
        near[0].start()
        local = pltpu.make_async_copy(x_ref, o_ref.at[s], own)
        local.start()
        if ride.count:
            ride.start(sent, got, sems, greet=False)
        for k, copy in enumerate(far):
            job.run(ins, outs, scratch) if k == 0 else None
            copy.wait_recv()
            near[k + 1].start()
        for copy in near:
            copy.wait()
        for copy in far:
            copy.wait_send()
        local.wait()
        if ride.count:
            ride.wait(sent, got, sems)

    length, features = values.shape
    whole, *got = pl.pallas_call(
        kern,
        out_shape=(jax.ShapeDtypeStruct((n, length, features), values.dtype),) + ride.shapes + job.outs,
        in_specs=[ANY] * (1 + ride.count + len(job.inputs)),
        out_specs=(ANY,) * (1 + ride.count) + (VM,) * len(job.outs),
        scratch_shapes=[pltpu.SemaphoreType.DMA] + [pltpu.SemaphoreType.DMA((n // 2,))] * 4
        + sems_used + job.scratch,
        compiler_params=pltpu.CompilerParams(
            collective_id=collective_id, has_side_effects=True, vmem_limit_bytes=56 * 2**20
        ),
        cost_estimate=cost(20.0),
        name="gather_seq",
    )(values, *[x for kind, x in plans], *job.inputs)
    whole = whole.reshape(n * length, features)
    return (whole, *got) if got else whole


def project_blocks(blocks, weight):
    length, width = blocks[0].shape[0], weight.shape[1]
    count = len(blocks)

    def kern(*refs):
        weight_ref, o_ref = refs[count], refs[count + 1]
        for k in range(count):
            o_ref[k * length : (k + 1) * length, :] = nn(refs[k][...], weight_ref[...]).astype(BF)

    return pl.pallas_call(
        kern,
        out_shape=jax.ShapeDtypeStruct((count * length, width), BF),
        in_specs=[VM] * (count + 1),
        out_specs=VM,
        compiler_params=pltpu.CompilerParams(vmem_limit_bytes=40 * 2**20),
        cost_estimate=cost(8.0),
        name="project_blocks",
    )(*blocks, weight)


def self_bwd(qkv,do,of,lse,fwd,qa,ka,plans,n,rows):
    Lq,W=qkv.shape[0],qkv.shape[1]//3; H=W//HD; nb=Lq//128
    ride=Exchange(plans,n,rows)
    def kern(qkv_ref,do_ref,of_ref,lse_ref,fwd_ref,qa_ref,ka_ref,*rest):
        sent,rest=rest[:ride.count],rest[ride.count:]
        grad_ref,gb_ref=rest[:2]
        got,rest=rest[2:2+ride.count],rest[2+ride.count:]
        (qaug,kaug,kdiag,vaug,doaug,dkacc,dvacc,dqs,dks,dvs,tz,ga),sems=rest[:12],rest[12:]
        h=pl.program_id(0)
        @pl.when(h==0)
        def _():
            ride.start(sent,got,sems)
        for hh in range(H):
            @pl.when(h==hh)
            def _():
                sl=slice(hh*HD,(hh+1)*HD)
                lane=lax.broadcasted_iota(jnp.int32,(Lq,HD),1)
                kaug[:,0:HD]=qkv_ref[:,W+hh*HD:W+(hh+1)*HD]
                ones=(lane>=3)&(lane<6)
                kaug[:,HD:]=jnp.where(ones,BF(1),ka_ref[...])
                kdiag[:,0:HD]=qkv_ref[:,W+hh*HD:W+(hh+1)*HD]
                kdiag[:,HD:]=jnp.where(ones,BF(1),BF(0)).astype(BF)
                vaug[:,0:HD]=qkv_ref[:,2*W+hh*HD:2*W+(hh+1)*HD]
                vaug[:,HD:]=jnp.where(lane<3,BF(1),BF(0)).astype(BF)
                a,b,c=split3(-lse_ref[:,hh:hh+1])
                qaug[:,0:HD]=qkv_ref[:,sl]*BF(0.125)
                qaug[:,HD:]=jnp.where(lane==3,a,jnp.where(lane==4,b,jnp.where(lane==5,c,qa_ref[...])))
                dd=do_ref[:,sl]
                delta=jnp.sum(dd.astype(F32)*of_ref[:,sl],axis=1,keepdims=True)
                a,b,c=split3(-delta)
                doaug[:,0:HD]=dd
                doaug[:,HD:]=jnp.where(lane==0,a,jnp.where(lane==1,b,jnp.where(lane==2,c,BF(0))))
        dkacc[...]=jnp.zeros_like(dkacc)
        dvacc[...]=jnp.zeros_like(dvacc)
        ga[...]=jnp.zeros_like(ga)
        bands=toeplitz(fwd_ref[pl.ds(h,1),:],nb*128)
        for d in range(nb):
            tz[d]=bands[:,d*128:(d+1)*128]
        eye=eye128()
        for q0 in range(0,Lq,256):
            qn=min(256,Lq-q0); kend=q0+qn
            qg=qaug[q0:kend,:]; dg=doaug[q0:kend,:]
            s=nt(kaug[0:kend,:],qg)
            g=nt(vaug[0:kend,:],dg)
            pcols=[]; dcols=[]
            for a in range(qn//128):
                qt=q0//128+a
                rows=slice(q0+a*128,q0+(a+1)*128)
                sd=nt(kdiag[rows,:],qaug[rows,:])
                pt=[]; dt=[]
                for b in range(kend//128):
                    d=qt-b
                    if d<0:
                        pt.append(jnp.zeros((128,128),BF)); dt.append(jnp.zeros((128,128),BF)); continue
                    t=s[b*128:(b+1)*128,a*128:(a+1)*128]
                    if d==0: t=jnp.where(eye,sd,t)
                    p=jnp.exp(t+tz[d])
                    ds=(p*g[b*128:(b+1)*128,a*128:(a+1)*128]).astype(BF)
                    ga[d]+=ds.astype(F32)
                    pt.append(p.astype(BF)); dt.append(ds)
                pcols.append(jnp.concatenate(pt,axis=0)); dcols.append(jnp.concatenate(dt,axis=0))
            P=jnp.concatenate(pcols,axis=1); DS=jnp.concatenate(dcols,axis=1)
            dvacc[0:kend,:]+=nn(P,dg[:,0:HD])
            dkacc[0:kend,:]+=nn(DS,qg[:,0:HD])
            dqs[h,q0:kend,:]=(tn(DS,kaug[0:kend,0:HD])*0.125).astype(BF)
        dks[h]=dkacc[...].astype(BF)
        dvs[h]=dvacc[...].astype(BF)
        flip=(lax.broadcasted_iota(jnp.int32,(128,128),0)+lax.broadcasted_iota(jnp.int32,(128,128),1)==127).astype(F32)
        y=jnp.concatenate([ga[d] for d in range(nb)],axis=1)
        y=lax.dot_general(flip,y,(((1,),(0,)),((),())),preferred_element_type=F32,precision=lax.Precision.HIGHEST)
        y=toeplitz_rows(jnp.concatenate([y,jnp.zeros((128,128),F32)],axis=1))
        gb_ref[pl.ds(h,1),:]=jnp.sum(y,axis=0,keepdims=True)
        @pl.when(h==H-1)
        def _():
            grad_ref[...]=jnp.concatenate([x[t] for x in (dqs,dks,dvs) for t in range(H)],axis=1)
            ride.wait(sent,got,sems)
    full=lambda s: pl.BlockSpec(s,lambda h:(0,)*len(s))
    return pl.pallas_call(kern,grid=(H,),
        out_shape=(jax.ShapeDtypeStruct((Lq,3*W),BF),jax.ShapeDtypeStruct((H,(nb+1)*128),F32))+ride.shapes,
        in_specs=[full((Lq,3*W))]+[full((Lq,W))]*2+[full((Lq,128)),full(fwd.shape),full((Lq,HD)),full((Lq,HD))]+[ANY]*ride.count,
        out_specs=(full((Lq,3*W)),full((H,(nb+1)*128)))+(ANY,)*ride.count,
        scratch_shapes=[pltpu.VMEM((Lq,2*HD),BF)]*5+[pltpu.VMEM((Lq,HD),F32)]*2+[pltpu.VMEM((H,Lq,HD),BF)]*3+[pltpu.VMEM((nb,128,128),F32)]*2+ride.scratch,
        compiler_params=pltpu.CompilerParams(vmem_limit_bytes=48*2**20,collective_id=11,has_side_effects=True),cost_estimate=cost(35.0),name="self_bwd")(
            qkv,do,of,lse,fwd,qa,ka,*[x for kind,x in plans])


MESH = pl.DeviceIdType.MESH


def sum_parts(first, cross, self_out, cross_out, n, wd):
    devices, count, wide = first.shape
    total = self_out.shape[0]

    def kern(first_ref, cross_ref, self_out_ref, cross_out_ref, sum_ref, col_ref, mean_ref):
        lane = lax.broadcasted_iota(jnp.int32, (count, 128), 1)
        means = jnp.zeros((count, 128), F32)
        sums = [None] * 8
        for ref, matrices in ((first_ref, (0, 1, 2)), (cross_ref, (4, 5, 6))):
            parts = []
            for s in range(n):
                part = ref[s].astype(F32)
                for r in range(1, devices // n):
                    part = part + ref[r * n + s].astype(F32)
                parts.append(part)
            for k, j in enumerate(matrices):
                if j > 4:
                    low = range(wd + (k - 1) * HD, 3 * wd, 2 * HD)
                    pieces = [part[:, c : c + HD] for part in parts for c in low]
                else:
                    pieces = [part[:, k * wd : (k + 1) * wd] for part in parts]
                sums[j] = jnp.concatenate(pieces, 1)[:, :D]
        for j, ref in ((3, self_out_ref), (7, cross_out_ref)):
            sums[j] = ref[0].astype(F32)
            for r in range(1, total):
                sums[j] = sums[j] + ref[r].astype(F32)
        for j in range(8):
            square = sums[j] * sums[j]
            sum_ref[j] = sums[j]
            col_ref[j : j + 1, :] = jnp.sum(square, 0, keepdims=True)
            means = jnp.where(lane == j, jnp.mean(square, 1, keepdims=True), means)
        mean_ref[...] = means

    return pl.pallas_call(
        kern,
        out_shape=(
            jax.ShapeDtypeStruct((8, count, D), F32),
            jax.ShapeDtypeStruct((8, D), F32),
            jax.ShapeDtypeStruct((count, 128), F32),
        ),
        in_specs=[VM] * 4,
        out_specs=(VM,) * 3,
        compiler_params=pltpu.CompilerParams(vmem_limit_bytes=32 * 2**20),
        cost_estimate=cost(4.0),name="sum_parts",
    )(first, cross, self_out, cross_out)


def sum_everywhere(arrays, n, rows):
    count = n * rows
    wide_tiles, tiles = FF // 128, D // 128
    table_at, sums_at = tiles + wide_tiles, tiles + wide_tiles + BUCKETS // 8
    assert sums_at < count

    def kern(att, exp, con, att_rows, exp_rows, con_rows, gain, table, *rest):
        outs, (x, o, got, mine, out_sem, in_sem, out_sem2, in_sem2) = rest[:6], rest[6:]
        me = lax.axis_index("rows") * n + lax.axis_index("seq")

        def place(step):
            j = lax.rem(me + step, count)
            return j, (lax.div(j, n), lax.rem(j, n))

        x[...] = jnp.zeros(x.shape, F32)
        for t in range(tiles):
            x[t] = att[:, t * 128 : (t + 1) * 128]
            x[tiles + t, 2:5, :] = gain[:, t * 128 : (t + 1) * 128]
            x[tiles + t, 5:6, :] = con[:, t * 128 : (t + 1) * 128]
        for t in range(wide_tiles):
            x[tiles + t, 0:2, :] = exp[:, t * 128 : (t + 1) * 128]
        for t in range(BUCKETS // 8):
            x[table_at + t, :, 0:HEADS] = table[t * 8 : (t + 1) * 8, :]
        x[sums_at, :, 0:1] = jnp.sum(att_rows[...], 1, keepdims=True)
        x[sums_at, 0:2, 1:2] = jnp.sum(exp_rows[...], 1, keepdims=True)
        x[sums_at, 0:1, 2:3] = jnp.sum(con_rows[...], 1, keepdims=True)
        greet_all(count, n)

        def piece(step):
            j, device = place(step)
            return pltpu.make_async_remote_copy(
                src_ref=x.at[j], dst_ref=got.at[step], send_sem=out_sem.at[step], recv_sem=in_sem.at[step],
                device_id=device, device_id_type=MESH,
            )

        def total(step):
            return pltpu.make_async_remote_copy(
                src_ref=mine, dst_ref=o.at[me], send_sem=out_sem2.at[step], recv_sem=in_sem2.at[step],
                device_id=place(step)[1], device_id_type=MESH,
            )

        def start_piece(step, carry):
            piece(step).start()
            return carry

        def add_piece(step, carry):
            piece(step).wait()
            return carry + got[step]

        def start_total(step, carry):
            total(step).start()
            return carry

        def wait_total(step, carry):
            total(step).wait()
            return carry

        lax.fori_loop(1, count, start_piece, 0)
        mine[...] = lax.fori_loop(1, count, add_piece, x[me])
        lax.fori_loop(1, count, start_total, 0)
        o[me] = mine[...]
        lax.fori_loop(1, count, wait_total, 0)
        att_out, exp_out, con_out, sums_out, gain_out, table_out = outs
        for t in range(tiles):
            att_out[:, t * 128 : (t + 1) * 128] = o[t]
            gain_out[:, t * 128 : (t + 1) * 128] = o[tiles + t, 2:5, :]
            con_out[:, t * 128 : (t + 1) * 128] = o[tiles + t, 5:6, :]
        for t in range(wide_tiles):
            exp_out[:, t * 128 : (t + 1) * 128] = o[tiles + t, 0:2, :]
        for t in range(BUCKETS // 8):
            table_out[t * 8 : (t + 1) * 8, :] = o[table_at + t, :, 0:HEADS]
        sums_out[...] = o[sums_at]

    shapes = ((8, D), (2, FF), (1, D), (8, 128), (3, D), (BUCKETS, HEADS))
    return pl.pallas_call(
        kern,
        out_shape=tuple(jax.ShapeDtypeStruct(shape, F32) for shape in shapes),
        in_specs=[VM] * 8,
        out_specs=(VM,) * 6,
        scratch_shapes=[pltpu.VMEM((count, 8, 128), F32)] * 3
        + [pltpu.VMEM((8, 128), F32)]
        + [pltpu.SemaphoreType.DMA((count,))] * 4,
        compiler_params=pltpu.CompilerParams(collective_id=1, has_side_effects=True),
        cost_estimate=cost(16.0),
        name="sum_everywhere",
    )(*arrays)


def normalize(values, scaling):
    return values * lax.rsqrt(jnp.mean(values * values, -1, keepdims=True) + NORM_EPS) * scaling


def gated(gate_values, up_values):
    return jax.nn.gelu(gate_values, approximate=True) * up_values


def factored_start(gradient, rowwise):
    square = gradient * gradient
    rowwise_new = BETA_TWO * rowwise + (1.0 - BETA_TWO) * jnp.mean(square, 2).T
    return (rowwise_new, jnp.sum(square, 0))


def factored_finish(gradient, moment, rowwise_new, colwise, weight, column_sum, row_sum, total_rows):
    colwise_new = BETA_TWO * colwise + (1.0 - BETA_TWO) * (column_sum / total_rows)
    moment_new = BETA_ONE * moment + (1.0 - BETA_ONE) * gradient
    second = rowwise_new.T[:, :, None] * colwise_new[None] / (row_sum / total_rows)[None, :, None]
    stepped = (
        moment_new / (1.0 - BETA_ONE**STEP) / (jnp.sqrt(second / (1.0 - BETA_TWO**STEP)) + ADAM_EPS)
    )
    updated = weight - MATRIX_RATE * (stepped + WEIGHT_DECAY * weight)
    return (moment_new, colwise_new, updated)


def adaptive(gradient, moment, second, weight):
    moment_new = BETA_ONE * moment + (1.0 - BETA_ONE) * gradient
    second_new = BETA_TWO * second + (1.0 - BETA_TWO) * gradient * gradient
    stepped = (
        moment_new
        / (1.0 - BETA_ONE**STEP)
        / (jnp.sqrt(second_new / (1.0 - BETA_TWO**STEP)) + ADAM_EPS)
    )
    return (moment_new, second_new, weight - VECTOR_RATE * stepped)


def make_shards(n, rows):
    devices = n * rows
    both = ("rows", "seq")
    hpd = -(-HEADS // n)
    wd = hpd * HD
    wide = n * wd

    def widen(values):
        extra = wide - values.shape[-1]
        return values if extra == 0 else jnp.pad(values, [(0, 0)] * (values.ndim - 1) + [(0, extra)])

    def blocks_along_seq(values, gate):
        blocks = []
        for step in range(0, n, 2):
            block = values
            if step:
                block = lax.ppermute(values, "seq", [(i, i ^ step) for i in range(n)])
                block = lax.optimization_barrier((block, gate))[0]
            blocks += [block, lax.ppermute(block, "seq", [(i, i ^ 1) for i in range(n)])]
        return blocks

    def by_heads(weight):
        count, j = weight.shape[:2]
        return jnp.moveaxis(widen(weight).reshape(count, j, n * hpd, HD), 2, 1).reshape(count, wide * j)

    def to_seq(values, collective_id):
        (parts,) = exchange([("seq", values.reshape(n, -1, values.shape[1]))], n, rows, collective_id)
        return side_by_side(parts)[:, :D]

    def side_by_side(parts):
        return jnp.moveaxis(parts, 0, 1).reshape(parts.shape[1], -1)

    def shards(
        decoder_input,
        encoder_output,
        cotangent,
        decoder_segment,
        decoder_padding,
        encoder_segment,
        encoder_padding,
        distance_bucket,
        attention_weight,
        attention_moment,
        attention_rowwise,
        attention_colwise,
        expand_weight,
        expand_moment,
        expand_rowwise,
        expand_colwise,
        contract_weight,
        contract_moment,
        contract_rowwise,
        contract_colwise,
        norm_gain,
        gain_moment,
        gain_second,
        relative_table,
        table_moment,
        table_second,
    ):
        shard = lax.axis_index("seq")
        length = decoder_segment.shape[1]
        attention_low = attention_weight.astype(BF)
        count = expand_weight.shape[0]
        first_parts = jnp.moveaxis(widen(attention_low[:, 0:3]).reshape(count, 3, n, wd), 2, 0)
        row_input, first_columns = gather_seq(
            decoder_input[0], n, rows, 3, [("own", first_parts.reshape(n, count, 3 * wd))]
        )
        first_columns = first_columns.reshape(D, 3 * wd)
        attention_full = lax.all_gather(
            jnp.concatenate(
                (
                    attention_low[:, 3],
                    attention_low[:, 7],
                    by_heads(attention_low[:, 4:5]),
                    by_heads(attention_low[:, 5:7]),
                ),
                1,
            ),
            both, axis=0, tiled=True,
        )
        deep = -(-contract_weight.shape[0] // count)
        spare = deep * count - contract_weight.shape[0]
        contract_low = jnp.pad(contract_weight.astype(BF), ((0, spare), (0, 0)))
        feed_full = lax.all_gather(
            jnp.concatenate(
                (
                    expand_weight.astype(BF).reshape(count, 2 * FF),
                    jnp.moveaxis(contract_low.reshape(deep, count, D), 0, 1).reshape(count, deep * D),
                ),
                1,
            ),
            both, axis=0, tiled=True,
        )
        expand_full = feed_full[:, 0 : 2 * FF]
        contract_full = jnp.concatenate(
            [
                feed_full[:, 2 * FF + g * D : 2 * FF + (g + 1) * D].reshape(devices, count, D)[
                    :, : contract_weight.shape[0] - g * count
                ]
                for g in range(deep)
            ],
            1,
        ).reshape(FF, D)
        edges = (0, D, 2 * D, 2 * D + wide, 2 * D + 3 * wide)
        self_out_weight, cross_out_weight, cross_query_weight, cross_pair_weight = (
            attention_full[:, low:high] for low, high in zip(edges[:-1], edges[1:])
        )
        cross_query_columns = lax.dynamic_slice_in_dim(cross_query_weight, shard * wd, wd, 1)
        cross_columns = lax.dynamic_slice_in_dim(cross_pair_weight, shard * 2 * wd, 2 * wd, 1)

        def own_rows(matrix):
            padded = jnp.pad(matrix, ((0, wide - D), (0, 0))) if wide > D else matrix
            return lax.dynamic_slice_in_dim(padded, shard * wd, wd, 0)

        document = jnp.arange(HD, dtype=jnp.int32)[None, :]
        decoder_document = decoder_segment[0][:, None] == document
        query_side = decoder_document.astype(BF)
        self_side = jnp.where(
            (document < 3) & ~(decoder_document & (decoder_padding[0][:, None] == 1)), NEG, 0.0
        ).astype(BF)
        real_document = jnp.where(encoder_padding[0] == 1, encoder_segment[0], -1).reshape(n, -1)
        real_document = jnp.concatenate(
            [lax.dynamic_slice_in_dim(real_document, shard ^ p, 1, 0)[0] for p in range(n)]
        )
        cross_side = jnp.where(
            (document < 3) & (real_document[:, None] != document), NEG, 0.0
        ).astype(BF)
        onehot = (
            distance_bucket[:, None] == jnp.arange(BUCKETS, dtype=jnp.int32)[None, :]
        ).astype(F32)
        table_own = lax.dynamic_slice_in_dim(
            jnp.pad(relative_table, ((0, 0), (0, n * hpd - HEADS))), shard * hpd, hpd, 1
        )
        bias = jnp.einsum("db,bh->hd", onehot, table_own, precision=HIGHEST)
        beyond = jnp.full((hpd, 128), NEG, F32)
        bias_forward = jnp.concatenate((beyond, bias), 1)
        bias_backward = jnp.concatenate((bias[:, ::-1], beyond), 1)

        def dot(left, right):
            return jnp.dot(left, right, preferred_element_type=F32)

        def dot_back(left, right):
            return lax.dot_general(left, right, (((1,), (1,)), ((), ())), preferred_element_type=F32)

        def outer(left, right):
            return lax.dot_general(left, right, (((0,), (0,)), ((), ())), preferred_element_type=F32)

        row_norm = normalize(row_input.astype(F32), norm_gain[0]).astype(BF)
        self_proj = dot(row_norm, first_columns).astype(BF)
        self_heads, self_exact, self_lse = self_fwd(
            self_proj, bias_backward, query_side, self_side
        )
        inputs = decoder_input[0].astype(F32)
        self_out = to_seq(self_heads, 8)
        after_self = inputs + dot(self_out, self_out_weight)
        encoder_blocks = blocks_along_seq(
            lax.optimization_barrier((encoder_output[0], row_input))[0], after_self
        )
        cross_norm = normalize(after_self, norm_gain[1]).astype(BF)
        row_cross_norm = gather_seq(cross_norm, n, rows, 4)
        cross_query = dot(row_cross_norm, cross_query_columns).astype(BF)
        cross_pair = project_blocks(encoder_blocks, cross_columns)
        cross_heads, cross_exact, cross_lse = cross_fwd(
            cross_query, cross_pair, query_side, cross_side
        )
        cross_out = to_seq(cross_heads, 9)
        after_cross = after_self + dot(cross_out, cross_out_weight)
        feed_norm = normalize(after_cross, norm_gain[2]).astype(BF)
        hidden_pair = dot(feed_norm, expand_full)
        gate_values, up_values = hidden_pair[:, 0:FF], hidden_pair[:, FF:]
        feed_branch = cotangent[0]
        grad_result = feed_branch.astype(F32)
        grad_hidden = dot_back(feed_branch, contract_full)
        hidden_wide, gated_back = jax.vjp(gated, gate_values, up_values)
        hidden = hidden_wide.astype(BF)
        grad_gate, grad_up = gated_back(grad_hidden)
        grad_pair = jnp.concatenate((grad_gate.astype(BF), grad_up.astype(BF)), 1)
        unused_norm, norm_back = jax.vjp(normalize, after_cross, norm_gain[2])
        feed_part, feed_gain = norm_back(dot_back(grad_pair, expand_full))
        grad_after_cross = grad_result + feed_part
        cross_branch = grad_after_cross.astype(BF)
        down_rows = deep * count - spare

        def feed_gradients(ins, outs):
            norm_ref, pair_ref, hidden_ref, branch_ref = ins
            (o_ref,) = outs
            for c in range(0, 2 * FF, 512):
                part = tn(norm_ref[...], pair_ref[:, c : c + 512])
                o_ref[:, :, c : c + 512] = part.reshape(devices, count, 512).astype(BF)
            group = devices * 1024 // FF
            for c in range(0, FF, 1024):
                part = tn(hidden_ref[:, c : c + 1024], branch_ref[...]).reshape(group, down_rows, D)
                first = c // 1024 * group
                for g in range(deep):
                    piece = part[:, g * count : (g + 1) * count]
                    if piece.shape[1] < count:
                        low = jnp.zeros((group, count - piece.shape[1], D), F32)
                        piece = jnp.concatenate((piece, low), 1)
                    o_ref[first : first + group, :, 2 * FF + g * D : 2 * FF + (g + 1) * D] = piece.astype(BF)

        if count % 8 == 0:
            row_cross_branch, feed_local = gather_seq(
                cross_branch, n, rows, 5,
                job=Job(
                    (feed_norm, grad_pair, hidden, feed_branch),
                    (jax.ShapeDtypeStruct((devices, count, 2 * FF + deep * D), BF),),
                    feed_gradients,
                ),
            )
            feed_local = feed_local.reshape(D, -1)
        else:
            row_cross_branch = gather_seq(cross_branch, n, rows, 5)
            contract_local = outer(hidden, feed_branch).astype(BF).reshape(devices, -1, D)
            contract_local = jnp.pad(contract_local, ((0, 0), (0, spare), (0, 0)))
            feed_local = jnp.concatenate(
                [outer(feed_norm, grad_pair).astype(BF)]
                + [contract_local[:, g * count : (g + 1) * count].reshape(D, D) for g in range(deep)],
                1,
            )
        feed_sum = lax.psum_scatter(feed_local, both, scatter_dimension=0, tiled=True).astype(F32)
        cross_grad = dot_back(row_cross_branch, own_rows(cross_out_weight)).astype(BF)
        expand_sum = feed_sum[:, 0 : 2 * FF].reshape(count, 2, FF)
        contract_sum = jnp.concatenate(
            [feed_sum[:, 2 * FF + g * D : 2 * FF + (g + 1) * D] for g in range(deep)], 0
        )[: deep * count - spare]
        matched = wide == D and wd == rows * count
        cross_out_local = outer(cross_heads, row_cross_branch).astype(BF)
        cross_plans = [("rows", cross_out_local.reshape(rows, count, D))] if matched else []
        cross_qparts, cross_home, cross_qgrad, *cross_grads = cross_bwd(
            cross_query, cross_pair, cross_grad, cross_exact, cross_lse, query_side, cross_side, cross_plans, n, rows
        )
        cross_rows, cross_grads = cross_grads[: len(cross_plans)], cross_grads[len(cross_plans) :]
        grad_cross_query = side_by_side(cross_qparts)[:, :D]
        unused_norm, norm_back = jax.vjp(normalize, after_self, norm_gain[1])
        cross_part, cross_gain = norm_back(dot_back(grad_cross_query, cross_query_weight[:, :D]))
        grad_after_self = grad_after_cross + cross_part
        self_branch = grad_after_self.astype(BF)
        def cross_gradients(ins, outs):
            norm_ref, query_ref = ins[:2]
            (o_ref,) = outs
            o_ref[:, 0:wd] = tn(norm_ref[...], query_ref[...]).astype(BF)
            pair = tn(ins[2][...], ins[2 + n][...])
            for p in range(1, n):
                pair = pair + tn(ins[2 + p][...], ins[2 + n + p][...])
            o_ref[:, wd : 3 * wd] = pair.astype(BF)

        row_self_branch, cross_local = gather_seq(
            self_branch, n, rows, 6,
            job=Job(
                (row_cross_norm, cross_qgrad.reshape(-1, wd))
                + tuple(encoder_blocks) + tuple(cross_grads),
                (jax.ShapeDtypeStruct((D, 3 * wd), BF),),
                cross_gradients,
            ),
        )
        self_grad = dot_back(row_self_branch, own_rows(self_out_weight)).astype(BF)
        self_out_local = outer(self_heads, row_self_branch).astype(BF)
        rows_local = (self_out_local, cross_out_local)
        self_grads, pair_bias, cross_parts = self_bwd(
            self_proj, self_grad, self_exact, self_lse, bias_forward, query_side, self_side,
            [("all", cross_local.reshape(devices, count, 3 * wd))], n, rows,
        )
        rows_plans = [("rows", self_out_local.reshape(rows, count, D))] if matched else []
        grad_bias = pair_bias[:, 128:]
        table_own_grad = jnp.einsum("hd,db->bh", grad_bias, onehot, precision=HIGHEST)
        table_local = lax.dynamic_update_slice_in_dim(
            jnp.zeros((BUCKETS, n * hpd), F32), table_own_grad, shard * hpd, 1
        )[:, :HEADS]
        self_back = dot_back(self_grads, first_columns).astype(BF)
        def encoder_job(ins, outs):
            home_ref, weight_ref, hidden_ref, down_ref, stream_ref = ins
            total = None
            for t in range(n):
                for h in range(hpd):
                    low = (t * hpd + h) * 2 * HD
                    part = nt(home_ref[t, h], weight_ref[:, low : low + 2 * HD])
                    total = part if total is None else total + part
            outs[0][...] = total
            outs[1][...] = (stream_ref[...] + nn(hidden_ref[...], down_ref[...])).astype(BF)

        self_back_parts, self_parts, *rest = exchange(
            [
                ("seq", self_back.reshape(n, -1, D)),
                ("all", outer(row_norm, self_grads).astype(BF).reshape(devices, count, 3 * wd)),
            ] + rows_plans,
            n, rows, 7,
            job=Job(
                (cross_home, cross_pair_weight, hidden, contract_full, after_cross),
                (
                    jax.ShapeDtypeStruct(encoder_output.shape[1:], F32),
                    jax.ShapeDtypeStruct(decoder_input.shape[1:], BF),
                ),
                encoder_job,
            ),
        )
        *rows_parts, encoder_gradient, layer_output = rest
        rows_parts += cross_rows
        if not matched:
            padded = lax.dynamic_update_slice_in_dim(
                jnp.zeros((wide, 2 * D), BF), jnp.concatenate(rows_local, 1), shard * wd, 0
            )[:D]
            whole = lax.psum_scatter(padded, both, scatter_dimension=0, tiled=True)[None]
            rows_parts = [whole[:, :, :D], whole[:, :, D:]]
        unused_norm, norm_back = jax.vjp(normalize, inputs, norm_gain[0])
        self_part, self_gain = norm_back(jnp.sum(self_back_parts.astype(F32), 0))
        input_gradient = grad_after_self + self_part

        attention_parts, attention_columns, attention_means = sum_parts(
            self_parts, cross_parts, *rows_parts, n, wd
        )
        attention_sum = jnp.moveaxis(attention_parts, 0, 1)
        attention_rows = BETA_TWO * attention_rowwise + (1.0 - BETA_TWO) * attention_means[:, 0:8].T
        expand_rows, expand_columns = factored_start(expand_sum, expand_rowwise)
        contract_rows, contract_columns = factored_start(
            contract_sum[:, None, :], contract_rowwise[None, :]
        )
        gain_local = jnp.stack((self_gain, cross_gain, feed_gain), 0)
        attention_total, expand_total, contract_total, row_totals, gain_gradient, table_gradient = (
            sum_everywhere(
                (
                    attention_columns,
                    expand_columns,
                    contract_columns,
                    attention_rows,
                    expand_rows,
                    contract_rows,
                    gain_local,
                    table_local,
                ),
                n, rows,
            )
        )
        attention_rowtotal, expand_rowtotal, contract_rowtotal = (
            row_totals[:, 0],
            row_totals[:2, 1],
            row_totals[:1, 2],
        )
        attention_new = factored_finish(
            attention_sum,
            attention_moment,
            attention_rows,
            attention_colwise,
            attention_weight,
            attention_total,
            attention_rowtotal,
            D,
        )
        expand_new = factored_finish(
            expand_sum,
            expand_moment,
            expand_rows,
            expand_colwise,
            expand_weight,
            expand_total,
            expand_rowtotal,
            D,
        )
        contract_new = factored_finish(
            contract_sum[:, None, :],
            contract_moment[:, None, :],
            contract_rows,
            contract_colwise[None, :],
            contract_weight[:, None, :],
            contract_total,
            contract_rowtotal,
            FF,
        )
        gain_new = adaptive(gain_gradient, gain_moment, gain_second, norm_gain)
        table_new = adaptive(table_gradient, table_moment, table_second, relative_table)
        return (
            layer_output[None],
            input_gradient[None],
            encoder_gradient[None],
            attention_sum,
            attention_new[0],
            attention_rows,
            attention_new[1],
            attention_new[2],
            expand_sum,
            expand_new[0],
            expand_rows,
            expand_new[1],
            expand_new[2],
            contract_sum,
            contract_new[0][:, 0],
            contract_rows[0],
            contract_new[1][0],
            contract_new[2][:, 0],
            gain_gradient,
            gain_new[0],
            gain_new[1],
            gain_new[2],
            table_gradient,
            table_new[0],
            table_new[1],
            table_new[2],
        )

    return shards


def solution(mesh):
    placed = (
        P("rows", "seq", None),
        P("rows", "seq", None),
        P("rows", "seq", None),
        P("rows", None),
        P("rows", None),
        P("rows", None),
        P("rows", None),
        P(),
        P(("rows", "seq"), None, None),
        P(("rows", "seq"), None, None),
        P(None, ("rows", "seq")),
        P(),
        P(("rows", "seq"), None, None),
        P(("rows", "seq"), None, None),
        P(None, ("rows", "seq")),
        P(),
        P(("rows", "seq"), None),
        P(("rows", "seq"), None),
        P(("rows", "seq")),
        P(),
        P(),
        P(),
        P(),
        P(),
        P(),
        P(),
    )
    return jax.shard_map(
        make_shards(mesh.shape["seq"], mesh.shape["rows"]),
        mesh=mesh,
        in_specs=placed,
        out_specs=(
            P("rows", "seq", None),
            P("rows", "seq", None),
            P("rows", "seq", None),
            P(("rows", "seq"), None, None),
            P(("rows", "seq"), None, None),
            P(None, ("rows", "seq")),
            P(),
            P(("rows", "seq"), None, None),
            P(("rows", "seq"), None, None),
            P(("rows", "seq"), None, None),
            P(None, ("rows", "seq")),
            P(),
            P(("rows", "seq"), None, None),
            P(("rows", "seq"), None),
            P(("rows", "seq"), None),
            P(("rows", "seq")),
            P(),
            P(("rows", "seq"), None),
            P(),
            P(),
            P(),
            P(),
            P(),
            P(),
            P(),
            P(),
        ),
        check_vma=False,
    )
```

```python
import jax
import jax.numpy as jnp
from jax import lax
from jax.experimental import pallas as pl
from jax.experimental.pallas import tpu as pltpu
from jax.sharding import PartitionSpec as P

D = 768
FF = 2048
HEADS = 12
BUCKETS = 32
STEP = 10
HIGHEST = lax.Precision.HIGHEST
NORM_EPS = 1e-06
BETA_ONE = 0.9
BETA_TWO = 0.999
ADAM_EPS = 1e-08
WEIGHT_DECAY = 0.01
MATRIX_RATE = 0.15
VECTOR_RATE = 1.0
HD = 64
NEG = -1e30
F32 = jnp.float32
BF = jnp.bfloat16

def nt(a,b): return lax.dot_general(a,b,(((1,),(1,)),((),())),preferred_element_type=F32)
def nn(a,b): return lax.dot_general(a,b,(((1,),(0,)),((),())),preferred_element_type=F32)
def tn(a,b): return lax.dot_general(a,b,(((0,),(0,)),((),())),preferred_element_type=F32)

def cross_fwd(q,kv,qa,ka,qb=352,kc=1024):
    Lq,W=q.shape; Lk=kv.shape[0]; H=W//HD
    nk=Lk//kc
    def kern(q_ref,kv_ref,qa_ref,ka_ref,o_ref,of_ref,lse_ref,kaug,vs,s_s,m_s,l_s,acc):
        @pl.when(pl.program_id(0)==0)
        def _():
            for h in range(H):
                kaug[h,:,0:HD]=kv_ref[:,2*h*HD:(2*h+1)*HD]
                kaug[h,:,HD:2*HD]=ka_ref[...]
                vs[h]=kv_ref[:,(2*h+1)*HD:(2*h+2)*HD]
        lane=lax.broadcasted_iota(jnp.int32,(qb,128),1)
        lses=jnp.zeros((qb,128),F32)
        outs=[]
        for h in range(H):
            qh=(q_ref[:,h*HD:(h+1)*HD]*BF(0.125)).astype(BF)
            qg=jnp.concatenate([qh,qa_ref[...]],axis=1)
            m_s[...]=jnp.full((qb,128),-3e38,F32)
            for c in range(nk):
                s=nt(qg,kaug[h,c*kc:(c+1)*kc,:])
                s_s[:,c*kc:(c+1)*kc]=s
                mm=m_s[...]
                for t in range(kc//128): mm=jnp.maximum(mm,s[:,t*128:(t+1)*128])
                m_s[...]=mm
            m=jnp.max(m_s[...],axis=1,keepdims=True)
            l_s[...]=jnp.zeros((qb,128),F32)
            acc[...]=jnp.zeros((qb,HD),F32)
            for c in range(nk):
                p=jnp.exp(s_s[:,c*kc:(c+1)*kc]-m)
                ll=l_s[...]
                for t in range(kc//128): ll=ll+p[:,t*128:(t+1)*128]
                l_s[...]=ll
                acc[...]+=nn(p.astype(BF),vs[h,c*kc:(c+1)*kc,:])
            l=jnp.sum(l_s[...],axis=1,keepdims=True)
            o=acc[...]/l
            outs.append(o)
            lses=jnp.where(lane==h,m+jnp.log(l),lses)
        oo=jnp.concatenate(outs,axis=1)
        o_ref[...]=oo.astype(BF)
        of_ref[...]=oo
        lse_ref[...]=lses
    full=lambda s: pl.BlockSpec(s,lambda i:(0,)*len(s))
    row=lambda w: pl.BlockSpec((qb,w),lambda i:(i,0))
    return pl.pallas_call(kern,grid=(Lq//qb,),
        out_shape=(jax.ShapeDtypeStruct((Lq,W),BF),jax.ShapeDtypeStruct((Lq,W),F32),jax.ShapeDtypeStruct((Lq,128),F32)),
        in_specs=[row(W),full((Lk,2*W)),row(HD),full((Lk,HD))],
        out_specs=(row(W),row(W),row(128)),
        scratch_shapes=[pltpu.VMEM((H,Lk,2*HD),BF),pltpu.VMEM((H,Lk,HD),BF),pltpu.VMEM((qb,Lk),F32),pltpu.VMEM((qb,128),F32),pltpu.VMEM((qb,128),F32),pltpu.VMEM((qb,HD),F32)],
        compiler_params=pltpu.CompilerParams(vmem_limit_bytes=56*2**20),cost_estimate=cost(31.0),name="cross_fwd")(q,kv,qa,ka)

def split3(x):
    a=x.astype(BF); r=x-a.astype(F32)
    b=r.astype(BF); c=(r-b.astype(F32)).astype(BF)
    return a,b,c

def cross_bwd(q,kv,do,of,lse,qa,ka,plans,n,rows,qb=256):
    Lq,W=q.shape; Lk=kv.shape[0]; H=W//HD; kc=Lk//n
    ride=Exchange(plans,n,rows); riders=ride.scratch if plans else []
    def kern(q_ref,kv_ref,do_ref,of_ref,lse_ref,qa_ref,ka_ref,*rest):
        sent,rest=rest[:ride.count],rest[ride.count:]
        dq_ref,home_ref,dqw=rest[:3]
        got,rest=rest[3:3+ride.count],rest[3+ride.count:]
        rest,sems=rest[:len(rest)-len(riders)],rest[len(rest)-len(riders):]
        dkv_refs=rest[:n]
        kaug,vaug,qaug,doaug,ps,dss,dqacc,kt,dqs,dkvs,q_out,q_in,kv_out,kv_in,own=rest[n:]
        h=pl.program_id(0); c=pl.program_id(1)
        r,s=lax.axis_index("rows"),lax.axis_index("seq")
        def home(p):
            return pltpu.make_async_remote_copy(src_ref=dkvs.at[h,p*kc:(p+1)*kc],dst_ref=home_ref.at[s,h],send_sem=kv_out.at[p,h],
                recv_sem=kv_in.at[p,h],device_id=(r,s^p),device_id_type=MESH)
        def keep():
            return pltpu.make_async_copy(dkvs.at[h,0:kc],home_ref.at[s,h],own.at[h])
        def turn(p):
            return pltpu.make_async_remote_copy(src_ref=dqw.at[s^p],dst_ref=dq_ref.at[s],send_sem=q_out.at[p],
                recv_sem=q_in.at[p],device_id=(r,s^p),device_id_type=MESH)
        def stay():
            return pltpu.make_async_copy(dqw.at[s],dq_ref.at[s],own.at[H])
        @pl.when((h==0)&(c==0))
        def _():
            greet_all(n*rows if plans else n,n)
            if plans: ride.start(sent,got,sems,greet=False)
        for hh in range(H):
            @pl.when((h==hh)&(c==0))
            def _():
                sl=slice(hh*HD,(hh+1)*HD)
                kaug[:,0:HD]=kv_ref[:,2*hh*HD:(2*hh+1)*HD]
                lane=lax.broadcasted_iota(jnp.int32,(Lk,HD),1)
                kaug[:,HD:2*HD]=jnp.where((lane>=3)&(lane<6),BF(1),ka_ref[...])
                vaug[:,0:HD]=kv_ref[:,(2*hh+1)*HD:(2*hh+2)*HD]
                vaug[:,HD:2*HD]=jnp.where(lane<3,BF(1),BF(0)).astype(BF)
                lq=lax.broadcasted_iota(jnp.int32,(Lq,HD),1)
                x,y,z=split3(-lse_ref[:,hh:hh+1])
                qaug[0:Lq,0:HD]=q_ref[:,sl]*BF(0.125)
                qaug[0:Lq,HD:2*HD]=jnp.where(lq==3,x,jnp.where(lq==4,y,jnp.where(lq==5,z,qa_ref[...])))
                dd=do_ref[:,sl]
                delta=jnp.sum(dd.astype(F32)*of_ref[:,sl],axis=1,keepdims=True)
                x,y,z=split3(-delta)
                doaug[0:Lq,0:HD]=dd
                doaug[0:Lq,HD:2*HD]=jnp.where(lq==0,x,jnp.where(lq==1,y,jnp.where(lq==2,z,BF(0))))
                dqacc[...]=jnp.zeros_like(dqacc)
                for b in range(n):
                    kt[b]=kv_ref[b*kc:(b+1)*kc,2*hh*HD:(2*hh+1)*HD].astype(F32).T.astype(BF)
        off=pl.multiple_of((n-1-c)*kc,kc)
        kk=kaug[pl.ds(off,kc),:]
        vv=vaug[pl.ds(off,kc),:]
        for i in range(0,Lq,qb):
            part=slice(i,min(i+qb,Lq))
            p=jnp.exp(nt(kk,qaug[part,:]))
            g=nt(vv,doaug[part,:])
            ps[:,part]=p.astype(BF)
            dss[:,part]=(p*g).astype(BF)
        dkvs[h,pl.ds(off,kc),0:HD]=nn(dss[...],qaug[:,0:HD]).astype(BF)
        dkvs[h,pl.ds(off,kc),HD:2*HD]=nn(ps[...],doaug[:,0:HD]).astype(BF)
        dqacc[...]+=nn(kt[n-1-c],dss[...])
        for p in range(1,n):
            @pl.when(c==n-1-p)
            def _():
                home(p).start()
        @pl.when(c==n-1)
        def _():
            keep().start()
            dqs[h]=(dqacc[...].T*0.125).astype(BF)
        @pl.when((c==n-1)&(h==H-1))
        def _():
            for b in range(n):
                dqw[b]=jnp.concatenate([dqs[t,b*(Lq//n):(b+1)*(Lq//n),:] for t in range(H)],axis=1)
            for p in range(1,n): turn(p).start()
            stay().start()
            for b,dkv_ref in enumerate(dkv_refs):
                for t in range(H): dkv_ref[:,2*t*HD:2*(t+1)*HD]=dkvs[t,b*kc:(b+1)*kc,:]
            for p in range(1,n): turn(p).wait()
            stay().wait()
            if plans: ride.wait(sent,got,sems)
        @pl.when(c==n-1)
        def _():
            for p in range(1,n): home(p).wait()
            keep().wait()
    full=lambda s: pl.BlockSpec(s,lambda h,c:(0,)*len(s))
    return pl.pallas_call(kern,grid=(H,n),
        out_shape=(jax.ShapeDtypeStruct((n,Lq//n,W),BF),jax.ShapeDtypeStruct((n,H,kc,2*HD),BF),jax.ShapeDtypeStruct((n,Lq//n,W),BF))+ride.shapes+(jax.ShapeDtypeStruct((kc,2*W),BF),)*n,
        in_specs=[full((Lq,W)),full((Lk,2*W)),full((Lq,W)),full((Lq,W)),full((Lq,128)),full((Lq,HD)),full((Lk,HD))]+[ANY]*ride.count,
        out_specs=(ANY,ANY,full((n,Lq//n,W)))+(ANY,)*ride.count+(full((kc,2*W)),)*n,
        scratch_shapes=[pltpu.VMEM((Lk,2*HD),BF),pltpu.VMEM((Lk,2*HD),BF),pltpu.VMEM((Lq,2*HD),BF),pltpu.VMEM((Lq,2*HD),BF),
            pltpu.VMEM((kc,Lq),BF),pltpu.VMEM((kc,Lq),BF),pltpu.VMEM((HD,Lq),F32),pltpu.VMEM((n,HD,kc),BF),pltpu.VMEM((H,Lq,HD),BF),pltpu.VMEM((H,Lk,2*HD),BF)]
            +[pltpu.SemaphoreType.DMA((n,))]*2+[pltpu.SemaphoreType.DMA((n,H))]*2+[pltpu.SemaphoreType.DMA((H+1,))]+riders,
        compiler_params=pltpu.CompilerParams(vmem_limit_bytes=60*2**20,collective_id=10,has_side_effects=True),cost_estimate=cost(68.0),name="cross_bwd")(q,kv,do,of,lse,qa,ka,*[x for kind,x in plans])

def toeplitz(line, shift):
    return pltpu.roll(jnp.broadcast_to(line,(128,line.shape[1])),shift,1,stride=1,stride_axis=0)

def toeplitz_rows(x):
    return pltpu.roll(x,1,1,stride=1,stride_axis=0)

def eye128():
    return lax.broadcasted_iota(jnp.int32,(128,128),0)==lax.broadcasted_iota(jnp.int32,(128,128),1)

def self_fwd(qkv,rev,qa,ka):
    Lq,W=qkv.shape[0],qkv.shape[1]//3; H=W//HD; nb=Lq//128
    def kern(qkv_ref,rev_ref,qa_ref,ka_ref,o_ref,of_ref,lse_ref,qaug,kaug,kdiag,vs,os,tz):
        h=pl.program_id(0)
        for hh in range(H):
            @pl.when(h==hh)
            def _():
                sl=slice(hh*HD,(hh+1)*HD)
                qaug[:,0:HD]=qkv_ref[:,sl]*BF(0.125); qaug[:,HD:]=qa_ref[...]
                kaug[:,0:HD]=qkv_ref[:,W+hh*HD:W+(hh+1)*HD]; kaug[:,HD:]=ka_ref[...]
                kdiag[:,0:HD]=qkv_ref[:,W+hh*HD:W+(hh+1)*HD]; kdiag[:,HD:]=jnp.zeros((Lq,HD),BF)
                vs[...]=qkv_ref[:,2*W+hh*HD:2*W+(hh+1)*HD]
        @pl.when(h==0)
        def _():
            lse_ref[...]=jnp.zeros((Lq,128),F32)
        bands=toeplitz(rev_ref[pl.ds(h,1),:],(nb+1)*128-127)
        for d in range(nb):
            tz[d]=bands[:,(nb-1-d)*128:(nb-d)*128]
        eye=eye128()
        lane=lax.broadcasted_iota(jnp.int32,(128,128),1)
        for q0 in range(0,Lq,256):
            qn=min(256,Lq-q0); kend=q0+qn
            s=nt(qaug[q0:q0+qn,:],kaug[0:kend,:])
            for a in range(qn//128):
                qt=q0//128+a
                r0=q0+a*128
                rows=slice(r0,r0+128)
                sd=nt(qaug[rows,:],kdiag[rows,:])
                tiles=[]
                for b in range(qt+1):
                    t=s[a*128:(a+1)*128,b*128:(b+1)*128]
                    if b==qt: t=jnp.where(eye,sd,t)
                    tiles.append(t+tz[qt-b])
                m=tiles[0]
                for t in tiles[1:]: m=jnp.maximum(m,t)
                m=jnp.max(m,axis=1,keepdims=True)
                ps=[jnp.exp(t-m) for t in tiles]
                l=ps[0]
                for t in ps[1:]: l=l+t
                l=jnp.sum(l,axis=1,keepdims=True)
                pb=jnp.concatenate([t.astype(BF) for t in ps],axis=1)
                os[h,rows,:]=nn(pb,vs[0:(qt+1)*128,:])/l
                lse_ref[rows,:]=jnp.where(lane==h,m+jnp.log(l),lse_ref[rows,:])
        @pl.when(h==H-1)
        def _():
            oo=jnp.concatenate([os[t] for t in range(H)],axis=1)
            o_ref[...]=oo.astype(BF)
            of_ref[...]=oo
    full=lambda s: pl.BlockSpec(s,lambda h:(0,)*len(s))
    return pl.pallas_call(kern,grid=(H,),
        out_shape=(jax.ShapeDtypeStruct((Lq,W),BF),jax.ShapeDtypeStruct((Lq,W),F32),jax.ShapeDtypeStruct((Lq,128),F32)),
        in_specs=[full((Lq,3*W)),full(rev.shape),full((Lq,HD)),full((Lq,HD))],
        out_specs=(full((Lq,W)),full((Lq,W)),full((Lq,128))),
        scratch_shapes=[pltpu.VMEM((Lq,2*HD),BF)]*3+[pltpu.VMEM((Lq,HD),BF),pltpu.VMEM((H,Lq,HD),F32),pltpu.VMEM((nb,128,128),F32)],
        compiler_params=pltpu.CompilerParams(vmem_limit_bytes=48*2**20),cost_estimate=cost(15.0),name="self_fwd")(qkv,rev,qa,ka)

MESH = pl.DeviceIdType.MESH
ANY = pl.BlockSpec(memory_space=pl.ANY)
VM = pl.BlockSpec(memory_space=pltpu.VMEM)


def cost(micros):
    return pl.CostEstimate(flops=int(micros * 1.0e9), bytes_accessed=int(micros * 3.0e6), transcendentals=0)


def greet_all(count, n):
    r, s = lax.axis_index("rows"), lax.axis_index("seq")
    barrier = pltpu.get_barrier_semaphore()

    def greet(step, carry):
        j = lax.rem((s if count == n else r * n + s) + step, count)
        device = (r, j) if count == n else (lax.div(j, n), lax.rem(j, n))
        pl.semaphore_signal(barrier, inc=1, device_id=device, device_id_type=MESH)
        return carry

    lax.fori_loop(1, count, greet, 0)
    pl.semaphore_wait(barrier, count - 1)


class Exchange:
    def __init__(self, plans, n, rows):
        self.kinds = [kind for kind, x in plans]
        self.count = len(plans)
        self.n, self.rows = n, rows
        shapes = [(n * rows,) + x.shape[1:] if kind == "own" else x.shape for kind, x in plans]
        self.shapes = tuple(jax.ShapeDtypeStruct(shape, x.dtype) for shape, (kind, x) in zip(shapes, plans))
        self.scratch = [pltpu.SemaphoreType.DMA((shape[0],)) for shape in shapes for side in range(2)]
        self.scratch += [pltpu.SemaphoreType.DMA((self.count,))]

    def each(self, sent, got, sems, act):
        n, rows = self.n, self.rows
        r, s = lax.axis_index("rows"), lax.axis_index("seq")
        me = r * n + s
        for p, kind in enumerate(self.kinds):
            x, y, out_sem, in_sem, own = sent[p], got[p], sems[2 * p], sems[2 * p + 1], sems[-1].at[p]

            def remote(block, slot, device, leave, arrive, x=x, y=y, out_sem=out_sem, in_sem=in_sem):
                return pltpu.make_async_remote_copy(
                    src_ref=x.at[block], dst_ref=y.at[slot], send_sem=out_sem.at[leave], recv_sem=in_sem.at[arrive],
                    device_id=device, device_id_type=MESH,
                )

            if kind == "rows":
                def send(j, carry, act=act, x=x, y=y, own=own, remote=remote):
                    target = s * rows + j
                    away = remote(j, r, (lax.div(target, n), lax.rem(target, n)), j, r)

                    @pl.when(target != me)
                    def _():
                        act(away, True)

                    @pl.when(target == me)
                    def _():
                        act(pltpu.make_async_copy(x.at[j], y.at[r], own), None)

                    return carry

                def take(q, carry, act=act, remote=remote):
                    @pl.when((q != r) | (lax.div(me, rows) != s))
                    def _():
                        act(remote(0, q, (r, s), 0, q), False)

                    return carry

                lax.fori_loop(0, rows, send, 0)
                lax.fori_loop(0, rows, take, 0)
                continue
            if kind == "xor":
                act(pltpu.make_async_copy(x.at[0], y.at[s], own), None)
                for p in range(1, n):
                    away = remote(p, s, (r, s ^ p), p, p)
                    act(away, True)
                    act(away, False)
                continue
            length, here = (n, s) if kind == "seq" else (n * rows, me)
            act(pltpu.make_async_copy(x.at[s if kind == "own" else here], y.at[here], own), None)

            def both_ways(step, carry, act=act, length=length, here=here, kind=kind, remote=remote):
                j = lax.rem(here + step, length)
                device = (r, j) if kind == "seq" else (lax.div(j, n), lax.rem(j, n))
                away = remote(lax.rem(j, n) if kind == "own" else j, here, device, step, step)
                act(away, True)
                act(away, False)
                return carry

            lax.fori_loop(1, length, both_ways, 0)

    def start(self, sent, got, sems, greet=True):
        near = all(kind == "seq" for kind in self.kinds)
        if greet:
            greet_all(self.n if near else self.n * self.rows, self.n)
        self.each(sent, got, sems, lambda copy, away: copy.start() if away is not False else None)

    def wait(self, sent, got, sems):
        def act(copy, away):
            if away is None:
                copy.wait()
            elif away:
                copy.wait_send()
            else:
                copy.wait_recv()

        self.each(sent, got, sems, act)


class Job:
    def __init__(self, inputs=(), outs=(), body=None):
        inputs = [x if isinstance(x, tuple) else (x, None) for x in inputs]
        self.inputs, self.columns = [x for x, part in inputs], [part for x, part in inputs]
        self.outs, self.body = tuple(outs), body
        self.scratch = [
            pltpu.VMEM(x.shape if part is None else (x.shape[0], part[1] - part[0]), x.dtype) for x, part in inputs
        ]
        self.scratch += [pltpu.SemaphoreType.DMA((len(self.inputs),))] if self.inputs else []

    def split(self, refs, before, between, after):
        i, o = len(self.inputs), len(self.outs)
        head, refs = refs[:before], refs[before:]
        ins, refs = refs[:i], refs[i:]
        middle, refs = refs[:between], refs[between:]
        outs, refs = refs[:o], refs[o:]
        return head + middle + refs[:after], ins, outs, refs[after:]

    def run(self, ins, outs, scratch):
        if not self.inputs:
            return
        held, sem = scratch[:-1], scratch[-1]
        copies = [
            pltpu.make_async_copy(x if part is None else x.at[:, part[0] : part[1]], y, sem.at[k])
            for k, (x, y, part) in enumerate(zip(ins, held, self.columns))
        ]
        for copy in copies:
            copy.start()
        for copy in copies:
            copy.wait()
        self.body(held, outs)


def exchange(plans, n, rows, collective_id, job=None):
    ride, job = Exchange(plans, n, rows), job or Job()

    def kern(*refs):
        refs, ins, outs, scratch = job.split(refs, ride.count, ride.count, len(ride.scratch))
        sent, got, sems = refs[: ride.count], refs[ride.count : 2 * ride.count], refs[2 * ride.count :]
        ride.start(sent, got, sems)
        job.run(ins, outs, scratch)
        ride.wait(sent, got, sems)

    return pl.pallas_call(
        kern,
        out_shape=ride.shapes + job.outs,
        in_specs=[ANY] * (ride.count + len(job.inputs)),
        out_specs=(ANY,) * ride.count + (VM,) * len(job.outs),
        scratch_shapes=ride.scratch + job.scratch,
        compiler_params=pltpu.CompilerParams(
            collective_id=collective_id, has_side_effects=True, vmem_limit_bytes=56 * 2**20
        ),
        cost_estimate=cost(20.0),name="exchange",
    )(*[x for kind, x in plans], *job.inputs)


def reduce_exchange(partial, plans, n, rows, collective_id, job):
    ride = Exchange(plans, n, rows)
    half, length, features = n // 2, partial.shape[1], partial.shape[2]

    def kern(*refs):
        refs, ins, outs, scratch = job.split(refs, 1 + ride.count, 1 + ride.count, 7 + len(ride.scratch))
        x_ref, sent, o_ref = refs[0], refs[1 : 1 + ride.count], refs[1 + ride.count]
        got, rest = refs[2 + ride.count : 2 + 2 * ride.count], refs[2 + 2 * ride.count :]
        near, far, send, near_out, near_in, far_out, far_in = rest[:7]
        sems = rest[7:]
        r, s = lax.axis_index("rows"), lax.axis_index("seq")
        chip, parity = lax.div(s, 2), lax.rem(s, 2)
        beside = s + 1 - 2 * parity
        greet_all(n * rows, n)

        def to_side(q):
            return pltpu.make_async_remote_copy(
                src_ref=x_ref.at[2 * q + 1 - parity], dst_ref=near.at[q], send_sem=near_out.at[q],
                recv_sem=near_in.at[q], device_id=(r, beside), device_id_type=MESH,
            )

        def to_chip(k):
            q = lax.rem(chip + k, half)
            return pltpu.make_async_remote_copy(
                src_ref=send.at[k], dst_ref=far.at[k], send_sem=far_out.at[k],
                recv_sem=far_in.at[k], device_id=(r, 2 * q + parity), device_id_type=MESH,
            )

        for q in range(half):
            to_side(q).start()
        ride.start(sent, got, sems, greet=False)
        for q in range(half):
            to_side(q).wait()

        def pair(k):
            q = lax.rem(chip + k, half)
            return x_ref[2 * q + parity].astype(F32) + near[q].astype(F32)

        for k in range(1, half):
            send[k] = pair(k).astype(BF)
            to_chip(k).start()
        o_ref[...] = pair(0)
        job.run(ins, outs, scratch)
        for k in range(1, half):
            to_chip(k).wait()
            o_ref[...] += far[k].astype(F32)
        ride.wait(sent, got, sems)

    block = pltpu.VMEM((half, length, features), BF)
    return pl.pallas_call(
        kern,
        out_shape=(jax.ShapeDtypeStruct((length, features), F32),) + ride.shapes + job.outs,
        in_specs=[VM] + [ANY] * (ride.count + len(job.inputs)),
        out_specs=(VM,) + (ANY,) * ride.count + (VM,) * len(job.outs),
        scratch_shapes=[block] * 3 + [pltpu.SemaphoreType.DMA((half,))] * 4 + ride.scratch + job.scratch,
        compiler_params=pltpu.CompilerParams(
            collective_id=collective_id, has_side_effects=True, vmem_limit_bytes=58 * 2**20
        ),
        cost_estimate=cost(40.0),
        name="reduce_exchange",
    )(partial, *[x for kind, x in plans], *job.inputs)


def gather_seq(values, n, rows, collective_id, plans=(), job=None):
    ride, job = Exchange(plans, n, rows), job or Job()
    sems_used = ride.scratch if ride.count else []

    def kern(*refs):
        refs, ins, outs, scratch = job.split(refs, 1 + ride.count, 1 + ride.count, 5 + len(sems_used))
        x_ref, sent, o_ref = refs[0], refs[1 : 1 + ride.count], refs[1 + ride.count]
        got, rest = refs[2 + ride.count : 2 + 2 * ride.count], refs[2 + 2 * ride.count :]
        own, out_sem, in_sem, side_out, side_in = rest[:5]
        sems = rest[5:]
        r, s = lax.axis_index("rows"), lax.axis_index("seq")
        beside = s + 1 - 2 * lax.rem(s, 2)
        if ride.count:
            greet_all(n * rows, n)
        else:
            barrier = pltpu.get_barrier_semaphore()
            for step in range(2, n, 2):
                pl.semaphore_signal(barrier, inc=1, device_id=(r, lax.rem(s + step, n)), device_id_type=MESH)
            pl.semaphore_signal(barrier, inc=1, device_id=(r, beside), device_id_type=MESH)
            pl.semaphore_wait(barrier, n // 2)
        far = [
            pltpu.make_async_remote_copy(
                src_ref=x_ref, dst_ref=o_ref.at[s], send_sem=out_sem.at[k], recv_sem=in_sem.at[k],
                device_id=(r, lax.rem(s + 2 * k, n)), device_id_type=MESH,
            )
            for k in range(1, n // 2)
        ]
        for copy in far:
            copy.start()

        def across(k):
            slot = lax.rem(s + n - 2 * k, n)
            return pltpu.make_async_remote_copy(
                src_ref=x_ref if k == 0 else o_ref.at[slot], dst_ref=o_ref.at[slot],
                send_sem=side_out.at[k], recv_sem=side_in.at[k], device_id=(r, beside), device_id_type=MESH,
            )

        near = [across(k) for k in range(n // 2)]
        near[0].start()
        local = pltpu.make_async_copy(x_ref, o_ref.at[s], own)
        local.start()
        if ride.count:
            ride.start(sent, got, sems, greet=False)
        for k, copy in enumerate(far):
            job.run(ins, outs, scratch) if k == 0 else None
            copy.wait_recv()
            near[k + 1].start()
        for copy in near:
            copy.wait()
        for copy in far:
            copy.wait_send()
        local.wait()
        if ride.count:
            ride.wait(sent, got, sems)

    length, features = values.shape
    whole, *got = pl.pallas_call(
        kern,
        out_shape=(jax.ShapeDtypeStruct((n, length, features), values.dtype),) + ride.shapes + job.outs,
        in_specs=[ANY] * (1 + ride.count + len(job.inputs)),
        out_specs=(ANY,) * (1 + ride.count) + (VM,) * len(job.outs),
        scratch_shapes=[pltpu.SemaphoreType.DMA] + [pltpu.SemaphoreType.DMA((n // 2,))] * 4
        + sems_used + job.scratch,
        compiler_params=pltpu.CompilerParams(
            collective_id=collective_id, has_side_effects=True, vmem_limit_bytes=56 * 2**20
        ),
        cost_estimate=cost(20.0),
        name="gather_seq",
    )(values, *[x for kind, x in plans], *job.inputs)
    whole = whole.reshape(n * length, features)
    return (whole, *got) if got else whole


def project_blocks(blocks, weight):
    length, width = blocks[0].shape[0], weight.shape[1]
    count = len(blocks)

    def kern(*refs):
        weight_ref, o_ref = refs[count], refs[count + 1]
        for k in range(count):
            o_ref[k * length : (k + 1) * length, :] = nn(refs[k][...], weight_ref[...]).astype(BF)

    return pl.pallas_call(
        kern,
        out_shape=jax.ShapeDtypeStruct((count * length, width), BF),
        in_specs=[VM] * (count + 1),
        out_specs=VM,
        compiler_params=pltpu.CompilerParams(vmem_limit_bytes=40 * 2**20),
        cost_estimate=cost(8.0),
        name="project_blocks",
    )(*blocks, weight)


def self_bwd(qkv,do,of,lse,fwd,qa,ka,plans,n,rows):
    Lq,W=qkv.shape[0],qkv.shape[1]//3; H=W//HD; nb=Lq//128
    ride=Exchange(plans,n,rows)
    def kern(qkv_ref,do_ref,of_ref,lse_ref,fwd_ref,qa_ref,ka_ref,*rest):
        sent,rest=rest[:ride.count],rest[ride.count:]
        grad_ref,gb_ref=rest[:2]
        got,rest=rest[2:2+ride.count],rest[2+ride.count:]
        (qaug,kaug,kdiag,vaug,doaug,dkacc,dvacc,dqs,dks,dvs,tz,ga),sems=rest[:12],rest[12:]
        h=pl.program_id(0)
        @pl.when(h==0)
        def _():
            ride.start(sent,got,sems)
        for hh in range(H):
            @pl.when(h==hh)
            def _():
                sl=slice(hh*HD,(hh+1)*HD)
                lane=lax.broadcasted_iota(jnp.int32,(Lq,HD),1)
                kaug[:,0:HD]=qkv_ref[:,W+hh*HD:W+(hh+1)*HD]
                ones=(lane>=3)&(lane<6)
                kaug[:,HD:]=jnp.where(ones,BF(1),ka_ref[...])
                kdiag[:,0:HD]=qkv_ref[:,W+hh*HD:W+(hh+1)*HD]
                kdiag[:,HD:]=jnp.where(ones,BF(1),BF(0)).astype(BF)
                vaug[:,0:HD]=qkv_ref[:,2*W+hh*HD:2*W+(hh+1)*HD]
                vaug[:,HD:]=jnp.where(lane<3,BF(1),BF(0)).astype(BF)
                a,b,c=split3(-lse_ref[:,hh:hh+1])
                qaug[:,0:HD]=qkv_ref[:,sl]*BF(0.125)
                qaug[:,HD:]=jnp.where(lane==3,a,jnp.where(lane==4,b,jnp.where(lane==5,c,qa_ref[...])))
                dd=do_ref[:,sl]
                delta=jnp.sum(dd.astype(F32)*of_ref[:,sl],axis=1,keepdims=True)
                a,b,c=split3(-delta)
                doaug[:,0:HD]=dd
                doaug[:,HD:]=jnp.where(lane==0,a,jnp.where(lane==1,b,jnp.where(lane==2,c,BF(0))))
        dkacc[...]=jnp.zeros_like(dkacc)
        dvacc[...]=jnp.zeros_like(dvacc)
        ga[...]=jnp.zeros_like(ga)
        bands=toeplitz(fwd_ref[pl.ds(h,1),:],nb*128)
        for d in range(nb):
            tz[d]=bands[:,d*128:(d+1)*128]
        eye=eye128()
        for q0 in range(0,Lq,256):
            qn=min(256,Lq-q0); kend=q0+qn
            qg=qaug[q0:kend,:]; dg=doaug[q0:kend,:]
            s=nt(kaug[0:kend,:],qg)
            g=nt(vaug[0:kend,:],dg)
            pcols=[]; dcols=[]
            for a in range(qn//128):
                qt=q0//128+a
                rows=slice(q0+a*128,q0+(a+1)*128)
                sd=nt(kdiag[rows,:],qaug[rows,:])
                pt=[]; dt=[]
                for b in range(kend//128):
                    d=qt-b
                    if d<0:
                        pt.append(jnp.zeros((128,128),BF)); dt.append(jnp.zeros((128,128),BF)); continue
                    t=s[b*128:(b+1)*128,a*128:(a+1)*128]
                    if d==0: t=jnp.where(eye,sd,t)
                    p=jnp.exp(t+tz[d])
                    ds=(p*g[b*128:(b+1)*128,a*128:(a+1)*128]).astype(BF)
                    ga[d]+=ds.astype(F32)
                    pt.append(p.astype(BF)); dt.append(ds)
                pcols.append(jnp.concatenate(pt,axis=0)); dcols.append(jnp.concatenate(dt,axis=0))
            P=jnp.concatenate(pcols,axis=1); DS=jnp.concatenate(dcols,axis=1)
            dvacc[0:kend,:]+=nn(P,dg[:,0:HD])
            dkacc[0:kend,:]+=nn(DS,qg[:,0:HD])
            dqs[h,q0:kend,:]=(tn(DS,kaug[0:kend,0:HD])*0.125).astype(BF)
        dks[h]=dkacc[...].astype(BF)
        dvs[h]=dvacc[...].astype(BF)
        flip=(lax.broadcasted_iota(jnp.int32,(128,128),0)+lax.broadcasted_iota(jnp.int32,(128,128),1)==127).astype(F32)
        y=jnp.concatenate([ga[d] for d in range(nb)],axis=1)
        y=lax.dot_general(flip,y,(((1,),(0,)),((),())),preferred_element_type=F32,precision=lax.Precision.HIGHEST)
        y=toeplitz_rows(jnp.concatenate([y,jnp.zeros((128,128),F32)],axis=1))
        gb_ref[pl.ds(h,1),:]=jnp.sum(y,axis=0,keepdims=True)
        @pl.when(h==H-1)
        def _():
            grad_ref[...]=jnp.concatenate([x[t] for x in (dqs,dks,dvs) for t in range(H)],axis=1)
            ride.wait(sent,got,sems)
    full=lambda s: pl.BlockSpec(s,lambda h:(0,)*len(s))
    return pl.pallas_call(kern,grid=(H,),
        out_shape=(jax.ShapeDtypeStruct((Lq,3*W),BF),jax.ShapeDtypeStruct((H,(nb+1)*128),F32))+ride.shapes,
        in_specs=[full((Lq,3*W))]+[full((Lq,W))]*2+[full((Lq,128)),full(fwd.shape),full((Lq,HD)),full((Lq,HD))]+[ANY]*ride.count,
        out_specs=(full((Lq,3*W)),full((H,(nb+1)*128)))+(ANY,)*ride.count,
        scratch_shapes=[pltpu.VMEM((Lq,2*HD),BF)]*5+[pltpu.VMEM((Lq,HD),F32)]*2+[pltpu.VMEM((H,Lq,HD),BF)]*3+[pltpu.VMEM((nb,128,128),F32)]*2+ride.scratch,
        compiler_params=pltpu.CompilerParams(vmem_limit_bytes=48*2**20,collective_id=11,has_side_effects=True),cost_estimate=cost(35.0),name="self_bwd")(
            qkv,do,of,lse,fwd,qa,ka,*[x for kind,x in plans])


MESH = pl.DeviceIdType.MESH


def sum_parts(first, cross, self_out, cross_out, n, wd):
    devices, count, wide = first.shape
    total = self_out.shape[0]

    def kern(first_ref, cross_ref, self_out_ref, cross_out_ref, sum_ref, col_ref, mean_ref):
        lane = lax.broadcasted_iota(jnp.int32, (count, 128), 1)
        means = jnp.zeros((count, 128), F32)
        sums = [None] * 8
        for ref, matrices in ((first_ref, (0, 1, 2)), (cross_ref, (4, 5, 6))):
            parts = []
            for s in range(n):
                part = ref[s].astype(F32)
                for r in range(1, devices // n):
                    part = part + ref[r * n + s].astype(F32)
                parts.append(part)
            for k, j in enumerate(matrices):
                if j > 4:
                    low = range(wd + (k - 1) * HD, 3 * wd, 2 * HD)
                    pieces = [part[:, c : c + HD] for part in parts for c in low]
                else:
                    pieces = [part[:, k * wd : (k + 1) * wd] for part in parts]
                sums[j] = jnp.concatenate(pieces, 1)[:, :D]
        for j, ref in ((3, self_out_ref), (7, cross_out_ref)):
            sums[j] = ref[0].astype(F32)
            for r in range(1, total):
                sums[j] = sums[j] + ref[r].astype(F32)
        for j in range(8):
            square = sums[j] * sums[j]
            sum_ref[:, j, :] = sums[j]
            col_ref[j : j + 1, :] = jnp.sum(square, 0, keepdims=True)
            means = jnp.where(lane == j, jnp.mean(square, 1, keepdims=True), means)
        mean_ref[...] = means

    return pl.pallas_call(
        kern,
        out_shape=(
            jax.ShapeDtypeStruct((count, 8, D), F32),
            jax.ShapeDtypeStruct((8, D), F32),
            jax.ShapeDtypeStruct((count, 128), F32),
        ),
        in_specs=[VM] * 4,
        out_specs=(VM,) * 3,
        compiler_params=pltpu.CompilerParams(vmem_limit_bytes=60 * 2**20),
        cost_estimate=cost(4.0),name="sum_parts",
    )(first, cross, self_out, cross_out)


def sum_everywhere(arrays, n, rows):
    count = n * rows
    wide_tiles, tiles = FF // 128, D // 128
    table_at, sums_at = tiles + wide_tiles, tiles + wide_tiles + 2
    assert sums_at < count

    def kern(att, exp, con, att_rows, exp_rows, con_rows, gain, table, *rest):
        outs, (x, o, got, mine, out_sem, in_sem, out_sem2, in_sem2) = rest[:6], rest[6:]
        me = lax.axis_index("rows") * n + lax.axis_index("seq")

        def place(step):
            j = lax.rem(me + step, count)
            return j, (lax.div(j, n), lax.rem(j, n))

        x[...] = jnp.zeros(x.shape, F32)
        for t in range(tiles):
            x[t] = att[:, t * 128 : (t + 1) * 128]
            x[tiles + t, 2:5, :] = gain[:, t * 128 : (t + 1) * 128]
            x[tiles + t, 5:6, :] = con[:, t * 128 : (t + 1) * 128]
        for t in range(wide_tiles):
            x[tiles + t, 0:2, :] = exp[:, t * 128 : (t + 1) * 128]
        x[table_at, :, 0:BUCKETS] = table[0:8, :]
        x[table_at + 1, 0 : HEADS - 8, 0:BUCKETS] = table[8:HEADS, :]
        x[sums_at, :, 0:1] = jnp.sum(att_rows[...], 1, keepdims=True)
        x[sums_at, 0:2, 1:2] = jnp.sum(exp_rows[...], 1, keepdims=True)
        x[sums_at, 0:1, 2:3] = jnp.sum(con_rows[...], 1, keepdims=True)
        greet_all(count, n)

        def piece(step):
            j, device = place(step)
            return pltpu.make_async_remote_copy(
                src_ref=x.at[j], dst_ref=got.at[step], send_sem=out_sem.at[step], recv_sem=in_sem.at[step],
                device_id=device, device_id_type=MESH,
            )

        def total(step):
            return pltpu.make_async_remote_copy(
                src_ref=mine, dst_ref=o.at[me], send_sem=out_sem2.at[step], recv_sem=in_sem2.at[step],
                device_id=place(step)[1], device_id_type=MESH,
            )

        def start_piece(step, carry):
            piece(step).start()
            return carry

        def add_piece(step, carry):
            piece(step).wait()
            return carry + got[step]

        def start_total(step, carry):
            total(step).start()
            return carry

        def wait_total(step, carry):
            total(step).wait()
            return carry

        lax.fori_loop(1, count, start_piece, 0)
        mine[...] = lax.fori_loop(1, count, add_piece, x[me])
        lax.fori_loop(1, count, start_total, 0)
        o[me] = mine[...]
        lax.fori_loop(1, count, wait_total, 0)
        att_out, exp_out, con_out, sums_out, gain_out, table_out = outs
        for t in range(tiles):
            att_out[:, t * 128 : (t + 1) * 128] = o[t]
            gain_out[:, t * 128 : (t + 1) * 128] = o[tiles + t, 2:5, :]
            con_out[:, t * 128 : (t + 1) * 128] = o[tiles + t, 5:6, :]
        for t in range(wide_tiles):
            exp_out[:, t * 128 : (t + 1) * 128] = o[tiles + t, 0:2, :]
        table_out[0:8, :] = o[table_at, :, 0:BUCKETS]
        table_out[8:HEADS, :] = o[table_at + 1, 0 : HEADS - 8, 0:BUCKETS]
        sums_out[...] = o[sums_at]

    shapes = ((8, D), (2, FF), (1, D), (8, 128), (3, D), (HEADS, BUCKETS))
    return pl.pallas_call(
        kern,
        out_shape=tuple(jax.ShapeDtypeStruct(shape, F32) for shape in shapes),
        in_specs=[VM] * 8,
        out_specs=(VM,) * 6,
        scratch_shapes=[pltpu.VMEM((count, 8, 128), F32)] * 3
        + [pltpu.VMEM((8, 128), F32)]
        + [pltpu.SemaphoreType.DMA((count,))] * 4,
        compiler_params=pltpu.CompilerParams(collective_id=1, has_side_effects=True),
        cost_estimate=cost(16.0),
        name="sum_everywhere",
    )(*arrays)


def feed_forward(norm, feed, contract, branch, part=512):
    length = norm.shape[0]
    scale = (2.0 / 3.141592653589793) ** 0.5

    def kern(norm_ref, gate_ref, up_ref, down_ref, branch_ref, hidden_ref, dgate_ref, dup_ref, dnorm_ref):
        a, b = nn(norm_ref[...], gate_ref[...]), nn(norm_ref[...], up_ref[...])
        grad = nt(branch_ref[...], down_ref[...])
        square = a * a
        t = jnp.tanh(scale * (a + 0.044715 * (a * square)))
        cdf = 0.5 * (1.0 + t)
        gelu = a * cdf
        slope = cdf + (0.5 * scale) * a * (1.0 - t * t) * (1.0 + 0.134145 * square)
        dgate, dup = (grad * b * slope).astype(BF), (grad * gelu).astype(BF)
        hidden_ref[...] = (gelu * b).astype(BF)
        dgate_ref[...], dup_ref[...] = dgate, dup
        dnorm = nt(dgate, gate_ref[...]) + nt(dup, up_ref[...])

        @pl.when(pl.program_id(0) == 0)
        def _():
            dnorm_ref[...] = dnorm

        @pl.when(pl.program_id(0) > 0)
        def _():
            dnorm_ref[...] += dnorm

    whole = pl.BlockSpec((length, D), lambda c: (0, 0))
    columns = pl.BlockSpec((length, part), lambda c: (0, c))
    wide = jax.ShapeDtypeStruct((length, FF), BF)
    return pl.pallas_call(
        kern,
        grid=(FF // part,),
        out_shape=(wide, wide, wide, jax.ShapeDtypeStruct((length, D), F32)),
        in_specs=[
            whole,
            pl.BlockSpec((D, part), lambda c: (0, c)),
            pl.BlockSpec((D, part), lambda c: (0, c + FF // part)),
            pl.BlockSpec((part, D), lambda c: (c, 0)),
            whole,
        ],
        out_specs=(columns, columns, columns, whole),
        compiler_params=pltpu.CompilerParams(vmem_limit_bytes=40 * 2**20),
        cost_estimate=cost(10.0),
        name="feed_forward",
    )(norm, feed, feed, contract, branch)


def normalize(values, scaling):
    return values * lax.rsqrt(jnp.mean(values * values, -1, keepdims=True) + NORM_EPS) * scaling


def update_all(totals, attention, expand, contract, feed, gain, table, passed, spare):
    count, deep = feed.shape[0], (feed.shape[1] - 2 * FF) // D

    def kern(total_ref, *refs):
        att, exp, con, (feed_ref,) = refs[:6], refs[6:11], refs[11:16], refs[16:17]
        vectors, held, outs = refs[17:25], refs[25 : 25 + len(passed)], refs[25 + len(passed) :]
        stops = len(passed)
        outs, kept, sem = outs[: 19 + stops], outs[19 + stops : -1], outs[-1]
        att_out, exp_out, con_out, vector_out = outs[:3], outs[3:7], outs[7:11], outs[11:19]
        arriving = [pltpu.make_async_copy(x, y, sem.at[0, k]) for k, (x, y) in enumerate(zip(held, kept))]
        leaving = [pltpu.make_async_copy(x, y, sem.at[1, k]) for k, (x, y) in enumerate(zip(kept, outs[19:]))]
        for copy in arriving:
            copy.start()
        for k in (0, 4):
            gradient = vectors[k][...]
            vector_out[k][...] = gradient
            vector_out[k + 1][...], vector_out[k + 2][...], vector_out[k + 3][...] = adaptive(
                gradient, vectors[k + 1][...], vectors[k + 2][...], vectors[k + 3][...]
            )

        def columns(old, summed, total):
            return BETA_TWO * old[...] + (1.0 - BETA_TWO) * (summed[...] / total)

        def step(gradient, moment, weight, row, column, row_mean):
            moment_new = BETA_ONE * moment + (1.0 - BETA_ONE) * gradient
            second = row * column / row_mean
            stepped = (
                moment_new
                / (1.0 - BETA_ONE**STEP)
                / (jnp.sqrt(second / (1.0 - BETA_TWO**STEP)) + ADAM_EPS)
            )
            return moment_new, weight - MATRIX_RATE * (stepped + WEIGHT_DECAY * weight)

        g, m, w, r, k, ks = att
        new = columns(k, ks, D)
        att_out[1][...] = new
        for j in range(8):
            mean = total_ref[j : j + 1, 0:1] / D
            att_out[0][:, j, :], att_out[2][:, j, :] = step(
                g[:, j, :], m[:, j, :], w[:, j, :], r[:, j : j + 1], new[j : j + 1], mean
            )
        for copy, onward in zip(arriving, leaving):
            copy.wait()
            onward.start()
        m, w, r, k, ks = exp
        new = columns(k, ks, D)
        exp_out[2][...] = new
        for j in range(2):
            mean = total_ref[j : j + 1, 1:2] / D
            gradient = feed_ref[:, j * FF : (j + 1) * FF].astype(F32)
            exp_out[0][:, j, :] = gradient
            exp_out[1][:, j, :], exp_out[3][:, j, :] = step(
                gradient, m[:, j, :], w[:, j, :], r[:, j : j + 1], new[j : j + 1], mean
            )
        m, w, r, k, ks = con
        new = columns(k, ks, FF)
        con_out[2][...] = new
        for group in range(deep):
            low, high = group * count, min((group + 1) * count, deep * count - spare)
            gradient = feed_ref[:, 2 * FF + group * D : 2 * FF + (group + 1) * D].astype(F32)[: high - low]
            con_out[0][low:high, :] = gradient
            con_out[1][low:high, :], con_out[3][low:high, :] = step(
                gradient, m[low:high, :], w[low:high, :], r[low:high, :], new, total_ref[0:1, 2:3] / FF
            )
        for copy in leaving:
            copy.wait()

    def like(x):
        return jax.ShapeDtypeStruct(x.shape, F32)

    g, m, w, r, k, ks = attention
    shapes = [like(m), like(k), like(w)]
    for m, w, r, k, ks in (expand, contract):
        shapes += [like(m), like(m), like(k), like(w)]
    shapes += [like(x) for x in gain + table] + [jax.ShapeDtypeStruct(x.shape, x.dtype) for x in passed]
    return pl.pallas_call(
        kern,
        out_shape=tuple(shapes),
        in_specs=[VM] * 26 + [ANY] * len(passed),
        out_specs=(VM,) * 19 + (ANY,) * len(passed),
        scratch_shapes=[pltpu.VMEM(x.shape, x.dtype) for x in passed] + [pltpu.SemaphoreType.DMA((2, len(passed)))],
        compiler_params=pltpu.CompilerParams(vmem_limit_bytes=60 * 2**20),
        cost_estimate=cost(5.0),
        name="update_all",
    )(totals, *attention, *expand, *contract, feed, *gain, *table, *passed)


def factored_start(gradient, rowwise):
    square = gradient * gradient
    rowwise_new = BETA_TWO * rowwise + (1.0 - BETA_TWO) * jnp.mean(square, 2).T
    return (rowwise_new, jnp.sum(square, 0))


def factored_finish(gradient, moment, rowwise_new, colwise, weight, column_sum, row_sum, total_rows):
    colwise_new = BETA_TWO * colwise + (1.0 - BETA_TWO) * (column_sum / total_rows)
    moment_new = BETA_ONE * moment + (1.0 - BETA_ONE) * gradient
    second = rowwise_new.T[:, :, None] * colwise_new[None] / (row_sum / total_rows)[None, :, None]
    stepped = (
        moment_new / (1.0 - BETA_ONE**STEP) / (jnp.sqrt(second / (1.0 - BETA_TWO**STEP)) + ADAM_EPS)
    )
    updated = weight - MATRIX_RATE * (stepped + WEIGHT_DECAY * weight)
    return (moment_new, colwise_new, updated)


def adaptive(gradient, moment, second, weight):
    moment_new = BETA_ONE * moment + (1.0 - BETA_ONE) * gradient
    second_new = BETA_TWO * second + (1.0 - BETA_TWO) * gradient * gradient
    stepped = (
        moment_new
        / (1.0 - BETA_ONE**STEP)
        / (jnp.sqrt(second_new / (1.0 - BETA_TWO**STEP)) + ADAM_EPS)
    )
    return (moment_new, second_new, weight - VECTOR_RATE * stepped)


def make_shards(n, rows):
    devices = n * rows
    both = ("rows", "seq")
    hpd = -(-HEADS // n)
    wd = hpd * HD
    wide = n * wd

    def widen(values):
        extra = wide - values.shape[-1]
        return values if extra == 0 else jnp.pad(values, [(0, 0)] * (values.ndim - 1) + [(0, extra)])

    def blocks_along_seq(values, gate):
        blocks = []
        for step in range(0, n, 2):
            block = values
            if step:
                block = lax.ppermute(values, "seq", [(i, i ^ step) for i in range(n)])
                block = lax.optimization_barrier((block, gate))[0]
            blocks += [block, lax.ppermute(block, "seq", [(i, i ^ 1) for i in range(n)])]
        return blocks

    def by_heads(weight):
        count, j = weight.shape[:2]
        return jnp.moveaxis(widen(weight).reshape(count, j, n * hpd, HD), 2, 1).reshape(count, wide * j)

    def to_seq(values, collective_id):
        (parts,) = exchange([("seq", values.reshape(n, -1, values.shape[1]))], n, rows, collective_id)
        return side_by_side(parts)[:, :D]

    def side_by_side(parts):
        return jnp.moveaxis(parts, 0, 1).reshape(parts.shape[1], -1)

    def shards(
        decoder_input,
        encoder_output,
        cotangent,
        decoder_segment,
        decoder_padding,
        encoder_segment,
        encoder_padding,
        distance_bucket,
        attention_weight,
        attention_moment,
        attention_rowwise,
        attention_colwise,
        expand_weight,
        expand_moment,
        expand_rowwise,
        expand_colwise,
        contract_weight,
        contract_moment,
        contract_rowwise,
        contract_colwise,
        norm_gain,
        gain_moment,
        gain_second,
        relative_table,
        table_moment,
        table_second,
    ):
        shard = lax.axis_index("seq")
        length = decoder_segment.shape[1]
        attention_low = attention_weight.astype(BF)
        count = expand_weight.shape[0]
        first_parts = jnp.moveaxis(widen(attention_low[:, 0:3]).reshape(count, 3, n, wd), 2, 0)
        row_input, first_columns = gather_seq(
            decoder_input[0], n, rows, 3, [("own", first_parts.reshape(n, count, 3 * wd))]
        )
        first_columns = first_columns.reshape(D, 3 * wd)
        attention_full = lax.all_gather(
            jnp.concatenate(
                (
                    attention_low[:, 3],
                    attention_low[:, 7],
                    by_heads(attention_low[:, 4:5]),
                    by_heads(attention_low[:, 5:7]),
                ),
                1,
            ),
            both, axis=0, tiled=True,
        )
        deep = -(-contract_weight.shape[0] // count)
        spare = deep * count - contract_weight.shape[0]
        contract_low = jnp.pad(contract_weight.astype(BF), ((0, spare), (0, 0)))
        feed_full = lax.all_gather(
            jnp.concatenate(
                (
                    expand_weight.astype(BF).reshape(count, 2 * FF),
                    jnp.moveaxis(contract_low.reshape(deep, count, D), 0, 1).reshape(count, deep * D),
                ),
                1,
            ),
            both, axis=0, tiled=True,
        )
        contract_full = jnp.concatenate(
            [
                feed_full[:, 2 * FF + g * D : 2 * FF + (g + 1) * D].reshape(devices, count, D)[
                    :, : contract_weight.shape[0] - g * count
                ]
                for g in range(deep)
            ],
            1,
        ).reshape(FF, D)
        edges = (0, D, 2 * D, 2 * D + wide, 2 * D + 3 * wide)
        self_out_weight, cross_out_weight, cross_query_weight, cross_pair_weight = (
            attention_full[:, low:high] for low, high in zip(edges[:-1], edges[1:])
        )
        cross_query_columns = lax.dynamic_slice_in_dim(cross_query_weight, shard * wd, wd, 1)
        cross_columns = lax.dynamic_slice_in_dim(cross_pair_weight, shard * 2 * wd, 2 * wd, 1)

        def own_rows(matrix):
            padded = jnp.pad(matrix, ((0, wide - D), (0, 0))) if wide > D else matrix
            return lax.dynamic_slice_in_dim(padded, shard * wd, wd, 0)

        document = jnp.arange(HD, dtype=jnp.int32)[None, :]
        decoder_document = decoder_segment[0][:, None] == document
        query_side = decoder_document.astype(BF)
        self_side = jnp.where(
            (document < 3) & ~(decoder_document & (decoder_padding[0][:, None] == 1)), NEG, 0.0
        ).astype(BF)
        real_document = jnp.where(encoder_padding[0] == 1, encoder_segment[0], -1).reshape(n, -1)
        real_document = jnp.concatenate(
            [lax.dynamic_slice_in_dim(real_document, shard ^ p, 1, 0)[0] for p in range(n)]
        )
        cross_side = jnp.where(
            (document < 3) & (real_document[:, None] != document), NEG, 0.0
        ).astype(BF)
        onehot = (
            distance_bucket[:, None] == jnp.arange(BUCKETS, dtype=jnp.int32)[None, :]
        ).astype(F32)
        table_own = lax.dynamic_slice_in_dim(
            jnp.pad(relative_table.T, ((0, n * hpd - HEADS), (0, 0))), shard * hpd, hpd, 0
        )
        bias = jnp.einsum("db,hb->hd", onehot, table_own, precision=HIGHEST)
        beyond = jnp.full((hpd, 128), NEG, F32)
        bias_forward = jnp.concatenate((beyond, bias), 1)
        bias_backward = jnp.concatenate((bias[:, ::-1], beyond), 1)

        def dot(left, right):
            return jnp.dot(left, right, preferred_element_type=F32)

        def dot_back(left, right):
            return lax.dot_general(left, right, (((1,), (1,)), ((), ())), preferred_element_type=F32)

        def outer(left, right):
            return lax.dot_general(left, right, (((0,), (0,)), ((), ())), preferred_element_type=F32)

        row_norm = normalize(row_input.astype(F32), norm_gain[0]).astype(BF)
        self_proj = dot(row_norm, first_columns).astype(BF)
        self_heads, self_exact, self_lse = self_fwd(
            self_proj, bias_backward, query_side, self_side
        )
        inputs = decoder_input[0].astype(F32)
        self_heads, cross_side = lax.optimization_barrier((self_heads, cross_side))
        self_out = to_seq(self_heads, 8)
        after_self = inputs + dot(self_out, self_out_weight)
        encoder_blocks = blocks_along_seq(
            lax.optimization_barrier((encoder_output[0], row_input))[0], after_self
        )
        cross_norm = normalize(after_self, norm_gain[1]).astype(BF)
        row_cross_norm = gather_seq(cross_norm, n, rows, 4)
        cross_query = dot(row_cross_norm, cross_query_columns).astype(BF)
        cross_pair = project_blocks(encoder_blocks, cross_columns)
        cross_heads, cross_exact, cross_lse = cross_fwd(
            cross_query, cross_pair, query_side, cross_side
        )
        cross_out = to_seq(cross_heads, 9)
        after_cross = after_self + dot(cross_out, cross_out_weight)
        feed_norm = normalize(after_cross, norm_gain[2]).astype(BF)
        feed_branch = cotangent[0]
        grad_result = feed_branch.astype(F32)
        hidden, grad_gate, grad_up, feed_norm_grad = feed_forward(feed_norm, feed_full, contract_full, feed_branch)
        unused_norm, norm_back = jax.vjp(normalize, after_cross, norm_gain[2])
        feed_part, feed_gain = norm_back(feed_norm_grad)
        grad_after_cross = grad_result + feed_part
        cross_branch = grad_after_cross.astype(BF)
        down_rows = deep * count - spare

        def feed_gradients(ins, outs):
            norm_ref, gate_ref, up_ref, hidden_ref, branch_ref = ins
            (o_ref,) = outs
            for c in range(0, 2 * FF, 512):
                low = c % FF
                part = tn(norm_ref[...], (gate_ref if c < FF else up_ref)[:, low : low + 512])
                o_ref[:, :, c : c + 512] = part.reshape(devices, count, 512).astype(BF)
            group = devices * 1024 // FF
            for c in range(0, FF, 1024):
                part = tn(hidden_ref[:, c : c + 1024], branch_ref[...]).reshape(group, down_rows, D)
                first = c // 1024 * group
                for g in range(deep):
                    piece = part[:, g * count : (g + 1) * count]
                    if piece.shape[1] < count:
                        low = jnp.zeros((group, count - piece.shape[1], D), F32)
                        piece = jnp.concatenate((piece, low), 1)
                    o_ref[first : first + group, :, 2 * FF + g * D : 2 * FF + (g + 1) * D] = piece.astype(BF)

        if count % 8 == 0:
            row_cross_branch, feed_local = gather_seq(
                cross_branch, n, rows, 5,
                job=Job(
                    (feed_norm, grad_gate, grad_up, hidden, feed_branch),
                    (jax.ShapeDtypeStruct((devices, count, 2 * FF + deep * D), BF),),
                    feed_gradients,
                ),
            )
            feed_local = feed_local.reshape(D, -1)
        else:
            row_cross_branch = gather_seq(cross_branch, n, rows, 5)
            contract_local = outer(hidden, feed_branch).astype(BF).reshape(devices, -1, D)
            contract_local = jnp.pad(contract_local, ((0, 0), (0, spare), (0, 0)))
            feed_local = jnp.concatenate(
                [outer(feed_norm, grad).astype(BF) for grad in (grad_gate, grad_up)]
                + [contract_local[:, g * count : (g + 1) * count].reshape(D, D) for g in range(deep)],
                1,
            )
        feed_low = lax.psum_scatter(feed_local, both, scatter_dimension=0, tiled=True)
        feed_sum = feed_low.astype(F32)
        cross_grad = dot_back(row_cross_branch, own_rows(cross_out_weight)).astype(BF)
        expand_sum = feed_sum[:, 0 : 2 * FF].reshape(count, 2, FF)
        contract_sum = jnp.concatenate(
            [feed_sum[:, 2 * FF + g * D : 2 * FF + (g + 1) * D] for g in range(deep)], 0
        )[: deep * count - spare]
        matched = wide == D and wd == rows * count
        cross_out_local = outer(cross_heads, row_cross_branch).astype(BF)
        cross_plans = [("rows", cross_out_local.reshape(rows, count, D))] if matched else []
        cross_qparts, cross_home, cross_qgrad, *cross_grads = cross_bwd(
            cross_query, cross_pair, cross_grad, cross_exact, cross_lse, query_side, cross_side, cross_plans, n, rows
        )
        cross_rows, cross_grads = cross_grads[: len(cross_plans)], cross_grads[len(cross_plans) :]
        grad_cross_query = side_by_side(cross_qparts)[:, :D]
        unused_norm, norm_back = jax.vjp(normalize, after_self, norm_gain[1])
        cross_part, cross_gain = norm_back(dot_back(grad_cross_query, cross_query_weight[:, :D]))
        grad_after_self = grad_after_cross + cross_part
        self_branch = grad_after_self.astype(BF)
        def cross_gradients(ins, outs):
            norm_ref, query_ref = ins[:2]
            (o_ref,) = outs
            o_ref[:, 0:wd] = tn(norm_ref[...], query_ref[...]).astype(BF)
            pair = tn(ins[2][...], ins[2 + n][...])
            for p in range(1, n):
                pair = pair + tn(ins[2 + p][...], ins[2 + n + p][...])
            o_ref[:, wd : 3 * wd] = pair.astype(BF)

        row_self_branch, cross_local = gather_seq(
            self_branch, n, rows, 6,
            job=Job(
                (row_cross_norm, cross_qgrad.reshape(-1, wd))
                + tuple(encoder_blocks) + tuple(cross_grads),
                (jax.ShapeDtypeStruct((D, 3 * wd), BF),),
                cross_gradients,
            ),
        )
        self_grad = dot_back(row_self_branch, own_rows(self_out_weight)).astype(BF)
        self_out_local = outer(self_heads, row_self_branch).astype(BF)
        rows_local = (self_out_local, cross_out_local)
        self_grads, pair_bias, cross_parts = self_bwd(
            self_proj, self_grad, self_exact, self_lse, bias_forward, query_side, self_side,
            [("all", cross_local.reshape(devices, count, 3 * wd))], n, rows,
        )
        rows_plans = [("rows", self_out_local.reshape(rows, count, D))] if matched else []
        grad_bias = pair_bias[:, 128:]
        table_own_grad = jnp.einsum("hd,db->hb", grad_bias, onehot, precision=HIGHEST)
        table_local = lax.dynamic_update_slice_in_dim(
            jnp.zeros((n * hpd, BUCKETS), F32), table_own_grad, shard * hpd, 0
        )[:HEADS]
        self_back = dot_back(self_grads, first_columns).astype(BF)
        def encoder_job(ins, outs):
            home_ref, weight_ref, hidden_ref, down_ref, stream_ref = ins
            total = None
            for t in range(n):
                for h in range(hpd):
                    low = (t * hpd + h) * 2 * HD
                    part = nt(home_ref[t, h], weight_ref[:, low : low + 2 * HD])
                    total = part if total is None else total + part
            outs[0][...] = total
            outs[1][...] = (stream_ref[...] + nn(hidden_ref[...], down_ref[...])).astype(BF)

        self_back_sum, self_parts, *rest = reduce_exchange(
            self_back.reshape(n, -1, D),
            [
                ("all", outer(row_norm, self_grads).astype(BF).reshape(devices, count, 3 * wd)),
            ] + rows_plans,
            n, rows, 7,
            job=Job(
                (
                    cross_home,
                    (attention_full, (2 * D + wide, 2 * D + 3 * wide)),
                    hidden,
                    contract_full,
                    after_cross,
                ),
                (
                    jax.ShapeDtypeStruct(encoder_output.shape[1:], F32),
                    jax.ShapeDtypeStruct(decoder_input.shape[1:], BF),
                ),
                encoder_job,
            ),
        )
        *rows_parts, encoder_gradient, layer_output = rest
        rows_parts += cross_rows
        if not matched:
            padded = lax.dynamic_update_slice_in_dim(
                jnp.zeros((wide, 2 * D), BF), jnp.concatenate(rows_local, 1), shard * wd, 0
            )[:D]
            whole = lax.psum_scatter(padded, both, scatter_dimension=0, tiled=True)[None]
            rows_parts = [whole[:, :, :D], whole[:, :, D:]]
        unused_norm, norm_back = jax.vjp(normalize, inputs, norm_gain[0])
        self_part, self_gain = norm_back(self_back_sum)
        input_gradient = grad_after_self + self_part

        attention_sum, attention_columns, attention_means = sum_parts(
            self_parts, cross_parts, *rows_parts, n, wd
        )
        attention_rows = BETA_TWO * attention_rowwise + (1.0 - BETA_TWO) * attention_means[:, 0:8].T
        expand_rows, expand_columns = factored_start(expand_sum, expand_rowwise)
        contract_rows, contract_columns = factored_start(
            contract_sum[:, None, :], contract_rowwise[None, :]
        )
        gain_local = jnp.stack((self_gain, cross_gain, feed_gain), 0)
        attention_total, expand_total, contract_total, row_totals, gain_gradient, table_gradient = (
            sum_everywhere(
                (
                    attention_columns,
                    expand_columns,
                    contract_columns,
                    attention_rows,
                    expand_rows,
                    contract_rows,
                    gain_local,
                    table_local,
                ),
                n, rows,
            )
        )
        attention_rowtotal, expand_rowtotal, contract_rowtotal = (
            row_totals[:, 0],
            row_totals[:2, 1],
            row_totals[:1, 2],
        )
        if count % 8 == 0:
            (
                *attention_new, expand_sum, moment_expand, colwise_expand, updated_expand,
                contract_sum, moment_contract, colwise_contract, updated_contract,
                gain_gradient, moment_gain, second_gain, updated_gain,
                table_gradient, moment_table, second_table, updated_table,
                encoder_gradient, layer_output,
            ) = update_all(
                row_totals,
                (
                    attention_sum, attention_moment, attention_weight, attention_rows.T,
                    attention_colwise, attention_total,
                ),
                (expand_moment, expand_weight, expand_rows.T, expand_colwise, expand_total),
                (contract_moment, contract_weight, contract_rows.T, contract_colwise[None], contract_total),
                feed_low,
                (gain_gradient, gain_moment, gain_second, norm_gain),
                (table_gradient, table_moment.T, table_second.T, relative_table.T),
                (encoder_gradient, layer_output),
                spare,
            )
            attention_new = attention_new[:3]
            gain_new = (moment_gain, second_gain, updated_gain)
            table_gradient = table_gradient.T
            table_new = (moment_table.T, second_table.T, updated_table.T)
            expand_new = (moment_expand, colwise_expand, updated_expand)
            contract_new = (moment_contract[:, None], colwise_contract, updated_contract[:, None])
        else:
            attention_new = factored_finish(
                attention_sum,
                attention_moment,
                attention_rows,
                attention_colwise,
                attention_weight,
                attention_total,
                attention_rowtotal,
                D,
            )
            expand_new = factored_finish(
                expand_sum,
                expand_moment,
                expand_rows,
                expand_colwise,
                expand_weight,
                expand_total,
                expand_rowtotal,
                D,
            )
            contract_new = factored_finish(
                contract_sum[:, None, :],
                contract_moment[:, None, :],
                contract_rows,
                contract_colwise[None, :],
                contract_weight[:, None, :],
                contract_total,
                contract_rowtotal,
                FF,
            )
            gain_new = adaptive(gain_gradient, gain_moment, gain_second, norm_gain)
            table_gradient = table_gradient.T
            table_new = adaptive(table_gradient, table_moment, table_second, relative_table)
        return (
            layer_output[None],
            input_gradient[None],
            encoder_gradient[None],
            attention_sum,
            attention_new[0],
            attention_rows,
            attention_new[1],
            attention_new[2],
            expand_sum,
            expand_new[0],
            expand_rows,
            expand_new[1],
            expand_new[2],
            contract_sum,
            contract_new[0][:, 0],
            contract_rows[0],
            contract_new[1][0],
            contract_new[2][:, 0],
            gain_gradient,
            gain_new[0],
            gain_new[1],
            gain_new[2],
            table_gradient,
            table_new[0],
            table_new[1],
            table_new[2],
        )

    return shards


def solution(mesh):
    placed = (
        P("rows", "seq", None),
        P("rows", "seq", None),
        P("rows", "seq", None),
        P("rows", None),
        P("rows", None),
        P("rows", None),
        P("rows", None),
        P(),
        P(("rows", "seq"), None, None),
        P(("rows", "seq"), None, None),
        P(None, ("rows", "seq")),
        P(),
        P(("rows", "seq"), None, None),
        P(("rows", "seq"), None, None),
        P(None, ("rows", "seq")),
        P(),
        P(("rows", "seq"), None),
        P(("rows", "seq"), None),
        P(("rows", "seq")),
        P(),
        P(),
        P(),
        P(),
        P(),
        P(),
        P(),
    )
    return jax.shard_map(
        make_shards(mesh.shape["seq"], mesh.shape["rows"]),
        mesh=mesh,
        in_specs=placed,
        out_specs=(
            P("rows", "seq", None),
            P("rows", "seq", None),
            P("rows", "seq", None),
            P(("rows", "seq"), None, None),
            P(("rows", "seq"), None, None),
            P(None, ("rows", "seq")),
            P(),
            P(("rows", "seq"), None, None),
            P(("rows", "seq"), None, None),
            P(("rows", "seq"), None, None),
            P(None, ("rows", "seq")),
            P(),
            P(("rows", "seq"), None, None),
            P(("rows", "seq"), None),
            P(("rows", "seq"), None),
            P(("rows", "seq")),
            P(),
            P(("rows", "seq"), None),
            P(),
            P(),
            P(),
            P(),
            P(),
            P(),
            P(),
            P(),
        ),
        check_vma=False,
    )
```

```python
import jax
import jax.numpy as jnp
from jax import lax
from jax.experimental import pallas as pl
from jax.experimental.pallas import tpu as pltpu
from jax.sharding import PartitionSpec as P

D = 768
FF = 2048
HEADS = 12
BUCKETS = 32
STEP = 10
HIGHEST = lax.Precision.HIGHEST
NORM_EPS = 1e-06
BETA_ONE = 0.9
BETA_TWO = 0.999
ADAM_EPS = 1e-08
WEIGHT_DECAY = 0.01
MATRIX_RATE = 0.15
VECTOR_RATE = 1.0
HD = 64
NEG = -1e30
F32 = jnp.float32
BF = jnp.bfloat16

def nt(a,b): return lax.dot_general(a,b,(((1,),(1,)),((),())),preferred_element_type=F32)
def nn(a,b): return lax.dot_general(a,b,(((1,),(0,)),((),())),preferred_element_type=F32)
def tn(a,b): return lax.dot_general(a,b,(((0,),(0,)),((),())),preferred_element_type=F32)

def cross_fwd(q,kv,qa,ka,qb=352,kc=1024):
    Lq,W=q.shape; Lk=kv.shape[0]; H=W//HD
    nk=Lk//kc
    def kern(q_ref,kv_ref,qa_ref,ka_ref,o_ref,of_ref,lse_ref,kaug,vs,s_s,m_s,l_s,acc):
        @pl.when(pl.program_id(0)==0)
        def _():
            for h in range(H):
                kaug[h,:,0:HD]=kv_ref[:,2*h*HD:(2*h+1)*HD]
                kaug[h,:,HD:2*HD]=ka_ref[...]
                vs[h]=kv_ref[:,(2*h+1)*HD:(2*h+2)*HD]
        lane=lax.broadcasted_iota(jnp.int32,(qb,128),1)
        lses=jnp.zeros((qb,128),F32)
        outs=[]
        for h in range(H):
            qh=(q_ref[:,h*HD:(h+1)*HD]*BF(0.125)).astype(BF)
            qg=jnp.concatenate([qh,qa_ref[...]],axis=1)
            m_s[...]=jnp.full((qb,128),-3e38,F32)
            for c in range(nk):
                s=nt(qg,kaug[h,c*kc:(c+1)*kc,:])
                s_s[:,c*kc:(c+1)*kc]=s
                mm=m_s[...]
                for t in range(kc//128): mm=jnp.maximum(mm,s[:,t*128:(t+1)*128])
                m_s[...]=mm
            m=jnp.max(m_s[...],axis=1,keepdims=True)
            l_s[...]=jnp.zeros((qb,128),F32)
            acc[...]=jnp.zeros((qb,HD),F32)
            for c in range(nk):
                p=jnp.exp(s_s[:,c*kc:(c+1)*kc]-m)
                ll=l_s[...]
                for t in range(kc//128): ll=ll+p[:,t*128:(t+1)*128]
                l_s[...]=ll
                acc[...]+=nn(p.astype(BF),vs[h,c*kc:(c+1)*kc,:])
            l=jnp.sum(l_s[...],axis=1,keepdims=True)
            o=acc[...]/l
            outs.append(o)
            lses=jnp.where(lane==h,m+jnp.log(l),lses)
        oo=jnp.concatenate(outs,axis=1)
        o_ref[...]=oo.astype(BF)
        of_ref[...]=oo
        lse_ref[...]=lses
    full=lambda s: pl.BlockSpec(s,lambda i:(0,)*len(s))
    row=lambda w: pl.BlockSpec((qb,w),lambda i:(i,0))
    return pl.pallas_call(kern,grid=(Lq//qb,),
        out_shape=(jax.ShapeDtypeStruct((Lq,W),BF),jax.ShapeDtypeStruct((Lq,W),F32),jax.ShapeDtypeStruct((Lq,128),F32)),
        in_specs=[row(W),full((Lk,2*W)),row(HD),full((Lk,HD))],
        out_specs=(row(W),row(W),row(128)),
        scratch_shapes=[pltpu.VMEM((H,Lk,2*HD),BF),pltpu.VMEM((H,Lk,HD),BF),pltpu.VMEM((qb,Lk),F32),pltpu.VMEM((qb,128),F32),pltpu.VMEM((qb,128),F32),pltpu.VMEM((qb,HD),F32)],
        compiler_params=pltpu.CompilerParams(vmem_limit_bytes=56*2**20),cost_estimate=cost(31.0),name="cross_fwd")(q,kv,qa,ka)

def split3(x):
    a=x.astype(BF); r=x-a.astype(F32)
    b=r.astype(BF); c=(r-b.astype(F32)).astype(BF)
    return a,b,c

def cross_bwd(q,kv,do,of,lse,qa,ka,plans,n,rows,qb=256):
    Lq,W=q.shape; Lk=kv.shape[0]; H=W//HD; kc=Lk//n
    ride=Exchange(plans,n,rows); riders=ride.scratch if plans else []
    def kern(q_ref,kv_ref,do_ref,of_ref,lse_ref,qa_ref,ka_ref,*rest):
        sent,rest=rest[:ride.count],rest[ride.count:]
        dq_ref,home_ref,dqw=rest[:3]
        got,rest=rest[3:3+ride.count],rest[3+ride.count:]
        rest,sems=rest[:len(rest)-len(riders)],rest[len(rest)-len(riders):]
        dkv_refs=rest[:n]
        kaug,vaug,qaug,doaug,ps,dss,dqacc,kt,dqs,dkvs,q_out,q_in,kv_out,kv_in,own=rest[n:]
        h=pl.program_id(0); c=pl.program_id(1)
        r,s=lax.axis_index("rows"),lax.axis_index("seq")
        def home(p):
            return pltpu.make_async_remote_copy(src_ref=dkvs.at[h,p*kc:(p+1)*kc],dst_ref=home_ref.at[s,h],send_sem=kv_out.at[p,h],
                recv_sem=kv_in.at[p,h],device_id=(r,s^p),device_id_type=MESH)
        def keep():
            return pltpu.make_async_copy(dkvs.at[h,0:kc],home_ref.at[s,h],own.at[h])
        def turn(p):
            return pltpu.make_async_remote_copy(src_ref=dqw.at[s^p],dst_ref=dq_ref.at[s],send_sem=q_out.at[p],
                recv_sem=q_in.at[p],device_id=(r,s^p),device_id_type=MESH)
        def stay():
            return pltpu.make_async_copy(dqw.at[s],dq_ref.at[s],own.at[H])
        @pl.when((h==0)&(c==0))
        def _():
            greet_all(n*rows if plans else n,n)
            if plans: ride.start(sent,got,sems,greet=False)
        for hh in range(H):
            @pl.when((h==hh)&(c==0))
            def _():
                sl=slice(hh*HD,(hh+1)*HD)
                kaug[:,0:HD]=kv_ref[:,2*hh*HD:(2*hh+1)*HD]
                lane=lax.broadcasted_iota(jnp.int32,(Lk,HD),1)
                kaug[:,HD:2*HD]=jnp.where((lane>=3)&(lane<6),BF(1),ka_ref[...])
                vaug[:,0:HD]=kv_ref[:,(2*hh+1)*HD:(2*hh+2)*HD]
                vaug[:,HD:2*HD]=jnp.where(lane<3,BF(1),BF(0)).astype(BF)
                lq=lax.broadcasted_iota(jnp.int32,(Lq,HD),1)
                x,y,z=split3(-lse_ref[:,hh:hh+1])
                qaug[0:Lq,0:HD]=q_ref[:,sl]*BF(0.125)
                qaug[0:Lq,HD:2*HD]=jnp.where(lq==3,x,jnp.where(lq==4,y,jnp.where(lq==5,z,qa_ref[...])))
                dd=do_ref[:,sl]
                delta=jnp.sum(dd.astype(F32)*of_ref[:,sl],axis=1,keepdims=True)
                x,y,z=split3(-delta)
                doaug[0:Lq,0:HD]=dd
                doaug[0:Lq,HD:2*HD]=jnp.where(lq==0,x,jnp.where(lq==1,y,jnp.where(lq==2,z,BF(0))))
                dqacc[...]=jnp.zeros_like(dqacc)
                for b in range(n):
                    kt[b]=kv_ref[b*kc:(b+1)*kc,2*hh*HD:(2*hh+1)*HD].astype(F32).T.astype(BF)
        off=pl.multiple_of((n-1-c)*kc,kc)
        kk=kaug[pl.ds(off,kc),:]
        vv=vaug[pl.ds(off,kc),:]
        for i in range(0,Lq,qb):
            part=slice(i,min(i+qb,Lq))
            p=jnp.exp(nt(kk,qaug[part,:]))
            g=nt(vv,doaug[part,:])
            ps[:,part]=p.astype(BF)
            dss[:,part]=(p*g).astype(BF)
        dkvs[h,pl.ds(off,kc),0:HD]=nn(dss[...],qaug[:,0:HD]).astype(BF)
        dkvs[h,pl.ds(off,kc),HD:2*HD]=nn(ps[...],doaug[:,0:HD]).astype(BF)
        dqacc[...]+=nn(kt[n-1-c],dss[...])
        for p in range(1,n):
            @pl.when(c==n-1-p)
            def _():
                home(p).start()
        @pl.when(c==n-1)
        def _():
            keep().start()
            dqs[h]=(dqacc[...].T*0.125).astype(BF)
        @pl.when((c==n-1)&(h==H-1))
        def _():
            for b in range(n):
                dqw[b]=jnp.concatenate([dqs[t,b*(Lq//n):(b+1)*(Lq//n),:] for t in range(H)],axis=1)
            for p in range(1,n): turn(p).start()
            stay().start()
            for b,dkv_ref in enumerate(dkv_refs):
                for t in range(H): dkv_ref[:,2*t*HD:2*(t+1)*HD]=dkvs[t,b*kc:(b+1)*kc,:]
            for p in range(1,n): turn(p).wait()
            stay().wait()
            if plans: ride.wait(sent,got,sems)
        @pl.when(c==n-1)
        def _():
            for p in range(1,n): home(p).wait()
            keep().wait()
    full=lambda s: pl.BlockSpec(s,lambda h,c:(0,)*len(s))
    return pl.pallas_call(kern,grid=(H,n),
        out_shape=(jax.ShapeDtypeStruct((n,Lq//n,W),BF),jax.ShapeDtypeStruct((n,H,kc,2*HD),BF),jax.ShapeDtypeStruct((n,Lq//n,W),BF))+ride.shapes+(jax.ShapeDtypeStruct((kc,2*W),BF),)*n,
        in_specs=[full((Lq,W)),full((Lk,2*W)),full((Lq,W)),full((Lq,W)),full((Lq,128)),full((Lq,HD)),full((Lk,HD))]+[ANY]*ride.count,
        out_specs=(ANY,ANY,full((n,Lq//n,W)))+(ANY,)*ride.count+(full((kc,2*W)),)*n,
        scratch_shapes=[pltpu.VMEM((Lk,2*HD),BF),pltpu.VMEM((Lk,2*HD),BF),pltpu.VMEM((Lq,2*HD),BF),pltpu.VMEM((Lq,2*HD),BF),
            pltpu.VMEM((kc,Lq),BF),pltpu.VMEM((kc,Lq),BF),pltpu.VMEM((HD,Lq),F32),pltpu.VMEM((n,HD,kc),BF),pltpu.VMEM((H,Lq,HD),BF),pltpu.VMEM((H,Lk,2*HD),BF)]
            +[pltpu.SemaphoreType.DMA((n,))]*2+[pltpu.SemaphoreType.DMA((n,H))]*2+[pltpu.SemaphoreType.DMA((H+1,))]+riders,
        compiler_params=pltpu.CompilerParams(vmem_limit_bytes=60*2**20,collective_id=10,has_side_effects=True),cost_estimate=cost(68.0),name="cross_bwd")(q,kv,do,of,lse,qa,ka,*[x for kind,x in plans])

def toeplitz(line, shift):
    return pltpu.roll(jnp.broadcast_to(line,(128,line.shape[1])),shift,1,stride=1,stride_axis=0)

def toeplitz_rows(x):
    return pltpu.roll(x,1,1,stride=1,stride_axis=0)

def eye128():
    return lax.broadcasted_iota(jnp.int32,(128,128),0)==lax.broadcasted_iota(jnp.int32,(128,128),1)

def self_fwd(qkv,rev,qa,ka):
    Lq,W=qkv.shape[0],qkv.shape[1]//3; H=W//HD; nb=Lq//128
    def kern(qkv_ref,rev_ref,qa_ref,ka_ref,o_ref,of_ref,lse_ref,qaug,kaug,kdiag,vs,os,tz):
        h=pl.program_id(0)
        for hh in range(H):
            @pl.when(h==hh)
            def _():
                sl=slice(hh*HD,(hh+1)*HD)
                qaug[:,0:HD]=qkv_ref[:,sl]*BF(0.125); qaug[:,HD:]=qa_ref[...]
                kaug[:,0:HD]=qkv_ref[:,W+hh*HD:W+(hh+1)*HD]; kaug[:,HD:]=ka_ref[...]
                kdiag[:,0:HD]=qkv_ref[:,W+hh*HD:W+(hh+1)*HD]; kdiag[:,HD:]=jnp.zeros((Lq,HD),BF)
                vs[...]=qkv_ref[:,2*W+hh*HD:2*W+(hh+1)*HD]
        @pl.when(h==0)
        def _():
            lse_ref[...]=jnp.zeros((Lq,128),F32)
        bands=toeplitz(rev_ref[pl.ds(h,1),:],(nb+1)*128-127)
        for d in range(nb):
            tz[d]=bands[:,(nb-1-d)*128:(nb-d)*128]
        eye=eye128()
        lane=lax.broadcasted_iota(jnp.int32,(128,128),1)
        for q0 in range(0,Lq,256):
            qn=min(256,Lq-q0); kend=q0+qn
            s=nt(qaug[q0:q0+qn,:],kaug[0:kend,:])
            for a in range(qn//128):
                qt=q0//128+a
                r0=q0+a*128
                rows=slice(r0,r0+128)
                sd=nt(qaug[rows,:],kdiag[rows,:])
                tiles=[]
                for b in range(qt+1):
                    t=s[a*128:(a+1)*128,b*128:(b+1)*128]
                    if b==qt: t=jnp.where(eye,sd,t)
                    tiles.append(t+tz[qt-b])
                m=tiles[0]
                for t in tiles[1:]: m=jnp.maximum(m,t)
                m=jnp.max(m,axis=1,keepdims=True)
                ps=[jnp.exp(t-m) for t in tiles]
                l=ps[0]
                for t in ps[1:]: l=l+t
                l=jnp.sum(l,axis=1,keepdims=True)
                pb=jnp.concatenate([t.astype(BF) for t in ps],axis=1)
                os[h,rows,:]=nn(pb,vs[0:(qt+1)*128,:])/l
                lse_ref[rows,:]=jnp.where(lane==h,m+jnp.log(l),lse_ref[rows,:])
        @pl.when(h==H-1)
        def _():
            oo=jnp.concatenate([os[t] for t in range(H)],axis=1)
            o_ref[...]=oo.astype(BF)
            of_ref[...]=oo
    full=lambda s: pl.BlockSpec(s,lambda h:(0,)*len(s))
    return pl.pallas_call(kern,grid=(H,),
        out_shape=(jax.ShapeDtypeStruct((Lq,W),BF),jax.ShapeDtypeStruct((Lq,W),F32),jax.ShapeDtypeStruct((Lq,128),F32)),
        in_specs=[full((Lq,3*W)),full(rev.shape),full((Lq,HD)),full((Lq,HD))],
        out_specs=(full((Lq,W)),full((Lq,W)),full((Lq,128))),
        scratch_shapes=[pltpu.VMEM((Lq,2*HD),BF)]*3+[pltpu.VMEM((Lq,HD),BF),pltpu.VMEM((H,Lq,HD),F32),pltpu.VMEM((nb,128,128),F32)],
        compiler_params=pltpu.CompilerParams(vmem_limit_bytes=48*2**20),cost_estimate=cost(15.0),name="self_fwd")(qkv,rev,qa,ka)

MESH = pl.DeviceIdType.MESH
ANY = pl.BlockSpec(memory_space=pl.ANY)
VM = pl.BlockSpec(memory_space=pltpu.VMEM)


def cost(micros):
    return pl.CostEstimate(flops=int(micros * 1.0e9), bytes_accessed=int(micros * 3.0e6), transcendentals=0)


def greet_all(count, n):
    r, s = lax.axis_index("rows"), lax.axis_index("seq")
    barrier = pltpu.get_barrier_semaphore()

    def greet(step, carry):
        j = lax.rem((s if count == n else r * n + s) + step, count)
        device = (r, j) if count == n else (lax.div(j, n), lax.rem(j, n))
        pl.semaphore_signal(barrier, inc=1, device_id=device, device_id_type=MESH)
        return carry

    lax.fori_loop(1, count, greet, 0)
    pl.semaphore_wait(barrier, count - 1)


class Exchange:
    def __init__(self, plans, n, rows):
        self.kinds = [kind for kind, x in plans]
        self.count = len(plans)
        self.n, self.rows = n, rows
        shapes = [(n * rows,) + x.shape[1:] if kind == "own" else x.shape for kind, x in plans]
        self.shapes = tuple(jax.ShapeDtypeStruct(shape, x.dtype) for shape, (kind, x) in zip(shapes, plans))
        self.scratch = [pltpu.SemaphoreType.DMA((shape[0],)) for shape in shapes for side in range(2)]
        self.scratch += [pltpu.SemaphoreType.DMA((self.count,))]

    def each(self, sent, got, sems, act):
        n, rows = self.n, self.rows
        r, s = lax.axis_index("rows"), lax.axis_index("seq")
        me = r * n + s
        for p, kind in enumerate(self.kinds):
            x, y, out_sem, in_sem, own = sent[p], got[p], sems[2 * p], sems[2 * p + 1], sems[-1].at[p]

            def remote(block, slot, device, leave, arrive, x=x, y=y, out_sem=out_sem, in_sem=in_sem):
                return pltpu.make_async_remote_copy(
                    src_ref=x.at[block], dst_ref=y.at[slot], send_sem=out_sem.at[leave], recv_sem=in_sem.at[arrive],
                    device_id=device, device_id_type=MESH,
                )

            if kind == "rows":
                def send(j, carry, act=act, x=x, y=y, own=own, remote=remote):
                    target = s * rows + j
                    away = remote(j, r, (lax.div(target, n), lax.rem(target, n)), j, r)

                    @pl.when(target != me)
                    def _():
                        act(away, True)

                    @pl.when(target == me)
                    def _():
                        act(pltpu.make_async_copy(x.at[j], y.at[r], own), None)

                    return carry

                def take(q, carry, act=act, remote=remote):
                    @pl.when((q != r) | (lax.div(me, rows) != s))
                    def _():
                        act(remote(0, q, (r, s), 0, q), False)

                    return carry

                lax.fori_loop(0, rows, send, 0)
                lax.fori_loop(0, rows, take, 0)
                continue
            if kind == "xor":
                act(pltpu.make_async_copy(x.at[0], y.at[s], own), None)
                for p in range(1, n):
                    away = remote(p, s, (r, s ^ p), p, p)
                    act(away, True)
                    act(away, False)
                continue
            length, here = (n, s) if kind == "seq" else (n * rows, me)
            act(pltpu.make_async_copy(x.at[s if kind == "own" else here], y.at[here], own), None)

            def both_ways(step, carry, act=act, length=length, here=here, kind=kind, remote=remote):
                j = lax.rem(here + step, length)
                device = (r, j) if kind == "seq" else (lax.div(j, n), lax.rem(j, n))
                away = remote(lax.rem(j, n) if kind == "own" else j, here, device, step, step)
                act(away, True)
                act(away, False)
                return carry

            lax.fori_loop(1, length, both_ways, 0)

    def start(self, sent, got, sems, greet=True):
        near = all(kind == "seq" for kind in self.kinds)
        if greet:
            greet_all(self.n if near else self.n * self.rows, self.n)
        self.each(sent, got, sems, lambda copy, away: copy.start() if away is not False else None)

    def wait(self, sent, got, sems):
        def act(copy, away):
            if away is None:
                copy.wait()
            elif away:
                copy.wait_send()
            else:
                copy.wait_recv()

        self.each(sent, got, sems, act)


class Job:
    def __init__(self, inputs=(), outs=(), body=None):
        inputs = [x if isinstance(x, tuple) else (x, None) for x in inputs]
        self.inputs, self.columns = [x for x, part in inputs], [part for x, part in inputs]
        self.outs, self.body = tuple(outs), body
        self.scratch = [
            pltpu.VMEM(x.shape if part is None else (x.shape[0], part[1] - part[0]), x.dtype) for x, part in inputs
        ]
        self.scratch += [pltpu.SemaphoreType.DMA((len(self.inputs),))] if self.inputs else []

    def split(self, refs, before, between, after):
        i, o = len(self.inputs), len(self.outs)
        head, refs = refs[:before], refs[before:]
        ins, refs = refs[:i], refs[i:]
        middle, refs = refs[:between], refs[between:]
        outs, refs = refs[:o], refs[o:]
        return head + middle + refs[:after], ins, outs, refs[after:]

    def run(self, ins, outs, scratch):
        if not self.inputs:
            return
        held, sem = scratch[:-1], scratch[-1]
        copies = [
            pltpu.make_async_copy(x if part is None else x.at[:, part[0] : part[1]], y, sem.at[k])
            for k, (x, y, part) in enumerate(zip(ins, held, self.columns))
        ]
        for copy in copies:
            copy.start()
        for copy in copies:
            copy.wait()
        self.body(held, outs)


def exchange(plans, n, rows, collective_id, job=None):
    ride, job = Exchange(plans, n, rows), job or Job()

    def kern(*refs):
        refs, ins, outs, scratch = job.split(refs, ride.count, ride.count, len(ride.scratch))
        sent, got, sems = refs[: ride.count], refs[ride.count : 2 * ride.count], refs[2 * ride.count :]
        ride.start(sent, got, sems)
        job.run(ins, outs, scratch)
        ride.wait(sent, got, sems)

    return pl.pallas_call(
        kern,
        out_shape=ride.shapes + job.outs,
        in_specs=[ANY] * (ride.count + len(job.inputs)),
        out_specs=(ANY,) * ride.count + (VM,) * len(job.outs),
        scratch_shapes=ride.scratch + job.scratch,
        compiler_params=pltpu.CompilerParams(
            collective_id=collective_id, has_side_effects=True, vmem_limit_bytes=56 * 2**20
        ),
        cost_estimate=cost(20.0),name="exchange",
    )(*[x for kind, x in plans], *job.inputs)


def reduce_exchange(partial, plans, n, rows, collective_id, job):
    ride = Exchange(plans, n, rows)
    half, length, features = n // 2, partial.shape[1], partial.shape[2]

    def kern(*refs):
        refs, ins, outs, scratch = job.split(refs, 1 + ride.count, 1 + ride.count, 7 + len(ride.scratch))
        x_ref, sent, o_ref = refs[0], refs[1 : 1 + ride.count], refs[1 + ride.count]
        got, rest = refs[2 + ride.count : 2 + 2 * ride.count], refs[2 + 2 * ride.count :]
        near, far, send, near_out, near_in, far_out, far_in = rest[:7]
        sems = rest[7:]
        r, s = lax.axis_index("rows"), lax.axis_index("seq")
        chip, parity = lax.div(s, 2), lax.rem(s, 2)
        beside = s + 1 - 2 * parity
        greet_all(n * rows, n)

        def to_side(q):
            return pltpu.make_async_remote_copy(
                src_ref=x_ref.at[2 * q + 1 - parity], dst_ref=near.at[q], send_sem=near_out.at[q],
                recv_sem=near_in.at[q], device_id=(r, beside), device_id_type=MESH,
            )

        def to_chip(k):
            q = lax.rem(chip + k, half)
            return pltpu.make_async_remote_copy(
                src_ref=send.at[k], dst_ref=far.at[k], send_sem=far_out.at[k],
                recv_sem=far_in.at[k], device_id=(r, 2 * q + parity), device_id_type=MESH,
            )

        for q in range(half):
            to_side(q).start()
        ride.start(sent, got, sems, greet=False)
        for q in range(half):
            to_side(q).wait()

        def pair(k):
            q = lax.rem(chip + k, half)
            return x_ref[2 * q + parity].astype(F32) + near[q].astype(F32)

        for k in range(1, half):
            send[k] = pair(k).astype(BF)
            to_chip(k).start()
        o_ref[...] = pair(0)
        job.run(ins, outs, scratch)
        for k in range(1, half):
            to_chip(k).wait()
            o_ref[...] += far[k].astype(F32)
        ride.wait(sent, got, sems)

    block = pltpu.VMEM((half, length, features), BF)
    return pl.pallas_call(
        kern,
        out_shape=(jax.ShapeDtypeStruct((length, features), F32),) + ride.shapes + job.outs,
        in_specs=[VM] + [ANY] * (ride.count + len(job.inputs)),
        out_specs=(VM,) + (ANY,) * ride.count + (VM,) * len(job.outs),
        scratch_shapes=[block] * 3 + [pltpu.SemaphoreType.DMA((half,))] * 4 + ride.scratch + job.scratch,
        compiler_params=pltpu.CompilerParams(
            collective_id=collective_id, has_side_effects=True, vmem_limit_bytes=58 * 2**20
        ),
        cost_estimate=cost(40.0),
        name="reduce_exchange",
    )(partial, *[x for kind, x in plans], *job.inputs)


def gather_seq(values, n, rows, collective_id, plans=(), job=None):
    ride, job = Exchange(plans, n, rows), job or Job()
    sems_used = ride.scratch if ride.count else []
    parts = next(p for p in (2, 1) if p == 1 or values.shape[0] % (16 * p) == 0)
    height = values.shape[0] // parts

    def kern(*refs):
        refs, ins, outs, scratch = job.split(refs, 1 + ride.count, 1 + ride.count, 5 + len(sems_used))
        x_ref, sent, o_ref = refs[0], refs[1 : 1 + ride.count], refs[1 + ride.count]
        got, rest = refs[2 + ride.count : 2 + 2 * ride.count], refs[2 + 2 * ride.count :]
        own, out_sem, in_sem, side_out, side_in = rest[:5]
        sems = rest[5:]
        r, s = lax.axis_index("rows"), lax.axis_index("seq")
        beside = s + 1 - 2 * lax.rem(s, 2)
        if ride.count:
            greet_all(n * rows, n)
        else:
            barrier = pltpu.get_barrier_semaphore()
            for step in range(2, n, 2):
                pl.semaphore_signal(barrier, inc=1, device_id=(r, lax.rem(s + step, n)), device_id_type=MESH)
            pl.semaphore_signal(barrier, inc=1, device_id=(r, beside), device_id_type=MESH)
            pl.semaphore_wait(barrier, n // 2)
        def rows_of(ref, part):
            return ref.at[part * height : (part + 1) * height]

        def afar(k, part):
            return pltpu.make_async_remote_copy(
                src_ref=rows_of(x_ref, part), dst_ref=rows_of(o_ref.at[s], part),
                send_sem=out_sem.at[k, part], recv_sem=in_sem.at[k, part],
                device_id=(r, lax.rem(s + 2 * k, n)), device_id_type=MESH,
            )

        def across(k, part):
            slot = lax.rem(s + n - 2 * k, n)
            return pltpu.make_async_remote_copy(
                src_ref=rows_of(x_ref if k == 0 else o_ref.at[slot], part), dst_ref=rows_of(o_ref.at[slot], part),
                send_sem=side_out.at[k, part], recv_sem=side_in.at[k, part],
                device_id=(r, beside), device_id_type=MESH,
            )

        chips, pieces = range(1, n // 2), range(parts)
        for k in chips:
            for part in pieces:
                afar(k, part).start()
        for part in pieces:
            across(0, part).start()
        local = pltpu.make_async_copy(x_ref, o_ref.at[s], own)
        local.start()
        if ride.count:
            ride.start(sent, got, sems, greet=False)
        job.run(ins, outs, scratch)
        for part in pieces:
            for k in chips:
                afar(k, part).wait_recv()
                across(k, part).start()
        for part in pieces:
            for k in range(n // 2):
                across(k, part).wait()
            for k in chips:
                afar(k, part).wait_send()
        local.wait()
        if ride.count:
            ride.wait(sent, got, sems)

    length, features = values.shape
    whole, *got = pl.pallas_call(
        kern,
        out_shape=(jax.ShapeDtypeStruct((n, length, features), values.dtype),) + ride.shapes + job.outs,
        in_specs=[ANY] * (1 + ride.count + len(job.inputs)),
        out_specs=(ANY,) * (1 + ride.count) + (VM,) * len(job.outs),
        scratch_shapes=[pltpu.SemaphoreType.DMA] + [pltpu.SemaphoreType.DMA((n // 2, parts))] * 4
        + sems_used + job.scratch,
        compiler_params=pltpu.CompilerParams(
            collective_id=collective_id, has_side_effects=True, vmem_limit_bytes=56 * 2**20
        ),
        cost_estimate=cost(20.0),
        name="gather_seq",
    )(values, *[x for kind, x in plans], *job.inputs)
    whole = whole.reshape(n * length, features)
    return (whole, *got) if got else whole


def project_blocks(blocks, weight):
    length, width = blocks[0].shape[0], weight.shape[1]
    count = len(blocks)

    def kern(*refs):
        weight_ref, o_ref = refs[count], refs[count + 1]
        for k in range(count):
            o_ref[k * length : (k + 1) * length, :] = nn(refs[k][...], weight_ref[...]).astype(BF)

    return pl.pallas_call(
        kern,
        out_shape=jax.ShapeDtypeStruct((count * length, width), BF),
        in_specs=[VM] * (count + 1),
        out_specs=VM,
        compiler_params=pltpu.CompilerParams(vmem_limit_bytes=40 * 2**20),
        cost_estimate=cost(8.0),
        name="project_blocks",
    )(*blocks, weight)


def self_bwd(qkv,do,of,lse,fwd,qa,ka,plans,n,rows):
    Lq,W=qkv.shape[0],qkv.shape[1]//3; H=W//HD; nb=Lq//128
    ride=Exchange(plans,n,rows)
    def kern(qkv_ref,do_ref,of_ref,lse_ref,fwd_ref,qa_ref,ka_ref,*rest):
        sent,rest=rest[:ride.count],rest[ride.count:]
        grad_ref,gb_ref=rest[:2]
        got,rest=rest[2:2+ride.count],rest[2+ride.count:]
        (qaug,kaug,kdiag,vaug,doaug,dkacc,dvacc,dqs,dks,dvs,tz,ga),sems=rest[:12],rest[12:]
        h=pl.program_id(0)
        @pl.when(h==0)
        def _():
            ride.start(sent,got,sems)
        for hh in range(H):
            @pl.when(h==hh)
            def _():
                sl=slice(hh*HD,(hh+1)*HD)
                lane=lax.broadcasted_iota(jnp.int32,(Lq,HD),1)
                kaug[:,0:HD]=qkv_ref[:,W+hh*HD:W+(hh+1)*HD]
                ones=(lane>=3)&(lane<6)
                kaug[:,HD:]=jnp.where(ones,BF(1),ka_ref[...])
                kdiag[:,0:HD]=qkv_ref[:,W+hh*HD:W+(hh+1)*HD]
                kdiag[:,HD:]=jnp.where(ones,BF(1),BF(0)).astype(BF)
                vaug[:,0:HD]=qkv_ref[:,2*W+hh*HD:2*W+(hh+1)*HD]
                vaug[:,HD:]=jnp.where(lane<3,BF(1),BF(0)).astype(BF)
                a,b,c=split3(-lse_ref[:,hh:hh+1])
                qaug[:,0:HD]=qkv_ref[:,sl]*BF(0.125)
                qaug[:,HD:]=jnp.where(lane==3,a,jnp.where(lane==4,b,jnp.where(lane==5,c,qa_ref[...])))
                dd=do_ref[:,sl]
                delta=jnp.sum(dd.astype(F32)*of_ref[:,sl],axis=1,keepdims=True)
                a,b,c=split3(-delta)
                doaug[:,0:HD]=dd
                doaug[:,HD:]=jnp.where(lane==0,a,jnp.where(lane==1,b,jnp.where(lane==2,c,BF(0))))
        dkacc[...]=jnp.zeros_like(dkacc)
        dvacc[...]=jnp.zeros_like(dvacc)
        ga[...]=jnp.zeros_like(ga)
        bands=toeplitz(fwd_ref[pl.ds(h,1),:],nb*128)
        for d in range(nb):
            tz[d]=bands[:,d*128:(d+1)*128]
        eye=eye128()
        for q0 in range(0,Lq,256):
            qn=min(256,Lq-q0); kend=q0+qn
            qg=qaug[q0:kend,:]; dg=doaug[q0:kend,:]
            s=nt(kaug[0:kend,:],qg)
            g=nt(vaug[0:kend,:],dg)
            pcols=[]; dcols=[]
            for a in range(qn//128):
                qt=q0//128+a
                rows=slice(q0+a*128,q0+(a+1)*128)
                sd=nt(kdiag[rows,:],qaug[rows,:])
                pt=[]; dt=[]
                for b in range(kend//128):
                    d=qt-b
                    if d<0:
                        pt.append(jnp.zeros((128,128),BF)); dt.append(jnp.zeros((128,128),BF)); continue
                    t=s[b*128:(b+1)*128,a*128:(a+1)*128]
                    if d==0: t=jnp.where(eye,sd,t)
                    p=jnp.exp(t+tz[d])
                    ds=(p*g[b*128:(b+1)*128,a*128:(a+1)*128]).astype(BF)
                    ga[d]+=ds.astype(F32)
                    pt.append(p.astype(BF)); dt.append(ds)
                pcols.append(jnp.concatenate(pt,axis=0)); dcols.append(jnp.concatenate(dt,axis=0))
            P=jnp.concatenate(pcols,axis=1); DS=jnp.concatenate(dcols,axis=1)
            dvacc[0:kend,:]+=nn(P,dg[:,0:HD])
            dkacc[0:kend,:]+=nn(DS,qg[:,0:HD])
            dqs[h,q0:kend,:]=(tn(DS,kaug[0:kend,0:HD])*0.125).astype(BF)
        dks[h]=dkacc[...].astype(BF)
        dvs[h]=dvacc[...].astype(BF)
        flip=(lax.broadcasted_iota(jnp.int32,(128,128),0)+lax.broadcasted_iota(jnp.int32,(128,128),1)==127).astype(F32)
        y=jnp.concatenate([ga[d] for d in range(nb)],axis=1)
        y=lax.dot_general(flip,y,(((1,),(0,)),((),())),preferred_element_type=F32,precision=lax.Precision.HIGHEST)
        y=toeplitz_rows(jnp.concatenate([y,jnp.zeros((128,128),F32)],axis=1))
        gb_ref[pl.ds(h,1),:]=jnp.sum(y,axis=0,keepdims=True)
        @pl.when(h==H-1)
        def _():
            grad_ref[...]=jnp.concatenate([x[t] for x in (dqs,dks,dvs) for t in range(H)],axis=1)
            ride.wait(sent,got,sems)
    full=lambda s: pl.BlockSpec(s,lambda h:(0,)*len(s))
    return pl.pallas_call(kern,grid=(H,),
        out_shape=(jax.ShapeDtypeStruct((Lq,3*W),BF),jax.ShapeDtypeStruct((H,(nb+1)*128),F32))+ride.shapes,
        in_specs=[full((Lq,3*W))]+[full((Lq,W))]*2+[full((Lq,128)),full(fwd.shape),full((Lq,HD)),full((Lq,HD))]+[ANY]*ride.count,
        out_specs=(full((Lq,3*W)),full((H,(nb+1)*128)))+(ANY,)*ride.count,
        scratch_shapes=[pltpu.VMEM((Lq,2*HD),BF)]*5+[pltpu.VMEM((Lq,HD),F32)]*2+[pltpu.VMEM((H,Lq,HD),BF)]*3+[pltpu.VMEM((nb,128,128),F32)]*2+ride.scratch,
        compiler_params=pltpu.CompilerParams(vmem_limit_bytes=48*2**20,collective_id=11,has_side_effects=True),cost_estimate=cost(35.0),name="self_bwd")(
            qkv,do,of,lse,fwd,qa,ka,*[x for kind,x in plans])


MESH = pl.DeviceIdType.MESH


def sum_parts(first, cross, self_out, cross_out, n, wd):
    devices, count, wide = first.shape
    total = self_out.shape[0]

    def kern(first_ref, cross_ref, self_out_ref, cross_out_ref, sum_ref, col_ref, mean_ref):
        lane = lax.broadcasted_iota(jnp.int32, (count, 128), 1)
        means = jnp.zeros((count, 128), F32)
        sums = [None] * 8
        for ref, matrices in ((first_ref, (0, 1, 2)), (cross_ref, (4, 5, 6))):
            parts = []
            for s in range(n):
                part = ref[s].astype(F32)
                for r in range(1, devices // n):
                    part = part + ref[r * n + s].astype(F32)
                parts.append(part)
            for k, j in enumerate(matrices):
                if j > 4:
                    low = range(wd + (k - 1) * HD, 3 * wd, 2 * HD)
                    pieces = [part[:, c : c + HD] for part in parts for c in low]
                else:
                    pieces = [part[:, k * wd : (k + 1) * wd] for part in parts]
                sums[j] = jnp.concatenate(pieces, 1)[:, :D]
        for j, ref in ((3, self_out_ref), (7, cross_out_ref)):
            sums[j] = ref[0].astype(F32)
            for r in range(1, total):
                sums[j] = sums[j] + ref[r].astype(F32)
        for j in range(8):
            square = sums[j] * sums[j]
            sum_ref[:, j, :] = sums[j]
            col_ref[j : j + 1, :] = jnp.sum(square, 0, keepdims=True)
            means = jnp.where(lane == j, jnp.mean(square, 1, keepdims=True), means)
        mean_ref[...] = means

    return pl.pallas_call(
        kern,
        out_shape=(
            jax.ShapeDtypeStruct((count, 8, D), F32),
            jax.ShapeDtypeStruct((8, D), F32),
            jax.ShapeDtypeStruct((count, 128), F32),
        ),
        in_specs=[VM] * 4,
        out_specs=(VM,) * 3,
        compiler_params=pltpu.CompilerParams(vmem_limit_bytes=60 * 2**20),
        cost_estimate=cost(4.0),name="sum_parts",
    )(first, cross, self_out, cross_out)


def sum_everywhere(arrays, n, rows):
    count = n * rows
    wide_tiles, tiles = FF // 128, D // 128
    table_at, sums_at = tiles + wide_tiles, tiles + wide_tiles + 2
    assert sums_at < count

    def kern(att, exp, con, att_rows, exp_rows, con_rows, gain, table, *rest):
        outs, (x, o, got, mine, out_sem, in_sem, out_sem2, in_sem2) = rest[:6], rest[6:]
        me = lax.axis_index("rows") * n + lax.axis_index("seq")

        def place(step):
            j = lax.rem(me + step, count)
            return j, (lax.div(j, n), lax.rem(j, n))

        x[...] = jnp.zeros(x.shape, F32)
        for t in range(tiles):
            x[t] = att[:, t * 128 : (t + 1) * 128]
            x[tiles + t, 2:5, :] = gain[:, t * 128 : (t + 1) * 128]
            x[tiles + t, 5:6, :] = con[:, t * 128 : (t + 1) * 128]
        for t in range(wide_tiles):
            x[tiles + t, 0:2, :] = exp[:, t * 128 : (t + 1) * 128]
        x[table_at, :, 0:BUCKETS] = table[0:8, :]
        x[table_at + 1, 0 : HEADS - 8, 0:BUCKETS] = table[8:HEADS, :]
        x[sums_at, :, 0:1] = jnp.sum(att_rows[...], 1, keepdims=True)
        x[sums_at, 0:2, 1:2] = jnp.sum(exp_rows[...], 1, keepdims=True)
        x[sums_at, 0:1, 2:3] = jnp.sum(con_rows[...], 1, keepdims=True)
        greet_all(count, n)

        def piece(step):
            j, device = place(step)
            return pltpu.make_async_remote_copy(
                src_ref=x.at[j], dst_ref=got.at[step], send_sem=out_sem.at[step], recv_sem=in_sem.at[step],
                device_id=device, device_id_type=MESH,
            )

        def total(step):
            return pltpu.make_async_remote_copy(
                src_ref=mine, dst_ref=o.at[me], send_sem=out_sem2.at[step], recv_sem=in_sem2.at[step],
                device_id=place(step)[1], device_id_type=MESH,
            )

        def start_piece(step, carry):
            piece(step).start()
            return carry

        def add_piece(step, carry):
            piece(step).wait()
            return carry + got[step]

        def start_total(step, carry):
            total(step).start()
            return carry

        def wait_total(step, carry):
            total(step).wait()
            return carry

        lax.fori_loop(1, count, start_piece, 0)
        mine[...] = lax.fori_loop(1, count, add_piece, x[me])
        lax.fori_loop(1, count, start_total, 0)
        o[me] = mine[...]
        lax.fori_loop(1, count, wait_total, 0)
        att_out, exp_out, con_out, sums_out, gain_out, table_out = outs
        for t in range(tiles):
            att_out[:, t * 128 : (t + 1) * 128] = o[t]
            gain_out[:, t * 128 : (t + 1) * 128] = o[tiles + t, 2:5, :]
            con_out[:, t * 128 : (t + 1) * 128] = o[tiles + t, 5:6, :]
        for t in range(wide_tiles):
            exp_out[:, t * 128 : (t + 1) * 128] = o[tiles + t, 0:2, :]
        table_out[0:8, :] = o[table_at, :, 0:BUCKETS]
        table_out[8:HEADS, :] = o[table_at + 1, 0 : HEADS - 8, 0:BUCKETS]
        sums_out[...] = o[sums_at]

    shapes = ((8, D), (2, FF), (1, D), (8, 128), (3, D), (HEADS, BUCKETS))
    return pl.pallas_call(
        kern,
        out_shape=tuple(jax.ShapeDtypeStruct(shape, F32) for shape in shapes),
        in_specs=[VM] * 8,
        out_specs=(VM,) * 6,
        scratch_shapes=[pltpu.VMEM((count, 8, 128), F32)] * 3
        + [pltpu.VMEM((8, 128), F32)]
        + [pltpu.SemaphoreType.DMA((count,))] * 4,
        compiler_params=pltpu.CompilerParams(collective_id=1, has_side_effects=True),
        cost_estimate=cost(16.0),
        name="sum_everywhere",
    )(*arrays)


def feed_forward(norm, feed, contract, branch, part=512):
    length = norm.shape[0]
    scale = (2.0 / 3.141592653589793) ** 0.5

    def kern(norm_ref, gate_ref, up_ref, down_ref, branch_ref, hidden_ref, dgate_ref, dup_ref, dnorm_ref):
        a, b = nn(norm_ref[...], gate_ref[...]), nn(norm_ref[...], up_ref[...])
        grad = nt(branch_ref[...], down_ref[...])
        square = a * a
        t = jnp.tanh(scale * (a + 0.044715 * (a * square)))
        cdf = 0.5 * (1.0 + t)
        gelu = a * cdf
        slope = cdf + (0.5 * scale) * a * (1.0 - t * t) * (1.0 + 0.134145 * square)
        dgate, dup = (grad * b * slope).astype(BF), (grad * gelu).astype(BF)
        hidden_ref[...] = (gelu * b).astype(BF)
        dgate_ref[...], dup_ref[...] = dgate, dup
        dnorm = nt(dgate, gate_ref[...]) + nt(dup, up_ref[...])

        @pl.when(pl.program_id(0) == 0)
        def _():
            dnorm_ref[...] = dnorm

        @pl.when(pl.program_id(0) > 0)
        def _():
            dnorm_ref[...] += dnorm

    whole = pl.BlockSpec((length, D), lambda c: (0, 0))
    columns = pl.BlockSpec((length, part), lambda c: (0, c))
    wide = jax.ShapeDtypeStruct((length, FF), BF)
    return pl.pallas_call(
        kern,
        grid=(FF // part,),
        out_shape=(wide, wide, wide, jax.ShapeDtypeStruct((length, D), F32)),
        in_specs=[
            whole,
            pl.BlockSpec((D, part), lambda c: (0, c)),
            pl.BlockSpec((D, part), lambda c: (0, c + FF // part)),
            pl.BlockSpec((part, D), lambda c: (c, 0)),
            whole,
        ],
        out_specs=(columns, columns, columns, whole),
        compiler_params=pltpu.CompilerParams(vmem_limit_bytes=40 * 2**20),
        cost_estimate=cost(10.0),
        name="feed_forward",
    )(norm, feed, feed, contract, branch)


def normalize(values, scaling):
    return values * lax.rsqrt(jnp.mean(values * values, -1, keepdims=True) + NORM_EPS) * scaling


def update_all(totals, attention, expand, contract, feed, gain, table, passed, spare):
    count, deep = feed.shape[0], (feed.shape[1] - 2 * FF) // D

    def kern(total_ref, *refs):
        att, exp, con, (feed_ref,) = refs[:6], refs[6:11], refs[11:16], refs[16:17]
        vectors, held, outs = refs[17:25], refs[25 : 25 + len(passed)], refs[25 + len(passed) :]
        stops = len(passed)
        outs, kept, sem = outs[: 19 + stops], outs[19 + stops : -1], outs[-1]
        att_out, exp_out, con_out, vector_out = outs[:3], outs[3:7], outs[7:11], outs[11:19]
        arriving = [pltpu.make_async_copy(x, y, sem.at[0, k]) for k, (x, y) in enumerate(zip(held, kept))]
        leaving = [pltpu.make_async_copy(x, y, sem.at[1, k]) for k, (x, y) in enumerate(zip(kept, outs[19:]))]
        for copy in arriving:
            copy.start()
        for k in (0, 4):
            gradient = vectors[k][...]
            vector_out[k][...] = gradient
            vector_out[k + 1][...], vector_out[k + 2][...], vector_out[k + 3][...] = adaptive(
                gradient, vectors[k + 1][...], vectors[k + 2][...], vectors[k + 3][...]
            )

        def columns(old, summed, total):
            return BETA_TWO * old[...] + (1.0 - BETA_TWO) * (summed[...] / total)

        def step(gradient, moment, weight, row, column, row_mean):
            moment_new = BETA_ONE * moment + (1.0 - BETA_ONE) * gradient
            second = row * column / row_mean
            stepped = (
                moment_new
                / (1.0 - BETA_ONE**STEP)
                / (jnp.sqrt(second / (1.0 - BETA_TWO**STEP)) + ADAM_EPS)
            )
            return moment_new, weight - MATRIX_RATE * (stepped + WEIGHT_DECAY * weight)

        g, m, w, r, k, ks = att
        new = columns(k, ks, D)
        att_out[1][...] = new
        for j in range(8):
            mean = total_ref[j : j + 1, 0:1] / D
            att_out[0][:, j, :], att_out[2][:, j, :] = step(
                g[:, j, :], m[:, j, :], w[:, j, :], r[:, j : j + 1], new[j : j + 1], mean
            )
        for copy, onward in zip(arriving, leaving):
            copy.wait()
            onward.start()
        m, w, r, k, ks = exp
        new = columns(k, ks, D)
        exp_out[2][...] = new
        for j in range(2):
            mean = total_ref[j : j + 1, 1:2] / D
            gradient = feed_ref[:, j * FF : (j + 1) * FF].astype(F32)
            exp_out[0][:, j, :] = gradient
            exp_out[1][:, j, :], exp_out[3][:, j, :] = step(
                gradient, m[:, j, :], w[:, j, :], r[:, j : j + 1], new[j : j + 1], mean
            )
        m, w, r, k, ks = con
        new = columns(k, ks, FF)
        con_out[2][...] = new
        for group in range(deep):
            low, high = group * count, min((group + 1) * count, deep * count - spare)
            gradient = feed_ref[:, 2 * FF + group * D : 2 * FF + (group + 1) * D].astype(F32)[: high - low]
            con_out[0][low:high, :] = gradient
            con_out[1][low:high, :], con_out[3][low:high, :] = step(
                gradient, m[low:high, :], w[low:high, :], r[low:high, :], new, total_ref[0:1, 2:3] / FF
            )
        for copy in leaving:
            copy.wait()

    def like(x):
        return jax.ShapeDtypeStruct(x.shape, F32)

    g, m, w, r, k, ks = attention
    shapes = [like(m), like(k), like(w)]
    for m, w, r, k, ks in (expand, contract):
        shapes += [like(m), like(m), like(k), like(w)]
    shapes += [like(x) for x in gain + table] + [jax.ShapeDtypeStruct(x.shape, x.dtype) for x in passed]
    return pl.pallas_call(
        kern,
        out_shape=tuple(shapes),
        in_specs=[VM] * 26 + [ANY] * len(passed),
        out_specs=(VM,) * 19 + (ANY,) * len(passed),
        scratch_shapes=[pltpu.VMEM(x.shape, x.dtype) for x in passed] + [pltpu.SemaphoreType.DMA((2, len(passed)))],
        compiler_params=pltpu.CompilerParams(vmem_limit_bytes=60 * 2**20),
        cost_estimate=cost(5.0),
        name="update_all",
    )(totals, *attention, *expand, *contract, feed, *gain, *table, *passed)


def factored_start(gradient, rowwise):
    square = gradient * gradient
    rowwise_new = BETA_TWO * rowwise + (1.0 - BETA_TWO) * jnp.mean(square, 2).T
    return (rowwise_new, jnp.sum(square, 0))


def factored_finish(gradient, moment, rowwise_new, colwise, weight, column_sum, row_sum, total_rows):
    colwise_new = BETA_TWO * colwise + (1.0 - BETA_TWO) * (column_sum / total_rows)
    moment_new = BETA_ONE * moment + (1.0 - BETA_ONE) * gradient
    second = rowwise_new.T[:, :, None] * colwise_new[None] / (row_sum / total_rows)[None, :, None]
    stepped = (
        moment_new / (1.0 - BETA_ONE**STEP) / (jnp.sqrt(second / (1.0 - BETA_TWO**STEP)) + ADAM_EPS)
    )
    updated = weight - MATRIX_RATE * (stepped + WEIGHT_DECAY * weight)
    return (moment_new, colwise_new, updated)


def adaptive(gradient, moment, second, weight):
    moment_new = BETA_ONE * moment + (1.0 - BETA_ONE) * gradient
    second_new = BETA_TWO * second + (1.0 - BETA_TWO) * gradient * gradient
    stepped = (
        moment_new
        / (1.0 - BETA_ONE**STEP)
        / (jnp.sqrt(second_new / (1.0 - BETA_TWO**STEP)) + ADAM_EPS)
    )
    return (moment_new, second_new, weight - VECTOR_RATE * stepped)


def make_shards(n, rows):
    devices = n * rows
    both = ("rows", "seq")
    hpd = -(-HEADS // n)
    wd = hpd * HD
    wide = n * wd

    def widen(values):
        extra = wide - values.shape[-1]
        return values if extra == 0 else jnp.pad(values, [(0, 0)] * (values.ndim - 1) + [(0, extra)])

    def blocks_along_seq(values, gate):
        blocks = []
        for step in range(0, n, 2):
            block = values
            if step:
                block = lax.ppermute(values, "seq", [(i, i ^ step) for i in range(n)])
                block = lax.optimization_barrier((block, gate))[0]
            blocks += [block, lax.ppermute(block, "seq", [(i, i ^ 1) for i in range(n)])]
        return blocks

    def by_heads(weight):
        count, j = weight.shape[:2]
        return jnp.moveaxis(widen(weight).reshape(count, j, n * hpd, HD), 2, 1).reshape(count, wide * j)

    def to_seq(values, collective_id):
        (parts,) = exchange([("seq", values.reshape(n, -1, values.shape[1]))], n, rows, collective_id)
        return side_by_side(parts)[:, :D]

    def side_by_side(parts):
        return jnp.moveaxis(parts, 0, 1).reshape(parts.shape[1], -1)

    def shards(
        decoder_input,
        encoder_output,
        cotangent,
        decoder_segment,
        decoder_padding,
        encoder_segment,
        encoder_padding,
        distance_bucket,
        attention_weight,
        attention_moment,
        attention_rowwise,
        attention_colwise,
        expand_weight,
        expand_moment,
        expand_rowwise,
        expand_colwise,
        contract_weight,
        contract_moment,
        contract_rowwise,
        contract_colwise,
        norm_gain,
        gain_moment,
        gain_second,
        relative_table,
        table_moment,
        table_second,
    ):
        shard = lax.axis_index("seq")
        length = decoder_segment.shape[1]
        attention_low = attention_weight.astype(BF)
        count = expand_weight.shape[0]
        first_parts = jnp.moveaxis(widen(attention_low[:, 0:3]).reshape(count, 3, n, wd), 2, 0)
        row_input, first_columns = gather_seq(
            decoder_input[0], n, rows, 3, [("own", first_parts.reshape(n, count, 3 * wd))]
        )
        first_columns = first_columns.reshape(D, 3 * wd)
        attention_full = lax.all_gather(
            jnp.concatenate(
                (
                    attention_low[:, 3],
                    attention_low[:, 7],
                    by_heads(attention_low[:, 4:5]),
                    by_heads(attention_low[:, 5:7]),
                ),
                1,
            ),
            both, axis=0, tiled=True,
        )
        deep = -(-contract_weight.shape[0] // count)
        spare = deep * count - contract_weight.shape[0]
        contract_low = jnp.pad(contract_weight.astype(BF), ((0, spare), (0, 0)))
        feed_full = lax.all_gather(
            jnp.concatenate(
                (
                    expand_weight.astype(BF).reshape(count, 2 * FF),
                    jnp.moveaxis(contract_low.reshape(deep, count, D), 0, 1).reshape(count, deep * D),
                ),
                1,
            ),
            both, axis=0, tiled=True,
        )
        contract_full = jnp.concatenate(
            [
                feed_full[:, 2 * FF + g * D : 2 * FF + (g + 1) * D].reshape(devices, count, D)[
                    :, : contract_weight.shape[0] - g * count
                ]
                for g in range(deep)
            ],
            1,
        ).reshape(FF, D)
        edges = (0, D, 2 * D, 2 * D + wide, 2 * D + 3 * wide)
        self_out_weight, cross_out_weight, cross_query_weight, cross_pair_weight = (
            attention_full[:, low:high] for low, high in zip(edges[:-1], edges[1:])
        )
        cross_query_columns = lax.dynamic_slice_in_dim(cross_query_weight, shard * wd, wd, 1)
        cross_columns = lax.dynamic_slice_in_dim(cross_pair_weight, shard * 2 * wd, 2 * wd, 1)

        def own_rows(matrix):
            padded = jnp.pad(matrix, ((0, wide - D), (0, 0))) if wide > D else matrix
            return lax.dynamic_slice_in_dim(padded, shard * wd, wd, 0)

        document = jnp.arange(HD, dtype=jnp.int32)[None, :]
        decoder_document = decoder_segment[0][:, None] == document
        query_side = decoder_document.astype(BF)
        self_side = jnp.where(
            (document < 3) & ~(decoder_document & (decoder_padding[0][:, None] == 1)), NEG, 0.0
        ).astype(BF)
        real_document = jnp.where(encoder_padding[0] == 1, encoder_segment[0], -1).reshape(n, -1)
        real_document = jnp.concatenate(
            [lax.dynamic_slice_in_dim(real_document, shard ^ p, 1, 0)[0] for p in range(n)]
        )
        cross_side = jnp.where(
            (document < 3) & (real_document[:, None] != document), NEG, 0.0
        ).astype(BF)
        onehot = (
            distance_bucket[:, None] == jnp.arange(BUCKETS, dtype=jnp.int32)[None, :]
        ).astype(F32)
        table_own = lax.dynamic_slice_in_dim(
            jnp.pad(relative_table.T, ((0, n * hpd - HEADS), (0, 0))), shard * hpd, hpd, 0
        )
        bias = jnp.einsum("db,hb->hd", onehot, table_own, precision=HIGHEST)
        beyond = jnp.full((hpd, 128), NEG, F32)
        bias_forward = jnp.concatenate((beyond, bias), 1)
        bias_backward = jnp.concatenate((bias[:, ::-1], beyond), 1)

        def dot(left, right):
            return jnp.dot(left, right, preferred_element_type=F32)

        def dot_back(left, right):
            return lax.dot_general(left, right, (((1,), (1,)), ((), ())), preferred_element_type=F32)

        def outer(left, right):
            return lax.dot_general(left, right, (((0,), (0,)), ((), ())), preferred_element_type=F32)

        row_norm = normalize(row_input.astype(F32), norm_gain[0]).astype(BF)
        self_proj = dot(row_norm, first_columns).astype(BF)
        self_heads, self_exact, self_lse = self_fwd(
            self_proj, bias_backward, query_side, self_side
        )
        inputs = decoder_input[0].astype(F32)
        self_heads, cross_side = lax.optimization_barrier((self_heads, cross_side))
        self_out = to_seq(self_heads, 8)
        after_self = inputs + dot(self_out, self_out_weight)
        encoder_blocks = blocks_along_seq(
            lax.optimization_barrier((encoder_output[0], row_input))[0], after_self
        )
        cross_norm = normalize(after_self, norm_gain[1]).astype(BF)
        row_cross_norm = gather_seq(cross_norm, n, rows, 4)
        cross_query = dot(row_cross_norm, cross_query_columns).astype(BF)
        cross_pair = project_blocks(encoder_blocks, cross_columns)
        cross_heads, cross_exact, cross_lse = cross_fwd(
            cross_query, cross_pair, query_side, cross_side
        )
        cross_out = to_seq(cross_heads, 9)
        after_cross = after_self + dot(cross_out, cross_out_weight)
        feed_norm = normalize(after_cross, norm_gain[2]).astype(BF)
        feed_branch = cotangent[0]
        grad_result = feed_branch.astype(F32)
        hidden, grad_gate, grad_up, feed_norm_grad = feed_forward(feed_norm, feed_full, contract_full, feed_branch)
        unused_norm, norm_back = jax.vjp(normalize, after_cross, norm_gain[2])
        feed_part, feed_gain = norm_back(feed_norm_grad)
        grad_after_cross = grad_result + feed_part
        cross_branch = grad_after_cross.astype(BF)
        down_rows = deep * count - spare

        def feed_gradients(ins, outs):
            norm_ref, gate_ref, up_ref, hidden_ref, branch_ref = ins
            (o_ref,) = outs
            for c in range(0, 2 * FF, 512):
                low = c % FF
                part = tn(norm_ref[...], (gate_ref if c < FF else up_ref)[:, low : low + 512])
                o_ref[:, :, c : c + 512] = part.reshape(devices, count, 512).astype(BF)
            group = devices * 1024 // FF
            for c in range(0, FF, 1024):
                part = tn(hidden_ref[:, c : c + 1024], branch_ref[...]).reshape(group, down_rows, D)
                first = c // 1024 * group
                for g in range(deep):
                    piece = part[:, g * count : (g + 1) * count]
                    if piece.shape[1] < count:
                        low = jnp.zeros((group, count - piece.shape[1], D), F32)
                        piece = jnp.concatenate((piece, low), 1)
                    o_ref[first : first + group, :, 2 * FF + g * D : 2 * FF + (g + 1) * D] = piece.astype(BF)

        if count % 8 == 0:
            row_cross_branch, feed_local = gather_seq(
                cross_branch, n, rows, 5,
                job=Job(
                    (feed_norm, grad_gate, grad_up, hidden, feed_branch),
                    (jax.ShapeDtypeStruct((devices, count, 2 * FF + deep * D), BF),),
                    feed_gradients,
                ),
            )
            feed_local = feed_local.reshape(D, -1)
        else:
            row_cross_branch = gather_seq(cross_branch, n, rows, 5)
            contract_local = outer(hidden, feed_branch).astype(BF).reshape(devices, -1, D)
            contract_local = jnp.pad(contract_local, ((0, 0), (0, spare), (0, 0)))
            feed_local = jnp.concatenate(
                [outer(feed_norm, grad).astype(BF) for grad in (grad_gate, grad_up)]
                + [contract_local[:, g * count : (g + 1) * count].reshape(D, D) for g in range(deep)],
                1,
            )
        feed_low = lax.psum_scatter(feed_local, both, scatter_dimension=0, tiled=True)
        feed_sum = feed_low.astype(F32)
        cross_grad = dot_back(row_cross_branch, own_rows(cross_out_weight)).astype(BF)
        expand_sum = feed_sum[:, 0 : 2 * FF].reshape(count, 2, FF)
        contract_sum = jnp.concatenate(
            [feed_sum[:, 2 * FF + g * D : 2 * FF + (g + 1) * D] for g in range(deep)], 0
        )[: deep * count - spare]
        matched = wide == D and wd == rows * count
        cross_out_local = outer(cross_heads, row_cross_branch).astype(BF)
        cross_plans = [("rows", cross_out_local.reshape(rows, count, D))] if matched else []
        cross_qparts, cross_home, cross_qgrad, *cross_grads = cross_bwd(
            cross_query, cross_pair, cross_grad, cross_exact, cross_lse, query_side, cross_side, cross_plans, n, rows
        )
        cross_rows, cross_grads = cross_grads[: len(cross_plans)], cross_grads[len(cross_plans) :]
        grad_cross_query = side_by_side(cross_qparts)[:, :D]
        unused_norm, norm_back = jax.vjp(normalize, after_self, norm_gain[1])
        cross_part, cross_gain = norm_back(dot_back(grad_cross_query, cross_query_weight[:, :D]))
        grad_after_self = grad_after_cross + cross_part
        self_branch = grad_after_self.astype(BF)
        def cross_gradients(ins, outs):
            norm_ref, query_ref = ins[:2]
            (o_ref,) = outs
            o_ref[:, 0:wd] = tn(norm_ref[...], query_ref[...]).astype(BF)
            pair = tn(ins[2][...], ins[2 + n][...])
            for p in range(1, n):
                pair = pair + tn(ins[2 + p][...], ins[2 + n + p][...])
            o_ref[:, wd : 3 * wd] = pair.astype(BF)

        row_self_branch, cross_local = gather_seq(
            self_branch, n, rows, 6,
            job=Job(
                (row_cross_norm, cross_qgrad.reshape(-1, wd))
                + tuple(encoder_blocks) + tuple(cross_grads),
                (jax.ShapeDtypeStruct((D, 3 * wd), BF),),
                cross_gradients,
            ),
        )
        self_grad = dot_back(row_self_branch, own_rows(self_out_weight)).astype(BF)
        self_out_local = outer(self_heads, row_self_branch).astype(BF)
        rows_local = (self_out_local, cross_out_local)
        self_grads, pair_bias, cross_parts = self_bwd(
            self_proj, self_grad, self_exact, self_lse, bias_forward, query_side, self_side,
            [("all", cross_local.reshape(devices, count, 3 * wd))], n, rows,
        )
        rows_plans = [("rows", self_out_local.reshape(rows, count, D))] if matched else []
        grad_bias = pair_bias[:, 128:]
        table_own_grad = jnp.einsum("hd,db->hb", grad_bias, onehot, precision=HIGHEST)
        table_local = lax.dynamic_update_slice_in_dim(
            jnp.zeros((n * hpd, BUCKETS), F32), table_own_grad, shard * hpd, 0
        )[:HEADS]
        self_back = dot_back(self_grads, first_columns).astype(BF)
        def encoder_job(ins, outs):
            home_ref, weight_ref, hidden_ref, down_ref, stream_ref = ins
            total = None
            for t in range(n):
                for h in range(hpd):
                    low = (t * hpd + h) * 2 * HD
                    part = nt(home_ref[t, h], weight_ref[:, low : low + 2 * HD])
                    total = part if total is None else total + part
            outs[0][...] = total
            outs[1][...] = (stream_ref[...] + nn(hidden_ref[...], down_ref[...])).astype(BF)

        self_back_sum, self_parts, *rest = reduce_exchange(
            self_back.reshape(n, -1, D),
            [
                ("all", outer(row_norm, self_grads).astype(BF).reshape(devices, count, 3 * wd)),
            ] + rows_plans,
            n, rows, 7,
            job=Job(
                (
                    cross_home,
                    (attention_full, (2 * D + wide, 2 * D + 3 * wide)),
                    hidden,
                    contract_full,
                    after_cross,
                ),
                (
                    jax.ShapeDtypeStruct(encoder_output.shape[1:], F32),
                    jax.ShapeDtypeStruct(decoder_input.shape[1:], BF),
                ),
                encoder_job,
            ),
        )
        *rows_parts, encoder_gradient, layer_output = rest
        rows_parts += cross_rows
        if not matched:
            padded = lax.dynamic_update_slice_in_dim(
                jnp.zeros((wide, 2 * D), BF), jnp.concatenate(rows_local, 1), shard * wd, 0
            )[:D]
            whole = lax.psum_scatter(padded, both, scatter_dimension=0, tiled=True)[None]
            rows_parts = [whole[:, :, :D], whole[:, :, D:]]
        unused_norm, norm_back = jax.vjp(normalize, inputs, norm_gain[0])
        self_part, self_gain = norm_back(self_back_sum)
        input_gradient = grad_after_self + self_part

        attention_sum, attention_columns, attention_means = sum_parts(
            self_parts, cross_parts, *rows_parts, n, wd
        )
        attention_rows = BETA_TWO * attention_rowwise + (1.0 - BETA_TWO) * attention_means[:, 0:8].T
        expand_rows, expand_columns = factored_start(expand_sum, expand_rowwise)
        contract_rows, contract_columns = factored_start(
            contract_sum[:, None, :], contract_rowwise[None, :]
        )
        gain_local = jnp.stack((self_gain, cross_gain, feed_gain), 0)
        attention_total, expand_total, contract_total, row_totals, gain_gradient, table_gradient = (
            sum_everywhere(
                (
                    attention_columns,
                    expand_columns,
                    contract_columns,
                    attention_rows,
                    expand_rows,
                    contract_rows,
                    gain_local,
                    table_local,
                ),
                n, rows,
            )
        )
        attention_rowtotal, expand_rowtotal, contract_rowtotal = (
            row_totals[:, 0],
            row_totals[:2, 1],
            row_totals[:1, 2],
        )
        if count % 8 == 0:
            (
                *attention_new, expand_sum, moment_expand, colwise_expand, updated_expand,
                contract_sum, moment_contract, colwise_contract, updated_contract,
                gain_gradient, moment_gain, second_gain, updated_gain,
                table_gradient, moment_table, second_table, updated_table,
                encoder_gradient, layer_output,
            ) = update_all(
                row_totals,
                (
                    attention_sum, attention_moment, attention_weight, attention_rows.T,
                    attention_colwise, attention_total,
                ),
                (expand_moment, expand_weight, expand_rows.T, expand_colwise, expand_total),
                (contract_moment, contract_weight, contract_rows.T, contract_colwise[None], contract_total),
                feed_low,
                (gain_gradient, gain_moment, gain_second, norm_gain),
                (table_gradient, table_moment.T, table_second.T, relative_table.T),
                (encoder_gradient, layer_output),
                spare,
            )
            attention_new = attention_new[:3]
            gain_new = (moment_gain, second_gain, updated_gain)
            table_gradient = table_gradient.T
            table_new = (moment_table.T, second_table.T, updated_table.T)
            expand_new = (moment_expand, colwise_expand, updated_expand)
            contract_new = (moment_contract[:, None], colwise_contract, updated_contract[:, None])
        else:
            attention_new = factored_finish(
                attention_sum,
                attention_moment,
                attention_rows,
                attention_colwise,
                attention_weight,
                attention_total,
                attention_rowtotal,
                D,
            )
            expand_new = factored_finish(
                expand_sum,
                expand_moment,
                expand_rows,
                expand_colwise,
                expand_weight,
                expand_total,
                expand_rowtotal,
                D,
            )
            contract_new = factored_finish(
                contract_sum[:, None, :],
                contract_moment[:, None, :],
                contract_rows,
                contract_colwise[None, :],
                contract_weight[:, None, :],
                contract_total,
                contract_rowtotal,
                FF,
            )
            gain_new = adaptive(gain_gradient, gain_moment, gain_second, norm_gain)
            table_gradient = table_gradient.T
            table_new = adaptive(table_gradient, table_moment, table_second, relative_table)
        return (
            layer_output[None],
            input_gradient[None],
            encoder_gradient[None],
            attention_sum,
            attention_new[0],
            attention_rows,
            attention_new[1],
            attention_new[2],
            expand_sum,
            expand_new[0],
            expand_rows,
            expand_new[1],
            expand_new[2],
            contract_sum,
            contract_new[0][:, 0],
            contract_rows[0],
            contract_new[1][0],
            contract_new[2][:, 0],
            gain_gradient,
            gain_new[0],
            gain_new[1],
            gain_new[2],
            table_gradient,
            table_new[0],
            table_new[1],
            table_new[2],
        )

    return shards


def solution(mesh):
    placed = (
        P("rows", "seq", None),
        P("rows", "seq", None),
        P("rows", "seq", None),
        P("rows", None),
        P("rows", None),
        P("rows", None),
        P("rows", None),
        P(),
        P(("rows", "seq"), None, None),
        P(("rows", "seq"), None, None),
        P(None, ("rows", "seq")),
        P(),
        P(("rows", "seq"), None, None),
        P(("rows", "seq"), None, None),
        P(None, ("rows", "seq")),
        P(),
        P(("rows", "seq"), None),
        P(("rows", "seq"), None),
        P(("rows", "seq")),
        P(),
        P(),
        P(),
        P(),
        P(),
        P(),
        P(),
    )
    return jax.shard_map(
        make_shards(mesh.shape["seq"], mesh.shape["rows"]),
        mesh=mesh,
        in_specs=placed,
        out_specs=(
            P("rows", "seq", None),
            P("rows", "seq", None),
            P("rows", "seq", None),
            P(("rows", "seq"), None, None),
            P(("rows", "seq"), None, None),
            P(None, ("rows", "seq")),
            P(),
            P(("rows", "seq"), None, None),
            P(("rows", "seq"), None, None),
            P(("rows", "seq"), None, None),
            P(None, ("rows", "seq")),
            P(),
            P(("rows", "seq"), None, None),
            P(("rows", "seq"), None),
            P(("rows", "seq"), None),
            P(("rows", "seq")),
            P(),
            P(("rows", "seq"), None),
            P(),
            P(),
            P(),
            P(),
            P(),
            P(),
            P(),
            P(),
        ),
        check_vma=False,
    )
```
